512 devices in a mesh: row: 32 (over x, z), height: 16 (over y, core).
Axes of the slice: x: 4, y: 8, z: 8, core: 2. Of those that a mesh axis runs over, the one named last changes fastest.
Arguments:
- streamwise_wind_edges: float32 [256, 32, 4096], P('height', None, 'row'), may hold values from -6 to 6
- climbing_wind_edges: float32 [256, 32, 4096], P('height', None, 'row'), may hold values from -5.5 to 5.5
- thermal_anomaly: float32 [256, 32, 4096], P('height', None, 'row'), may hold values from -4 to 4
- foliage_group_index: int32 [256, 32, 4096], P('height', None, 'row'), may hold values from 0 to 7
- paved_surface_flag: int32 [32, 4096], P(None, 'row'), may hold values 0 or 1
- sunlight_flux_crown: float32 [32, 4096], P(None, 'row'), may hold values from 4 to 32
- foliage_area_lookup: float32 [8], replicated, may hold values from 0.02 to 0.2
Outputs:
- u_next: float32 [256, 32, 4096], P('height', None, 'row')
- w_next: float32 [256, 32, 4096], P('height', None, 'row')
- renewed_thermal_anomaly: float32 [256, 32, 4096], P('height', None, 'row')
The draws below stay inside these ranges and needn't reach their ends.
All inputs are finite; a program needn't handle non-finite values. No bound on the sum of `paved_surface_flag` on one device may be relied on, other than what follows from the above.
Results may differ from the reference program's by a relative error of at most 0.0003.
Values sent between devices are 32-bit elements; how exact they have to be, the bound alone decides.
A program may use at most 64 MiB of HBM per device.

```python
import math
import jax
import jax.numpy as jnp
from jax import lax

STREAMWISE_BINS = 4096
HEIGHT_LAYERS = 256
CANOPY = 48
NCLASS = 8
SECTION_NUMBER = 32


def turn_cosine(phase_count, period):
    return jnp.cos((phase_count % period).astype(jnp.float32) * (2.0 * math.pi / period))


def turn_sine(phase_count, period):
    return jnp.sin((phase_count % period).astype(jnp.float32) * (2.0 * math.pi / period))


def smooth_rows(key, plane_count, column_count, lowest, highest, least_gain, most_gain):
    columns = jnp.arange(column_count, dtype=jnp.int32)[None, :]
    envelope = jnp.zeros((plane_count, column_count), jnp.float32)
    for component in range(3):
        part_key = jax.random.fold_in(key, component)
        wave_keys = jax.random.split(part_key, 3)
        wavenum = jax.random.randint(wave_keys[0], (plane_count, 1), lowest, highest)
        offset = jax.random.randint(wave_keys[1], (plane_count, 1), 0, column_count)
        weight = jax.random.uniform(wave_keys[2], (plane_count, 1), jnp.float32, least_gain, most_gain)
        envelope = envelope + weight * turn_cosine(wavenum * columns + offset, column_count)
    return envelope


def draw_streamwise_wind_edges(key, part):
    key = jax.random.fold_in(key, 29)
    draw_keys = jax.random.split(key, 6)
    level_count = HEIGHT_LAYERS
    plane_count = SECTION_NUMBER
    column_count = STREAMWISE_BINS
    row_low = max(1, 256 * column_count // 4096)
    row_high = max(row_low + 1, 273 * column_count // 4096)
    lift_low = max(1, level_count // 128)
    lift_high = max(lift_low + 1, level_count // 48 + 1)
    columns = jnp.arange(column_count, dtype=jnp.int32)[None, :]
    levels = jnp.arange(level_count, dtype=jnp.int32)[:, None]
    row_wave = jax.random.randint(draw_keys[0], (plane_count, 1), row_low, row_high)
    row_shift = jax.random.randint(draw_keys[1], (plane_count, 1), 0, column_count)
    lift_wave = jax.random.randint(draw_keys[2], (1, plane_count), lift_low, lift_high)
    lift_shift = jax.random.randint(draw_keys[3], (1, plane_count), 0, level_count)
    shape = (level_count, plane_count, column_count)
    mean_flow = jax.random.uniform(draw_keys[4], shape, jnp.float32, -1.0, 3.0)
    plane_gain = jax.random.uniform(draw_keys[5], (1, plane_count), jnp.float32, 0.8, 1.2)
    profile = plane_gain * (1.0 + 0.8 * turn_cosine(lift_wave * levels + lift_shift, level_count))
    oscillation = turn_cosine(row_wave * columns + row_shift, column_count)
    return mean_flow + profile[:, :, None] * oscillation[None]


def draw_climbing_wind_edges(key, part):
    key = jax.random.fold_in(key, 17)
    draw_keys = jax.random.split(key, 5)
    level_count = HEIGHT_LAYERS
    plane_count = SECTION_NUMBER
    column_count = STREAMWISE_BINS
    levels_plus = jnp.arange(level_count, dtype=jnp.int32)[:, None, None] + 1
    first_low = max(1, 8 * level_count // 256)
    first_high = max(first_low + 1, 11 * level_count // 256)
    second_low = max(1, 11 * level_count // 256)
    second_high = max(second_low + 1, 17 * level_count // 256)
    wave_low = max(1, column_count // 512)
    wave_high = max(wave_low + 1, column_count // 64 + 1)
    first_mode = jax.random.randint(draw_keys[0], (1, plane_count, 1), first_low, first_high)
    second_mode = jax.random.randint(draw_keys[1], (1, plane_count, 1), second_low, second_high)
    shape = (level_count, plane_count, column_count)
    background = jnp.clip(0.3 * jax.random.normal(draw_keys[2], shape, jnp.float32), -1.0, 1.0)
    least_gain = 0.5
    most_gain = 0.8
    first_rows = smooth_rows(draw_keys[3], plane_count, column_count, wave_low, wave_high, least_gain, most_gain)
    second_rows = smooth_rows(draw_keys[4], plane_count, column_count, wave_low, wave_high, least_gain, most_gain)
    first_profile = turn_sine(first_mode * levels_plus, 2 * level_count)
    second_profile = turn_sine(second_mode * levels_plus, 2 * level_count)
    return background + first_profile * first_rows[None] + 0.5 * second_profile * second_rows[None]


def plant(result, rng, smallest, top_value):
    place = [jax.random.randint(jax.random.fold_in(rng, axis), (), 0, length) for axis, length in enumerate(result.shape)]
    longest = result.shape.index(max(result.shape))
    next_to = place[:longest] + [(place[longest] + 1) % result.shape[longest]] + place[longest + 1:]
    return result.at[tuple(place)].set(smallest).at[tuple(next_to)].set(top_value)


def steps_of(key, shape, cuts, least, largest):
    level, own = 1.0, jax.random.fold_in(key, 6)
    for dim, blocks in cuts:
        draws = jnp.exp(jax.random.uniform(jax.random.fold_in(own, dim), (blocks,), jnp.float32, least / len(cuts), largest / len(cuts)))
        level = level * jnp.repeat(draws, shape[dim] // blocks).reshape([-1 if axis == dim else 1 for axis in range(len(shape))])
    return level


def noise(stream_key, shape, width, bound, shards=(), held_as=jnp.bfloat16):
    entries = jax.random.normal(stream_key, shape, jnp.float32) * width
    if len(shards) > 0:
        entries = steps_of(stream_key, shape, shards, -0.22, 0.18) * entries
    return jnp.clip(entries, min=-bound, max=bound).astype(held_as)


def setup_inputs(seed: int = 0) -> dict:
    seeds = jax.random.split(jax.random.key(seed), 8)
    streamwise_wind_edges = draw_streamwise_wind_edges(jax.random.fold_in(seeds[7], 71), 0)
    climbing_wind_edges = draw_climbing_wind_edges(jax.random.fold_in(seeds[7], 71), 0)
    thermal_anomaly = noise(seeds[2], (HEIGHT_LAYERS, SECTION_NUMBER, STREAMWISE_BINS), 1.0, 4.0, ((0, 16), (2, 32)), jnp.float32)
    foliage_group_index = plant(jax.random.randint(seeds[3], (HEIGHT_LAYERS, SECTION_NUMBER, STREAMWISE_BINS), 0, NCLASS), jax.random.fold_in(seeds[3], 1), 0, NCLASS - 1).astype(jnp.int32)
    paved_surface_flag = plant((jax.random.randint(seeds[4], (SECTION_NUMBER, STREAMWISE_BINS), 0, 2) < 1).astype(jnp.int32), jax.random.fold_in(seeds[4], 1), 0, 1)
    sunlight_flux_crown = jnp.clip(jnp.exp(math.log(32.0) - 2.0794415 * jax.random.uniform(seeds[5], (SECTION_NUMBER, STREAMWISE_BINS), jnp.float32) ** steps_of(seeds[5], (SECTION_NUMBER, STREAMWISE_BINS), ((1, 32),), -0.2, 0.2)), 4.0, 32.0)
    foliage_area_lookup = jnp.clip(jnp.exp(jax.random.uniform(seeds[6], (NCLASS,), jnp.float32, math.log(0.02), math.log(0.2))), 0.02, 0.2)
    return {"streamwise_wind_edges": streamwise_wind_edges, "climbing_wind_edges": climbing_wind_edges, "thermal_anomaly": thermal_anomaly, "foliage_group_index": foliage_group_index, "paved_surface_flag": paved_surface_flag, "sunlight_flux_crown": sunlight_flux_crown, "foliage_area_lookup": foliage_area_lookup}


TIME_INCREMENT = 0.25
VISCOSITY = 0.05
DRAG_COEF = 0.2
THERMAL_LIFT = 0.2
SPAN_VAR = 0.25
HAZE_EXTINCT = 0.02
COLUMN_HEIGHT = 256.0
PAVED_ABSORB = 0.9
GRASS_ABSORB = 0.5
HIGHEST_PREC = lax.Precision.HIGHEST

def cosine_levels(count_levels):
    mode_index = jnp.arange(count_levels, dtype=jnp.int32)
    phase_index = mode_index[:, None] * (2 * mode_index[None, :] + 1) % (4 * count_levels)
    angles = phase_index.astype(jnp.float32) * (math.pi / (2.0 * count_levels))
    weights = jnp.where(mode_index == 0, math.sqrt(1.0 / count_levels), math.sqrt(2.0 / count_levels)).astype(jnp.float32)
    return jnp.cos(angles) * weights[:, None]

def hartley(samples):
    spectrum = jnp.fft.fft(samples, axis=-1)
    return jnp.real(spectrum) - jnp.imag(spectrum)

def shifted_levels(samples, upward):
    zero_level = jnp.zeros_like(samples[:1])
    if upward:
        return jnp.concatenate([samples[1:], zero_level], 0)
    return jnp.concatenate([zero_level, samples[:-1]], 0)

def rates_of_growth(samples, streamwise_wind_edges, climbing_wind_edges):
    east_cells = jnp.roll(samples, -1, axis=2)
    west_cells = jnp.roll(samples, 1, axis=2)
    above_cells = shifted_levels(samples, True)
    below_cells = shifted_levels(samples, False)
    advect = streamwise_wind_edges * (east_cells - west_cells) * 0.5 + climbing_wind_edges * (above_cells - below_cells) * 0.5
    diffuse = VISCOSITY * (east_cells + west_cells + above_cells + below_cells - 4.0 * samples)
    return diffuse - advect

def reference(streamwise_wind_edges, climbing_wind_edges, thermal_anomaly, foliage_group_index, paved_surface_flag, sunlight_flux_crown, foliage_area_lookup):
    level_index = jnp.arange(HEIGHT_LAYERS, dtype=jnp.int32)[:, None, None]
    top_level = level_index == HEIGHT_LAYERS - 1
    leaf_area = jnp.where(level_index < CANOPY, foliage_area_lookup[foliage_group_index], 0.0)
    thickness = COLUMN_HEIGHT / HEIGHT_LAYERS
    haze = HAZE_EXTINCT * jnp.exp(-4.0 * (level_index.astype(jnp.float32) + 0.5) / HEIGHT_LAYERS)
    optical = (0.5 * leaf_area + haze) * thickness
    inclusive = jnp.flip(jnp.cumsum(jnp.flip(optical, 0), 0), 0)
    depth_top = shifted_levels(inclusive, True)
    trans_top = jnp.exp(-depth_top)
    trans_bottom = jnp.exp(-(depth_top + optical))
    sunlight_warming = sunlight_flux_crown[None] * (trans_top - trans_bottom) / thickness
    absorb = jnp.where(paved_surface_flag == 1, PAVED_ABSORB, GRASS_ABSORB)
    surface = sunlight_flux_crown * trans_bottom[0] * absorb / thickness
    sunlight_warming = jnp.concatenate([sunlight_warming[:1] + surface[None], sunlight_warming[1:]], 0)
    wind_speed = jnp.sqrt(streamwise_wind_edges * streamwise_wind_edges + climbing_wind_edges * climbing_wind_edges + SPAN_VAR)
    foliage_friction_coefficient = DRAG_COEF * leaf_area * wind_speed
    trial_streamwise_wind = streamwise_wind_edges + TIME_INCREMENT * (rates_of_growth(streamwise_wind_edges, streamwise_wind_edges, climbing_wind_edges) - foliage_friction_coefficient * streamwise_wind_edges)
    trial_climbing_wind = climbing_wind_edges + TIME_INCREMENT * (rates_of_growth(climbing_wind_edges, streamwise_wind_edges, climbing_wind_edges) - foliage_friction_coefficient * climbing_wind_edges + THERMAL_LIFT * thermal_anomaly)
    trial_climbing_wind = jnp.where(top_level, 0.0, trial_climbing_wind)
    renewed_thermal_anomaly = thermal_anomaly + TIME_INCREMENT * (rates_of_growth(thermal_anomaly, streamwise_wind_edges, climbing_wind_edges) + sunlight_warming)
    divergence = trial_streamwise_wind - jnp.roll(trial_streamwise_wind, 1, axis=2) + (trial_climbing_wind - shifted_levels(trial_climbing_wind, False))
    cosine_table = cosine_levels(HEIGHT_LAYERS)
    spectrum = hartley(divergence)
    modal_field = jnp.einsum('mz,zyx->myx', cosine_table, spectrum, precision=HIGHEST_PREC)
    wavenumber = jnp.arange(STREAMWISE_BINS, dtype=jnp.int32)
    mode_index = jnp.arange(HEIGHT_LAYERS, dtype=jnp.int32)
    eigen_x = -4.0 * jnp.sin(wavenumber.astype(jnp.float32) * (math.pi / STREAMWISE_BINS)) ** 2
    eigen_z = -4.0 * jnp.sin(mode_index.astype(jnp.float32) * (math.pi / (2.0 * HEIGHT_LAYERS))) ** 2
    total_eigen = eigen_z[:, None, None] + eigen_x[None, None, :]
    singular = (mode_index[:, None, None] == 0) & (wavenumber[None, None, :] == 0)
    modal_field = jnp.where(singular, 0.0, modal_field / jnp.where(singular, 1.0, total_eigen))
    spectrum = jnp.einsum('mz,myx->zyx', cosine_table, modal_field, precision=HIGHEST_PREC)
    potential = hartley(spectrum) / STREAMWISE_BINS
    streamwise_push_gradient = jnp.roll(potential, -1, axis=2) - potential
    climbing_push_gradient = jnp.where(top_level, 0.0, shifted_levels(potential, True) - potential)
    return (trial_streamwise_wind - streamwise_push_gradient, trial_climbing_wind - climbing_push_gradient, renewed_thermal_anomaly)
```

```python
import functools
import math

import jax
import jax.numpy as jnp
import numpy as np
from jax import lax
from jax.experimental import pallas as pl
from jax.experimental.pallas import tpu as pltpu
from jax.sharding import PartitionSpec as P

CANOPY = 48
DT = 0.25
VISCOSITY = 0.05
DRAG_COEF = 0.2
THERMAL_LIFT = 0.2
SPAN_VAR = 0.25
HAZE_EXTINCT = 0.02
PAVED_ABSORB = 0.9
GRASS_ABSORB = 0.5
MESH = pl.DeviceIdType.MESH
HIGHEST = lax.Precision.HIGHEST
LANES = 128


def tables(levels, columns, row_count):
    m = np.arange(levels, dtype=np.float64)
    z = np.arange(levels, dtype=np.float64)
    cosine = np.cos(np.pi * m[:, None] * (z[None, :] + 0.5) / levels)
    cosine *= np.where(m == 0, math.sqrt(1.0 / levels), math.sqrt(2.0 / levels))[:, None]
    mu = 2.0 * np.arcsinh(np.sin(np.pi * m / (2.0 * levels)))
    safe = np.where(m == 0, 1.0, mu)
    gain = np.where(m == 0, 0.0, -1.0 / (2.0 * np.sinh(safe)))
    x = np.arange(LANES, dtype=np.float64)
    rates = np.zeros((levels, LANES))
    for k in range(7):
        rates[:, k] = np.exp(-mu * 2.0**k)
    rates[:, 7] = gain
    phi_west = np.where(m[:, None] == 0, 1.0, gain[:, None] * np.exp(-mu[:, None] * (x + 1.0)))
    phi_east = np.where(m[:, None] == 0, x, gain[:, None] * np.exp(-mu[:, None] * (LANES - x)))
    near = 0.5 * np.abs(x[:, None] - x[None, :]) + x[:, None] * x[None, :] / columns
    lane = np.arange(LANES)
    odd = lane % 2 == 1
    group = np.where(odd, (lane + 1) // 2, lane // 2) % 64
    per_plane = levels // 8
    used = group < 2 * per_plane
    mode = 8 * (group % per_plane)[None, :] + np.arange(8)[:, None]
    mode_mu = mu[mode]
    safe_mu = np.where(mode == 0, 1.0, mode_mu)
    direct = np.zeros((row_count, 8, LANES))
    cross = np.zeros((row_count, 8, LANES))
    for shift in range(row_count):
        to_east = shift if shift else row_count
        to_west = row_count - shift
        steps = np.where(odd, to_west, to_east)[None, :]
        usual = np.exp(-safe_mu * LANES * (steps - 1)) / (1.0 - np.exp(-safe_mu * columns))
        away = float(LANES * shift)
        if shift:
            zero_direct = np.where(odd, away / 2 - away**2 / (2 * columns), 1.0 / columns)
            zero_cross = np.where(odd, -0.5 + away / columns, 0.5 - away / columns)
        else:
            zero_direct = np.zeros(LANES)
            zero_cross = np.zeros(LANES)
        direct[shift] = np.where(mode == 0, zero_direct[None, :], usual) * used
        cross[shift] = np.where(mode == 0, zero_cross[None, :], 0.0) * used
    haze = HAZE_EXTINCT * np.exp(-4.0 * (z + 0.5) / levels)
    haze_above = np.concatenate([np.cumsum(haze[::-1])[::-1], [0.0]])
    f32 = lambda a: np.ascontiguousarray(a, dtype=np.float32)
    return dict(
        cosine=f32(cosine), cosine_t=f32(cosine.T), rates=f32(rates), phi_west=f32(phi_west),
        phi_east=f32(phi_east), near=f32(near), direct=f32(direct), cross=f32(cross),
        haze=f32(haze_above),
    )


def kernel(
    rows, heights,
    u_hbm, w_hbm, t_hbm, class_ref, paved_ref, sun_ref, lookup_ref, haze_ref,
    cosine_ref, cosine_t_ref, rates_ref, phi_w_ref, phi_e_ref, near_ref, direct_ref, cross_ref,
    un_ref, wn_ref, tn_ref,
    ext, leaf, leaf_sum, leaf_in, side_out, side_in, side, us, ws, us_out, us_in,
    d_out, d_in, pm, mom, p_out, p_in, p_up, pc_out, pc_in,
    in_sem, z_sem, side_sem, leaf_sem, star_sem, a2a_sem, mom_sem, back_sem, edge_sem,
):
    r = lax.axis_index("row")
    h = lax.axis_index("height")
    levels_here = class_ref.shape[0]
    planes = class_ref.shape[1]
    nz = levels_here * heights
    block = 2 * levels_here
    groups = nz // 8

    def at(dr, dh):
        return (lax.rem(r + dr + rows, rows), lax.rem(h + dh + heights, heights))

    loads = [
        pltpu.make_async_copy(ref, ext.at[f, pl.ds(1, levels_here)], in_sem.at[f])
        for f, ref in enumerate((u_hbm, w_hbm, t_hbm))
    ]
    for load in loads:
        load.start()

    barrier = pltpu.get_barrier_semaphore()

    def greet_height(i, c):
        pl.semaphore_signal(barrier, inc=1, device_id=at(0, i), device_id_type=MESH)
        return c

    def greet_row(i, c):
        pl.semaphore_signal(barrier, inc=1, device_id=at(i, 0), device_id_type=MESH)
        return c

    lax.fori_loop(1, heights, greet_height, 0)
    lax.fori_loop(1, rows, greet_row, 0)
    for load in loads:
        load.wait()
    lane = lax.broadcasted_iota(jnp.int32, (planes, LANES), 1)

    def pack_sides(z, acc):
        for f in range(3):
            j = 2 * (f * levels_here + z)
            turned = pltpu.roll(ext[f, z + 1], j, 1)
            mine = (lane == j) | (lane == lax.rem(j + LANES - 1, LANES))
            acc = jnp.where(mine, turned, acc)
        return acc

    side_out[...] = lax.fori_loop(0, levels_here, pack_sides, jnp.zeros((planes, LANES), jnp.float32))
    pl.semaphore_wait(barrier, heights + rows - 2)

    def remote(src, dst, sems, slot, device):
        return pltpu.make_async_remote_copy(
            src_ref=src, dst_ref=dst, send_sem=sems.at[0, slot], recv_sem=sems.at[1, slot],
            device_id=device, device_id_type=MESH,
        )

    halo = [
        remote(side_out, side_in.at[0], side_sem, 0, at(1, 0)),
        remote(side_out, side_in.at[1], side_sem, 1, at(-1, 0)),
        remote(ext.at[:, levels_here], ext.at[:, 0], z_sem, 0, at(0, 1)),
        remote(ext.at[:, 1], ext.at[:, levels_here + 1], z_sem, 1, at(0, -1)),
    ]
    for copy in halo:
        copy.start()

    def leaf_level(z, total):
        classes = class_ref[z]
        area = jnp.zeros((planes, LANES), jnp.float32)
        for c in range(lookup_ref.shape[0]):
            area = jnp.where(classes == c, lookup_ref[c], area)
        area = jnp.where(h * levels_here + z < CANOPY, area, 0.0)
        leaf[z] = area
        return total + area

    leaf_sum[...] = lax.fori_loop(0, levels_here, leaf_level, jnp.zeros((planes, LANES), jnp.float32))
    leaf_copies = [
        remote(leaf_sum, leaf_in.at[0], leaf_sem, 0, at(0, -1)),
        remote(leaf_sum, leaf_in.at[1], leaf_sem, 1, at(0, -2)),
    ]
    for copy in leaf_copies:
        copy.start()

    for copy in halo:
        copy.wait()

    @pl.when(h == 0)
    def _():
        ext[:, 0] = jnp.zeros((3, planes, LANES), jnp.float32)

    @pl.when(h == heights - 1)
    def _():
        ext[:, levels_here + 1] = jnp.zeros((3, planes, LANES), jnp.float32)

    even = lax.rem(lane, 2) == 0
    side[...] = jnp.where(even, pltpu.roll(side_in[0], 1, 1), pltpu.roll(side_in[1], LANES - 1, 1))

    def growth(f, z, u, w):
        q = ext[f, z + 1]
        j = 2 * (f * levels_here + z)
        edge = pltpu.roll(side[...], lax.rem(LANES - j, LANES), 1)
        east = jnp.where(lane == LANES - 1, edge, pltpu.roll(q, LANES - 1, 1))
        west = jnp.where(lane == 0, edge, pltpu.roll(q, 1, 1))
        above = ext[f, z + 2]
        below = ext[f, z]
        advect = u * (east - west) * 0.5 + w * (above - below) * 0.5
        diffuse = VISCOSITY * (east + west + above + below - 4.0 * q)
        return diffuse - advect

    def winds(z, acc):
        u = ext[0, z + 1]
        w = ext[1, z + 1]
        t = ext[2, z + 1]
        friction = DRAG_COEF * leaf[z] * jnp.sqrt(u * u + w * w + SPAN_VAR)
        u_star = u + DT * (growth(0, z, u, w) - friction * u)
        w_star = w + DT * (growth(1, z, u, w) - friction * w + THERMAL_LIFT * t)
        w_star = jnp.where(h * levels_here + z == nz - 1, 0.0, w_star)
        us[z] = u_star
        ws[z + 1] = w_star
        return jnp.where(lane == z, pltpu.roll(u_star, z + 1, 1), acc)

    us_out[...] = lax.fori_loop(0, levels_here, winds, jnp.zeros((planes, LANES), jnp.float32))
    star = [
        remote(us_out, us_in, star_sem, 0, at(1, 0)),
        remote(ws.at[levels_here], ws.at[0], star_sem, 1, at(0, 1)),
    ]
    for copy in star:
        copy.start()
    for copy in star:
        copy.wait()

    @pl.when(h == 0)
    def _():
        ws[0] = jnp.zeros((planes, LANES), jnp.float32)

    def divergence(z, c):
        u_star = us[z]
        edge = pltpu.roll(us_in[...], lax.rem(LANES - z, LANES), 1)
        west = jnp.where(lane == 0, edge, pltpu.roll(u_star, 1, 1))
        d_out[pl.ds(z, planes, stride=levels_here), :] = u_star - west + (ws[z + 1] - ws[z])
        return c

    lax.fori_loop(0, levels_here, divergence, 0)

    def exchange(out, into, sems):
        def send(i, c):
            to = lax.rem(h + i, heights)
            pltpu.make_async_remote_copy(
                src_ref=out.at[pl.ds(to * block, block)], dst_ref=into.at[pl.ds(h * block, block)],
                send_sem=sems.at[0], recv_sem=sems.at[1],
                device_id=(r, to), device_id_type=MESH,
            ).start()
            return c

        lax.fori_loop(1, heights, send, 0)
        mine = pl.ds(h * block, block)
        into[mine] = out[mine]

    def finish(buffer, count, sem):
        part = buffer.at[pl.ds(0, count)]
        pltpu.make_async_copy(part, part, sem).wait()

    exchange(d_out, d_in, a2a_sem)

    for copy in leaf_copies:
        copy.wait()
    above1 = jnp.where(h < heights - 1, leaf_in[0], 0.0)
    above2 = jnp.where(h < heights - 2, leaf_in[1], 0.0)
    over = above1 + above2
    sun = sun_ref[...]
    first = jnp.exp(-(0.5 * over + haze_ref[h * levels_here + levels_here]))

    def heat(k, state):
        over, top = state
        z = levels_here - 1 - k
        over = over + leaf[z]
        bottom = jnp.exp(-(0.5 * over + haze_ref[h * levels_here + z]))
        warming = sun * (top - bottom)
        absorb = jnp.where(paved_ref[...] == 1, PAVED_ABSORB, GRASS_ABSORB)
        warming = warming + jnp.where(h * levels_here + z == 0, sun * bottom * absorb, 0.0)
        t = ext[2, z + 1]
        tn_ref[z] = t + DT * (growth(2, z, ext[0, z + 1], ext[1, z + 1]) + warming)
        return over, bottom

    lax.fori_loop(0, levels_here, heat, (over, first))

    finish(d_in, (heights - 1) * block, a2a_sem.at[1])
    grid = d_in[...].reshape(heights, 2, levels_here, LANES)
    both = jnp.concatenate([grid[:, 0].reshape(nz, LANES), grid[:, 1].reshape(nz, LANES)], axis=1)
    modes = jnp.dot(cosine_ref[...], both, precision=HIGHEST, preferred_element_type=jnp.float32)
    pm[...] = modes

    lane8 = lax.broadcasted_iota(jnp.int32, (8, LANES), 1)
    sub8 = lax.broadcasted_iota(jnp.int32, (8, LANES), 0)

    packed = jnp.zeros((8, LANES), jnp.float32)
    for y in range(2):
        columns = pl.ds(y * LANES, LANES)

        def scan_rows(g, acc, y=y, columns=columns):
            at_rows = pl.ds(pl.multiple_of(g * 8, 8), 8)
            d = pm[at_rows, columns]
            rate = rates_ref[at_rows, :]
            fwd = d
            bwd = d
            for k in range(7):
                s = 1 << k
                rk = jnp.broadcast_to(rate[:, k : k + 1], (8, LANES))
                fwd = fwd + rk * jnp.where(lane8 >= s, pltpu.roll(fwd, s, 1), 0.0)
                bwd = bwd + rk * jnp.where(lane8 < LANES - s, pltpu.roll(bwd, LANES - s, 1), 0.0)
            gain = jnp.broadcast_to(rate[:, 7:8], (8, LANES))
            pm[at_rows, columns] = gain * (fwd + bwd - d)
            j = 2 * (y * groups + g)
            ends = jnp.where(lane8 == 0, bwd, fwd)
            turned = pltpu.roll(ends, j, 1)
            mine = (lane8 == j) | (lane8 == lax.rem(j + LANES - 1, LANES))
            return jnp.where(mine, turned, acc)

        zero = modes[0:8, y * LANES : (y + 1) * LANES]
        packed = lax.fori_loop(0, groups, scan_rows, packed)
        own = jnp.dot(zero, near_ref[...], precision=HIGHEST, preferred_element_type=jnp.float32)
        pm[0:8, columns] = jnp.where(sub8 == 0, own, pm[0:8, columns])
        first_moment = jnp.sum(zero * lane8.astype(jnp.float32), axis=1, keepdims=True)
        slot = (sub8 == 0) & (lane8 == 2 * y * groups)
        packed = jnp.where(slot, jnp.broadcast_to(first_moment, (8, LANES)), packed)

    mom[r] = packed

    def send_moments(i, c):
        pltpu.make_async_remote_copy(
            src_ref=mom.at[r], dst_ref=mom.at[r], send_sem=mom_sem.at[0], recv_sem=mom_sem.at[1],
            device_id=at(i, 0), device_id_type=MESH,
        ).start()
        return c

    lax.fori_loop(1, rows, send_moments, 0)
    finish(mom, rows - 1, mom_sem.at[1])

    def gather_moments(i, state):
        direct, cross = state
        values = mom[lax.rem(r + i, rows)]
        return direct + direct_ref[i] * values, cross + cross_ref[i] * values

    nothing = jnp.zeros((8, LANES), jnp.float32)
    direct, cross = lax.fori_loop(0, rows, gather_moments, (nothing, nothing))
    inflow = direct + jnp.where(
        lax.rem(lane8, 2) == 0, pltpu.roll(cross, 1, 1), pltpu.roll(cross, LANES - 1, 1)
    )

    for y in range(2):
        columns = pl.ds(y * LANES, LANES)

        def add_inflow(g, c, y=y, columns=columns):
            at_rows = pl.ds(pl.multiple_of(g * 8, 8), 8)
            j = 2 * (y * groups + g)
            turned = pltpu.roll(inflow, lax.rem(LANES - j, LANES), 1)
            from_east = jnp.broadcast_to(turned[:, 0:1], (8, LANES))
            from_west = jnp.broadcast_to(turned[:, LANES - 1 : LANES], (8, LANES))
            pm[at_rows, columns] = (
                pm[at_rows, columns]
                + phi_w_ref[at_rows, :] * from_west
                + phi_e_ref[at_rows, :] * from_east
            )
            return c

        lax.fori_loop(0, groups, add_inflow, 0)

    solved = jnp.dot(cosine_t_ref[...], pm[...], precision=HIGHEST, preferred_element_type=jnp.float32)
    halves = [
        solved[:, y * LANES : (y + 1) * LANES].reshape(heights, 1, levels_here, LANES) for y in range(2)
    ]
    p_out[...] = jnp.concatenate(halves, axis=1).reshape(nz * 2, LANES)
    exchange(p_out, p_in, back_sem)
    finish(p_in, (heights - 1) * block, back_sem.at[1])

    def first_columns(z, acc):
        p = p_in[pl.ds(z, planes, stride=levels_here), :]
        return jnp.where(lane == z, pltpu.roll(p, z, 1), acc)

    pc_out[0] = lax.fori_loop(0, levels_here, first_columns, jnp.zeros((planes, LANES), jnp.float32))
    pc_out[1] = p_in[pl.ds(0, planes, stride=levels_here), :]
    edges = [
        remote(pc_out.at[0], pc_in, edge_sem, 0, at(-1, 0)),
        remote(pc_out.at[1], p_up, edge_sem, 1, at(0, -1)),
    ]
    for copy in edges:
        copy.start()
    for copy in edges:
        copy.wait()

    def project(z, p):
        edge = pltpu.roll(pc_in[...], LANES - 1 - z, 1)
        east = jnp.where(lane == LANES - 1, edge, pltpu.roll(p, LANES - 1, 1))
        un_ref[z] = us[z] - (east - p)
        inside = p_in[pl.ds(jnp.minimum(z + 1, levels_here - 1), planes, stride=levels_here), :]
        above = jnp.where(z == levels_here - 1, p_up[...], inside)
        rise = jnp.where(h * levels_here + z == nz - 1, 0.0, above - p)
        wn_ref[z] = ws[z + 1] - rise
        return above

    lax.fori_loop(0, levels_here, project, pc_out[1])

    finish(d_out, (heights - 1) * block, a2a_sem.at[0])
    finish(mom, rows - 1, mom_sem.at[0])
    finish(p_out, (heights - 1) * block, back_sem.at[0])


def solution(mesh):
    rows, heights = mesh.shape["row"], mesh.shape["height"]

    def per_device(u, w, t, classes, paved, sun, lookup):
        levels_here, planes, width = u.shape
        nz = levels_here * heights
        table = tables(nz, width * rows, rows)
        vmem = pl.BlockSpec(memory_space=pltpu.VMEM)
        smem = pl.BlockSpec(memory_space=pltpu.SMEM)
        hbm = pl.BlockSpec(memory_space=pl.ANY)
        field = jax.ShapeDtypeStruct(u.shape, jnp.float32)
        plane = (planes, LANES)
        f32 = jnp.float32
        dma = pltpu.SemaphoreType.DMA
        call = pl.pallas_call(
            functools.partial(kernel, rows, heights),
            out_shape=(field, field, field),
            in_specs=[hbm] * 3 + [vmem] * 3 + [smem] * 2 + [vmem] * 8,
            out_specs=(vmem, vmem, vmem),
            scratch_shapes=[
                pltpu.VMEM((3, levels_here + 2) + plane, f32),
                pltpu.VMEM((levels_here,) + plane, f32),
                pltpu.VMEM(plane, f32),
                pltpu.VMEM((2,) + plane, f32),
                pltpu.VMEM(plane, f32),
                pltpu.VMEM((2,) + plane, f32),
                pltpu.VMEM(plane, f32),
                pltpu.VMEM((levels_here,) + plane, f32),
                pltpu.VMEM((levels_here + 1,) + plane, f32),
                pltpu.VMEM(plane, f32),
                pltpu.VMEM(plane, f32),
                pltpu.VMEM((2 * nz, LANES), f32),
                pltpu.VMEM((2 * nz, LANES), f32),
                pltpu.VMEM((nz, 2 * LANES), f32),
                pltpu.VMEM((rows, 8, LANES), f32),
                pltpu.VMEM((2 * nz, LANES), f32),
                pltpu.VMEM((2 * nz, LANES), f32),
                pltpu.VMEM(plane, f32),
                pltpu.VMEM((2,) + plane, f32),
                pltpu.VMEM(plane, f32),
                dma((3,)), dma((2, 2)), dma((2, 2)), dma((2, 2)), dma((2, 2)),
                dma((2,)), dma((2,)), dma((2,)), dma((2, 2)),
            ],
            compiler_params=pltpu.CompilerParams(
                collective_id=0, has_side_effects=True, vmem_limit_bytes=32 * 1024 * 1024
            ),
        )
        return call(
            u, w, t, classes, paved, sun, lookup, table["haze"], table["cosine"],
            table["cosine_t"], table["rates"], table["phi_west"], table["phi_east"],
            table["near"], table["direct"], table["cross"],
        )

    field = P("height", None, "row")
    line = P(None, "row")
    return jax.shard_map(
        per_device, mesh=mesh, in_specs=(field, field, field, field, line, line, P()),
        out_specs=(field, field, field), check_vma=False,
    )
```

```python
import functools
import math

import jax
import jax.numpy as jnp
import numpy as np
from jax import lax
from jax.experimental import pallas as pl
from jax.experimental.pallas import tpu as pltpu
from jax.sharding import PartitionSpec as P

CANOPY = 48
DT = 0.25
VISCOSITY = 0.05
DRAG_COEF = 0.2
THERMAL_LIFT = 0.2
SPAN_VAR = 0.25
HAZE_EXTINCT = 0.02
PAVED_ABSORB = 0.9
GRASS_ABSORB = 0.5
MESH = pl.DeviceIdType.MESH
HIGHEST = lax.Precision.HIGHEST
LANES = 128


def tables(levels, columns, row_count):
    m = np.arange(levels, dtype=np.float64)
    z = np.arange(levels, dtype=np.float64)
    cosine = np.cos(np.pi * m[:, None] * (z[None, :] + 0.5) / levels)
    cosine *= np.where(m == 0, math.sqrt(1.0 / levels), math.sqrt(2.0 / levels))[:, None]
    mu = 2.0 * np.arcsinh(np.sin(np.pi * m / (2.0 * levels)))
    safe = np.where(m == 0, 1.0, mu)
    gain = np.where(m == 0, 0.0, -1.0 / (2.0 * np.sinh(safe)))
    x = np.arange(LANES, dtype=np.float64)
    scan_e = np.zeros((7, levels, LANES))
    scan_w = np.zeros((7, levels, LANES))
    for k in range(7):
        rate = np.exp(-mu * 2.0**k)[:, None]
        scan_e[k] = np.where(x[None, :] >= 2**k, rate, 0.0)
        scan_w[k] = np.where(x[None, :] < LANES - 2**k, rate, 0.0)
    gain_full = np.broadcast_to(gain[:, None], (levels, LANES))
    phi_west = np.where(m[:, None] == 0, 1.0, gain[:, None] * np.exp(-mu[:, None] * (x + 1.0)))
    phi_east = np.where(m[:, None] == 0, x, gain[:, None] * np.exp(-mu[:, None] * (LANES - x)))
    near = 0.5 * np.abs(x[:, None] - x[None, :]) + x[:, None] * x[None, :] / columns
    lane = np.arange(LANES)
    odd = lane % 2 == 1
    group = np.where(odd, (lane + 1) // 2, lane // 2) % 64
    per_plane = levels // 8
    used = group < 2 * per_plane
    mode = 8 * (group % per_plane)[None, :] + np.arange(8)[:, None]
    mode_mu = mu[mode]
    safe_mu = np.where(mode == 0, 1.0, mode_mu)
    direct = np.zeros((row_count, 8, LANES))
    cross = np.zeros((row_count, 8, LANES))
    for shift in range(row_count):
        to_east = shift if shift else row_count
        to_west = row_count - shift
        steps = np.where(odd, to_west, to_east)[None, :]
        usual = np.exp(-safe_mu * LANES * (steps - 1)) / (1.0 - np.exp(-safe_mu * columns))
        away = float(LANES * shift)
        if shift:
            zero_direct = np.where(odd, away / 2 - away**2 / (2 * columns), 1.0 / columns)
            zero_cross = np.where(odd, -0.5 + away / columns, 0.5 - away / columns)
        else:
            zero_direct = np.zeros(LANES)
            zero_cross = np.zeros(LANES)
        direct[shift] = np.where(mode == 0, zero_direct[None, :], usual) * used
        cross[shift] = np.where(mode == 0, zero_cross[None, :], 0.0) * used
    haze = HAZE_EXTINCT * np.exp(-4.0 * (z + 0.5) / levels)
    haze_above = np.concatenate([np.cumsum(haze[::-1])[::-1], [0.0]])
    f32 = lambda a: np.ascontiguousarray(a, dtype=np.float32)
    return dict(
        cosine=f32(cosine), cosine_t=f32(cosine.T), scan_e=f32(scan_e), scan_w=f32(scan_w), gain=f32(gain_full), phi_west=f32(phi_west),
        phi_east=f32(phi_east), near=f32(near), direct=f32(direct), cross=f32(cross),
        haze=f32(haze_above),
    )


def kernel(
    rows, heights,
    u_hbm, w_hbm, t_hbm, class_hbm, paved_hbm, sun_hbm, lookup_ref, haze_ref,
    cosine_hbm, cosine_t_hbm, scan_e_hbm, scan_w_hbm, gain_hbm, phi_w_hbm, phi_e_hbm, near_hbm,
    direct_hbm, cross_hbm,
    un_hbm, wn_hbm, tn_hbm,
    class_ref, paved_ref, sun_ref,
    cosine_ref, cosine_t_ref, scan_e_ref, scan_w_ref, gain_ref, phi_w_ref, phi_e_ref, near_ref,
    direct_ref, cross_ref,
    un_ref, wn_ref, tn_ref,
    ext, leaf, leaf_sum, leaf_in, side_out, side_in, side, us, ws, us_out, us_in,
    d_out, d_in, pm, mom, p_out, p_in, p_up, pc_out, pc_in,
    in_sem, other_sem, out_sem,
    z_sem, side_sem, leaf_sem, star_sem, a2a_sem, mom_sem, back_sem, edge_sem,
):
    r = lax.axis_index("row")
    h = lax.axis_index("height")
    levels_here = class_ref.shape[0]
    planes = class_ref.shape[1]
    nz = levels_here * heights
    block = 2 * levels_here
    groups = nz // 8

    def at(dr, dh):
        return (lax.rem(r + dr + rows, rows), lax.rem(h + dh + heights, heights))

    loads = [
        pltpu.make_async_copy(ref, ext.at[f, pl.ds(1, levels_here)], in_sem.at[f])
        for f, ref in enumerate((u_hbm, w_hbm, t_hbm))
    ]
    for load in loads:
        load.start()
    others = [
        pltpu.make_async_copy(src, dst, other_sem.at[i])
        for i, (src, dst) in enumerate((
            (class_hbm, class_ref), (paved_hbm, paved_ref), (sun_hbm, sun_ref),
            (cosine_hbm, cosine_ref), (scan_e_hbm, scan_e_ref), (scan_w_hbm, scan_w_ref),
            (gain_hbm, gain_ref), (near_hbm, near_ref), (phi_w_hbm, phi_w_ref),
            (phi_e_hbm, phi_e_ref), (direct_hbm, direct_ref), (cross_hbm, cross_ref),
            (cosine_t_hbm, cosine_t_ref),
        ))
    ]

    barrier = pltpu.get_barrier_semaphore()

    def greet_height(i, c):
        pl.semaphore_signal(barrier, inc=1, device_id=at(0, i), device_id_type=MESH)
        return c

    def greet_row(i, c):
        pl.semaphore_signal(barrier, inc=1, device_id=at(i, 0), device_id_type=MESH)
        return c

    lax.fori_loop(1, heights, greet_height, 0)
    lax.fori_loop(1, rows, greet_row, 0)
    for copy in others:
        copy.start()
    for load in loads:
        load.wait()
    lane = lax.broadcasted_iota(jnp.int32, (planes, LANES), 1)

    def pack_sides(z, acc):
        for f in range(3):
            j = 2 * (f * levels_here + z)
            turned = pltpu.roll(ext[f, z + 1], j, 1)
            mine = (lane == j) | (lane == lax.rem(j + LANES - 1, LANES))
            acc = jnp.where(mine, turned, acc)
        return acc

    side_out[...] = lax.fori_loop(0, levels_here, pack_sides, jnp.zeros((planes, LANES), jnp.float32), unroll=True)
    pl.semaphore_wait(barrier, heights + rows - 2)

    def remote(src, dst, sems, slot, device):
        return pltpu.make_async_remote_copy(
            src_ref=src, dst_ref=dst, send_sem=sems.at[0, slot], recv_sem=sems.at[1, slot],
            device_id=device, device_id_type=MESH,
        )

    halo = [
        remote(side_out, side_in.at[0], side_sem, 0, at(1, 0)),
        remote(side_out, side_in.at[1], side_sem, 1, at(-1, 0)),
        remote(ext.at[:, levels_here], ext.at[:, 0], z_sem, 0, at(0, 1)),
        remote(ext.at[:, 1], ext.at[:, levels_here + 1], z_sem, 1, at(0, -1)),
    ]
    for copy in halo:
        copy.start()

    for copy in others[:3]:
        copy.wait()

    def leaf_level(z, total):
        classes = class_ref[z]
        area = jnp.zeros((planes, LANES), jnp.float32)
        for c in range(lookup_ref.shape[0]):
            area = jnp.where(classes == c, lookup_ref[c], area)
        area = jnp.where(h * levels_here + z < CANOPY, area, 0.0)
        leaf[z] = area
        return total + area

    leaf_sum[...] = lax.fori_loop(0, levels_here, leaf_level, jnp.zeros((planes, LANES), jnp.float32))
    leaf_copies = [
        remote(leaf_sum, leaf_in.at[0], leaf_sem, 0, at(0, -1)),
        remote(leaf_sum, leaf_in.at[1], leaf_sem, 1, at(0, -2)),
    ]
    for copy in leaf_copies:
        copy.start()

    for copy in halo:
        copy.wait()

    @pl.when(h == 0)
    def _():
        ext[:, 0] = jnp.zeros((3, planes, LANES), jnp.float32)

    @pl.when(h == heights - 1)
    def _():
        ext[:, levels_here + 1] = jnp.zeros((3, planes, LANES), jnp.float32)

    even = lax.rem(lane, 2) == 0
    side[...] = jnp.where(even, pltpu.roll(side_in[0], 1, 1), pltpu.roll(side_in[1], LANES - 1, 1))

    def growth(f, z, u, w):
        q = ext[f, z + 1]
        j = 2 * (f * levels_here + z)
        edge = pltpu.roll(side[...], lax.rem(LANES - j, LANES), 1)
        east = jnp.where(lane == LANES - 1, edge, pltpu.roll(q, LANES - 1, 1))
        west = jnp.where(lane == 0, edge, pltpu.roll(q, 1, 1))
        above = ext[f, z + 2]
        below = ext[f, z]
        advect = u * (east - west) * 0.5 + w * (above - below) * 0.5
        diffuse = VISCOSITY * (east + west + above + below - 4.0 * q)
        return diffuse - advect

    def winds(z, acc):
        u = ext[0, z + 1]
        w = ext[1, z + 1]
        t = ext[2, z + 1]
        friction = DRAG_COEF * leaf[z] * jnp.sqrt(u * u + w * w + SPAN_VAR)
        u_star = u + DT * (growth(0, z, u, w) - friction * u)
        w_star = w + DT * (growth(1, z, u, w) - friction * w + THERMAL_LIFT * t)
        w_star = jnp.where(h * levels_here + z == nz - 1, 0.0, w_star)
        us[z] = u_star
        ws[z + 1] = w_star
        return jnp.where(lane == z, pltpu.roll(u_star, z + 1, 1), acc)

    us_out[...] = lax.fori_loop(0, levels_here, winds, jnp.zeros((planes, LANES), jnp.float32))
    star = [
        remote(us_out, us_in, star_sem, 0, at(1, 0)),
        remote(ws.at[levels_here], ws.at[0], star_sem, 1, at(0, 1)),
    ]
    for copy in star:
        copy.start()
    for copy in star:
        copy.wait()

    @pl.when(h == 0)
    def _():
        ws[0] = jnp.zeros((planes, LANES), jnp.float32)

    def divergence(z, c):
        u_star = us[z]
        edge = pltpu.roll(us_in[...], lax.rem(LANES - z, LANES), 1)
        west = jnp.where(lane == 0, edge, pltpu.roll(u_star, 1, 1))
        d_out[pl.ds(z, planes, stride=levels_here), :] = u_star - west + (ws[z + 1] - ws[z])
        return c

    lax.fori_loop(0, levels_here, divergence, 0)

    def exchange(out, into, sems):
        def send(i, c):
            to = lax.rem(h + i, heights)
            pltpu.make_async_remote_copy(
                src_ref=out.at[pl.ds(to * block, block)], dst_ref=into.at[pl.ds(h * block, block)],
                send_sem=sems.at[0], recv_sem=sems.at[1],
                device_id=(r, to), device_id_type=MESH,
            ).start()
            return c

        lax.fori_loop(1, heights, send, 0)
        mine = pl.ds(h * block, block)
        into[mine] = out[mine]

    def finish(buffer, count, sem):
        part = buffer.at[pl.ds(0, count)]
        pltpu.make_async_copy(part, part, sem).wait()

    exchange(d_out, d_in, a2a_sem)

    for copy in leaf_copies:
        copy.wait()
    above1 = jnp.where(h < heights - 1, leaf_in[0], 0.0)
    above2 = jnp.where(h < heights - 2, leaf_in[1], 0.0)
    over = above1 + above2
    sun = sun_ref[...]
    first = jnp.exp(-(0.5 * over + haze_ref[h * levels_here + levels_here]))

    def heat(k, state):
        over, top = state
        z = levels_here - 1 - k
        over = over + leaf[z]
        bottom = jnp.exp(-(0.5 * over + haze_ref[h * levels_here + z]))
        warming = sun * (top - bottom)
        absorb = jnp.where(paved_ref[...] == 1, PAVED_ABSORB, GRASS_ABSORB)
        warming = warming + jnp.where(h * levels_here + z == 0, sun * bottom * absorb, 0.0)
        t = ext[2, z + 1]
        tn_ref[z] = t + DT * (growth(2, z, ext[0, z + 1], ext[1, z + 1]) + warming)
        return over, bottom

    lax.fori_loop(0, levels_here, heat, (over, first))
    warm_out = pltpu.make_async_copy(tn_ref, tn_hbm, out_sem.at[2])
    warm_out.start()
    for copy in others[3:]:
        copy.wait()

    finish(d_in, (heights - 1) * block, a2a_sem.at[1])
    grid = d_in[...].reshape(heights, 2, levels_here, LANES)
    both = jnp.concatenate([grid[:, 0].reshape(nz, LANES), grid[:, 1].reshape(nz, LANES)], axis=1)
    modes = jnp.dot(cosine_ref[...], both, precision=HIGHEST, preferred_element_type=jnp.float32)

    lane8 = lax.broadcasted_iota(jnp.int32, (8, LANES), 1)
    sub8 = lax.broadcasted_iota(jnp.int32, (8, LANES), 0)
    chunk = min(64, nz)
    lane_c = lax.broadcasted_iota(jnp.int32, (chunk, LANES), 1)

    packed = jnp.zeros((8, LANES), jnp.float32)
    for y in range(2):
        columns = slice(y * LANES, (y + 1) * LANES)
        for start in range(0, nz, chunk):
            part = slice(start, start + chunk)
            d = modes[part, columns]
            fwd = d
            bwd = d
            for k in range(7):
                s = 1 << k
                fwd = fwd + scan_e_ref[k, part, :] * pltpu.roll(fwd, s, 1)
                bwd = bwd + scan_w_ref[k, part, :] * pltpu.roll(bwd, LANES - s, 1)
            local = gain_ref[part, :] * (fwd + bwd - d)
            ends = jnp.where(lane_c == 0, bwd, fwd)
            if start == 0:
                zero = d[0:8]
                own = jnp.dot(
                    zero, near_ref[...], precision=HIGHEST, preferred_element_type=jnp.float32
                )
                first_moment = jnp.sum(zero * lane8.astype(jnp.float32), axis=1, keepdims=True)
                slot = (sub8 == 0) & (lane8 == 0)
                pm[0:8, columns] = jnp.where(sub8 == 0, own, local[0:8])
                pm[8:chunk, columns] = local[8:]
            else:
                pm[part, columns] = local
            for i in range(chunk // 8):
                value = ends[8 * i : 8 * i + 8]
                if start == 0 and i == 0:
                    value = jnp.where(slot, jnp.broadcast_to(first_moment, (8, LANES)), value)
                j = 2 * (y * groups + start // 8 + i)
                turned = pltpu.roll(value, j, 1) if j else value
                mine = (lane8 == j) | (lane8 == (j + LANES - 1) % LANES)
                packed = jnp.where(mine, turned, packed)

    mom[r] = packed

    def send_moments(i, c):
        pltpu.make_async_remote_copy(
            src_ref=mom.at[r], dst_ref=mom.at[r], send_sem=mom_sem.at[0], recv_sem=mom_sem.at[1],
            device_id=at(i, 0), device_id_type=MESH,
        ).start()
        return c

    lax.fori_loop(1, rows, send_moments, 0)
    finish(mom, rows - 1, mom_sem.at[1])

    def gather_moments(i, state):
        direct, cross = state
        values = mom[lax.rem(r + i, rows)]
        return direct + direct_ref[i] * values, cross + cross_ref[i] * values

    nothing = jnp.zeros((8, LANES), jnp.float32)
    direct, cross = lax.fori_loop(0, rows, gather_moments, (nothing, nothing))
    inflow = direct + jnp.where(
        lax.rem(lane8, 2) == 0, pltpu.roll(cross, 1, 1), pltpu.roll(cross, LANES - 1, 1)
    )

    for y in range(2):
        columns = slice(y * LANES, (y + 1) * LANES)
        for g in range(groups):
            part = slice(8 * g, 8 * g + 8)
            j = 2 * (y * groups + g)
            west = (j + LANES - 1) % LANES
            from_east = jnp.broadcast_to(inflow[:, j : j + 1], (8, LANES))
            from_west = jnp.broadcast_to(inflow[:, west : west + 1], (8, LANES))
            pm[part, columns] = (
                pm[part, columns] + phi_w_ref[part, :] * from_west + phi_e_ref[part, :] * from_east
            )

    solved = jnp.dot(cosine_t_ref[...], pm[...], precision=HIGHEST, preferred_element_type=jnp.float32)
    halves = [
        solved[:, y * LANES : (y + 1) * LANES].reshape(heights, 1, levels_here, LANES) for y in range(2)
    ]
    p_out[...] = jnp.concatenate(halves, axis=1).reshape(nz * 2, LANES)
    exchange(p_out, p_in, back_sem)
    finish(p_in, (heights - 1) * block, back_sem.at[1])

    def first_columns(z, acc):
        p = p_in[pl.ds(z, planes, stride=levels_here), :]
        return jnp.where(lane == z, pltpu.roll(p, z, 1), acc)

    pc_out[0] = lax.fori_loop(0, levels_here, first_columns, jnp.zeros((planes, LANES), jnp.float32))
    pc_out[1] = p_in[pl.ds(0, planes, stride=levels_here), :]
    edges = [
        remote(pc_out.at[0], pc_in, edge_sem, 0, at(-1, 0)),
        remote(pc_out.at[1], p_up, edge_sem, 1, at(0, -1)),
    ]
    for copy in edges:
        copy.start()
    for copy in edges:
        copy.wait()

    def project(z, p):
        edge = pltpu.roll(pc_in[...], LANES - 1 - z, 1)
        east = jnp.where(lane == LANES - 1, edge, pltpu.roll(p, LANES - 1, 1))
        un_ref[z] = us[z] - (east - p)
        inside = p_in[pl.ds(jnp.minimum(z + 1, levels_here - 1), planes, stride=levels_here), :]
        above = jnp.where(z == levels_here - 1, p_up[...], inside)
        rise = jnp.where(h * levels_here + z == nz - 1, 0.0, above - p)
        wn_ref[z] = ws[z + 1] - rise
        return above

    lax.fori_loop(0, levels_here, project, pc_out[1])
    ends_out = [
        pltpu.make_async_copy(un_ref, un_hbm, out_sem.at[0]),
        pltpu.make_async_copy(wn_ref, wn_hbm, out_sem.at[1]),
    ]
    for copy in ends_out:
        copy.start()
    warm_out.wait()
    for copy in ends_out:
        copy.wait()

    finish(d_out, (heights - 1) * block, a2a_sem.at[0])
    finish(mom, rows - 1, mom_sem.at[0])
    finish(p_out, (heights - 1) * block, back_sem.at[0])


def solution(mesh):
    rows, heights = mesh.shape["row"], mesh.shape["height"]

    def per_device(u, w, t, classes, paved, sun, lookup):
        levels_here, planes, width = u.shape
        nz = levels_here * heights
        table = tables(nz, width * rows, rows)
        smem = pl.BlockSpec(memory_space=pltpu.SMEM)
        hbm = pl.BlockSpec(memory_space=pl.ANY)
        field = jax.ShapeDtypeStruct(u.shape, jnp.float32)
        plane = (planes, LANES)
        f32 = jnp.float32
        dma = pltpu.SemaphoreType.DMA
        call = pl.pallas_call(
            functools.partial(kernel, rows, heights),
            out_shape=(field, field, field),
            in_specs=[hbm] * 6 + [smem] * 2 + [hbm] * 10,
            out_specs=(hbm, hbm, hbm),
            scratch_shapes=[
                pltpu.VMEM((levels_here,) + plane, jnp.int32),
                pltpu.VMEM(plane, jnp.int32),
                pltpu.VMEM(plane, f32),
                pltpu.VMEM((nz, nz), f32),
                pltpu.VMEM((nz, nz), f32),
                pltpu.VMEM((7, nz, LANES), f32),
                pltpu.VMEM((7, nz, LANES), f32),
                pltpu.VMEM((nz, LANES), f32),
                pltpu.VMEM((nz, LANES), f32),
                pltpu.VMEM((nz, LANES), f32),
                pltpu.VMEM((LANES, LANES), f32),
                pltpu.VMEM((rows, 8, LANES), f32),
                pltpu.VMEM((rows, 8, LANES), f32),
                pltpu.VMEM(u.shape, f32),
                pltpu.VMEM(u.shape, f32),
                pltpu.VMEM(u.shape, f32),
                pltpu.VMEM((3, levels_here + 2) + plane, f32),
                pltpu.VMEM((levels_here,) + plane, f32),
                pltpu.VMEM(plane, f32),
                pltpu.VMEM((2,) + plane, f32),
                pltpu.VMEM(plane, f32),
                pltpu.VMEM((2,) + plane, f32),
                pltpu.VMEM(plane, f32),
                pltpu.VMEM((levels_here,) + plane, f32),
                pltpu.VMEM((levels_here + 1,) + plane, f32),
                pltpu.VMEM(plane, f32),
                pltpu.VMEM(plane, f32),
                pltpu.VMEM((2 * nz, LANES), f32),
                pltpu.VMEM((2 * nz, LANES), f32),
                pltpu.VMEM((nz, 2 * LANES), f32),
                pltpu.VMEM((rows, 8, LANES), f32),
                pltpu.VMEM((2 * nz, LANES), f32),
                pltpu.VMEM((2 * nz, LANES), f32),
                pltpu.VMEM(plane, f32),
                pltpu.VMEM((2,) + plane, f32),
                pltpu.VMEM(plane, f32),
                dma((3,)), dma((13,)), dma((3,)), dma((2, 2)), dma((2, 2)), dma((2, 2)), dma((2, 2)),
                dma((2,)), dma((2,)), dma((2,)), dma((2, 2)),
            ],
            compiler_params=pltpu.CompilerParams(
                collective_id=0, has_side_effects=True, vmem_limit_bytes=60 * 1024 * 1024
            ),
        )
        return call(
            u, w, t, classes, paved, sun, lookup, table["haze"], table["cosine"],
            table["cosine_t"], table["scan_e"], table["scan_w"], table["gain"],
            table["phi_west"], table["phi_east"], table["near"], table["direct"], table["cross"],
        )

    field = P("height", None, "row")
    line = P(None, "row")
    return jax.shard_map(
        per_device, mesh=mesh, in_specs=(field, field, field, field, line, line, P()),
        out_specs=(field, field, field), check_vma=False,
    )
```

```python
import functools
import math

import jax
import jax.numpy as jnp
import numpy as np
from jax import lax
from jax.experimental import pallas as pl
from jax.experimental.pallas import tpu as pltpu
from jax.sharding import PartitionSpec as P

CANOPY = 48
DT = 0.25
VISCOSITY = 0.05
DRAG_COEF = 0.2
THERMAL_LIFT = 0.2
SPAN_VAR = 0.25
HAZE_EXTINCT = 0.02
PAVED_ABSORB = 0.9
GRASS_ABSORB = 0.5
MESH = pl.DeviceIdType.MESH
UNROLL = True
HIGHEST = lax.Precision.HIGHEST
LANES = 128


def tables(levels, columns, row_count):
    m = np.arange(levels, dtype=np.float64)
    z = np.arange(levels, dtype=np.float64)
    cosine = np.cos(np.pi * m[:, None] * (z[None, :] + 0.5) / levels)
    cosine *= np.where(m == 0, math.sqrt(1.0 / levels), math.sqrt(2.0 / levels))[:, None]
    mu = 2.0 * np.arcsinh(np.sin(np.pi * m / (2.0 * levels)))
    safe = np.where(m == 0, 1.0, mu)
    gain = np.where(m == 0, 0.0, -1.0 / (2.0 * np.sinh(safe)))
    x = np.arange(LANES, dtype=np.float64)
    scan_e = np.zeros((7, levels, LANES))
    scan_w = np.zeros((7, levels, LANES))
    for k in range(7):
        rate = np.exp(-mu * 2.0**k)[:, None]
        scan_e[k] = np.where(x[None, :] >= 2**k, rate, 0.0)
        scan_w[k] = np.where(x[None, :] < LANES - 2**k, rate, 0.0)
    gain_full = np.broadcast_to(gain[:, None], (levels, LANES))
    phi_west = np.where(m[:, None] == 0, 1.0, gain[:, None] * np.exp(-mu[:, None] * (x + 1.0)))
    phi_east = np.where(m[:, None] == 0, x, gain[:, None] * np.exp(-mu[:, None] * (LANES - x)))
    near = 0.5 * np.abs(x[:, None] - x[None, :]) + x[:, None] * x[None, :] / columns
    near_next = np.broadcast_to((0.5 * (LANES - x) + LANES * x / columns)[:, None], (LANES, LANES))
    lane = np.arange(LANES)
    odd = lane % 2 == 1
    group = np.where(odd, (lane + 1) // 2, lane // 2) % 64
    per_plane = levels // 8
    used = group < 2 * per_plane
    mode = 8 * (group % per_plane)[None, :] + np.arange(8)[:, None]
    mode_mu = mu[mode]
    safe_mu = np.where(mode == 0, 1.0, mode_mu)
    direct = np.zeros((row_count, 8, LANES))
    cross = np.zeros((row_count, 8, LANES))
    for shift in range(row_count):
        to_east = shift if shift else row_count
        to_west = row_count - shift
        steps = np.where(odd, to_west, to_east)[None, :]
        usual = np.exp(-safe_mu * LANES * (steps - 1)) / (1.0 - np.exp(-safe_mu * columns))
        away = float(LANES * shift)
        if shift:
            zero_direct = np.where(odd, away / 2 - away**2 / (2 * columns), 1.0 / columns)
            zero_cross = np.where(odd, -0.5 + away / columns, 0.5 - away / columns)
        else:
            zero_direct = np.zeros(LANES)
            zero_cross = np.zeros(LANES)
        direct[shift] = np.where(mode == 0, zero_direct[None, :], usual) * used
        cross[shift] = np.where(mode == 0, zero_cross[None, :], 0.0) * used
    haze = HAZE_EXTINCT * np.exp(-4.0 * (z + 0.5) / levels)
    haze_above = np.concatenate([np.cumsum(haze[::-1])[::-1], [0.0]])
    f32 = lambda a: np.ascontiguousarray(a, dtype=np.float32)
    return dict(
        cosine=f32(cosine), cosine_t=f32(cosine.T), scan_e=f32(scan_e), scan_w=f32(scan_w), gain=f32(gain_full), phi_west=f32(phi_west),
        phi_east=f32(phi_east), near=f32(near), near_next=f32(near_next), direct=f32(direct), cross=f32(cross),
        haze=f32(haze_above),
    )


def kernel(
    rows, heights,
    u_hbm, w_hbm, t_hbm, class_hbm, paved_hbm, sun_hbm, lookup_ref, haze_ref,
    cosine_hbm, cosine_t_hbm, scan_e_hbm, scan_w_hbm, gain_hbm, phi_w_hbm, phi_e_hbm, near_hbm,
    near_next_hbm, direct_hbm, cross_hbm,
    us_hbm, ws_hbm, p_in, tn_hbm,
    class_ref, paved_ref, sun_ref,
    cosine_ref, cosine_t_ref, scan_e_ref, scan_w_ref, gain_ref, phi_w_ref, phi_e_ref, near_ref,
    near_next_ref, direct_ref, cross_ref,
    tn_ref,
    ext, leaf, leaf_sum, leaf_in, low_out, low_in, side_out, side_in, side, u_side, us, ws,
    d_out, d_in, pm, extra, mom, p_out,
    in_sem, other_sem, out_sem,
    z_sem, side_sem, leaf_sem, a2a_sem, mom_sem, back_sem,
):
    r = lax.axis_index("row")
    h = lax.axis_index("height")
    levels_here = class_ref.shape[0]
    planes = class_ref.shape[1]
    nz = levels_here * heights
    block = 2 * levels_here
    groups = nz // 8

    def at(dr, dh):
        return (lax.rem(r + dr + rows, rows), lax.rem(h + dh + heights, heights))

    first_class = pltpu.make_async_copy(class_hbm, class_ref, other_sem.at[0])
    loads = [
        pltpu.make_async_copy(ref, ext.at[f, pl.ds(1, levels_here)], in_sem.at[f])
        for f, ref in enumerate((u_hbm, w_hbm, t_hbm))
    ]
    for load in loads:
        load.start()
    first_class.start()
    others = [
        pltpu.make_async_copy(src, dst, other_sem.at[i + 1])
        for i, (src, dst) in enumerate((
            (paved_hbm, paved_ref), (sun_hbm, sun_ref),
            (cosine_hbm, cosine_ref), (scan_e_hbm, scan_e_ref), (scan_w_hbm, scan_w_ref),
            (gain_hbm, gain_ref), (near_hbm, near_ref), (phi_w_hbm, phi_w_ref),
            (phi_e_hbm, phi_e_ref), (near_next_hbm, near_next_ref), (direct_hbm, direct_ref), (cross_hbm, cross_ref),
            (cosine_t_hbm, cosine_t_ref),
        ))
    ]

    barrier = pltpu.get_barrier_semaphore()

    def greet_height(i, c):
        pl.semaphore_signal(barrier, inc=1, device_id=at(0, i), device_id_type=MESH)
        return c

    def greet_row(i, c):
        pl.semaphore_signal(barrier, inc=1, device_id=at(i, 0), device_id_type=MESH)
        return c

    lax.fori_loop(1, heights, greet_height, 0)
    lax.fori_loop(1, rows, greet_row, 0)
    corners = (at(1, 1), at(1, -1), at(-1, 1))
    for corner in (*corners, at(-1, -1)):
        pl.semaphore_signal(barrier, inc=1, device_id=corner, device_id_type=MESH)
    for copy in others:
        copy.start()
    for load in loads:
        load.wait()
    lane = lax.broadcasted_iota(jnp.int32, (planes, LANES), 1)

    def leaf_of(classes):
        area = jnp.zeros((planes, LANES), jnp.float32)
        for c in range(lookup_ref.shape[0]):
            area = jnp.where(classes == c, lookup_ref[c], area)
        return area

    def pack_sides(z, acc):
        for f in range(3):
            j = 2 * (f * levels_here + z)
            turned = pltpu.roll(ext[f, z + 1], j + 1, 1)
            acc = jnp.where((lane == j) | (lane == j + 1), turned, acc)
        j = 6 * levels_here + 2 * z
        turned = pltpu.roll(ext[0, z + 1], lax.rem(j + 2, LANES), 1)
        acc = jnp.where(lane == j, turned, acc)
        turned = pltpu.roll(class_ref[z].astype(jnp.float32), lax.rem(j + 2, LANES), 1)
        return jnp.where(lane == j + 1, turned, acc)

    first_class.wait()
    side_out[...] = lax.fori_loop(0, levels_here, pack_sides, jnp.zeros((planes, LANES), jnp.float32), unroll=True)
    low_out[0] = ext[1, levels_here - 1]
    low_out[1] = leaf_of(class_ref[levels_here - 1])
    pl.semaphore_wait(barrier, heights + rows + 2)

    def remote(src, dst, sems, slot, device):
        return pltpu.make_async_remote_copy(
            src_ref=src, dst_ref=dst, send_sem=sems.at[0, slot], recv_sem=sems.at[1, slot],
            device_id=device, device_id_type=MESH,
        )

    halo = [
        remote(side_out, side_in.at[0], side_sem, 0, at(1, 0)),
        remote(side_out, side_in.at[1], side_sem, 1, at(-1, 0)),
        remote(ext.at[:, levels_here], ext.at[:, 0], z_sem, 0, at(0, 1)),
        remote(ext.at[:, 1], ext.at[:, levels_here + 1], z_sem, 1, at(0, -1)),
        remote(low_out, low_in, z_sem, 2, at(0, 1)),
    ] + [
        remote(side_out, side_in.at[2 + i], side_sem, 2 + i, corner) for i, corner in enumerate(corners)
    ]
    for copy in halo:
        copy.start()

    def leaf_level(z, total):
        area = leaf_of(class_ref[z])
        area = jnp.where(h * levels_here + z < CANOPY, area, 0.0)
        leaf[z] = area
        return total + area

    leaf_sum[...] = lax.fori_loop(0, levels_here, leaf_level, jnp.zeros((planes, LANES), jnp.float32), unroll=UNROLL)
    leaf_copies = [
        remote(leaf_sum, leaf_in.at[0], leaf_sem, 0, at(0, -1)),
        remote(leaf_sum, leaf_in.at[1], leaf_sem, 1, at(0, -2)),
    ]
    for copy in leaf_copies:
        copy.start()

    for copy in halo:
        copy.wait()

    @pl.when(h == 0)
    def _():
        ext[:, 0] = jnp.zeros((3, planes, LANES), jnp.float32)

    @pl.when(h == heights - 1)
    def _():
        ext[:, levels_here + 1] = jnp.zeros((3, planes, LANES), jnp.float32)

    even = lax.rem(lane, 2) == 0
    from_left = side_in[0]
    side[...] = jnp.where(even, pltpu.roll(side_in[1], LANES - 1, 1), pltpu.roll(from_left, 1, 1))

    def stretch(q, u, w, east, west, above, below):
        advect = u * (east - west) * 0.5 + w * (above - below) * 0.5
        diffuse = VISCOSITY * (east + west + above + below - 4.0 * q)
        return diffuse - advect

    def drag(area, u, w):
        return DRAG_COEF * area * jnp.sqrt(u * u + w * w + SPAN_VAR)

    last = 2 * (levels_here - 1)
    w_left = pltpu.roll(from_left, LANES - 2 * levels_here, 1)
    u_far = pltpu.roll(from_left, LANES - 6 * levels_here, 1)
    class_left = pltpu.roll(from_left, LANES - 6 * levels_here - 1, 1)
    z_of_lane = h * levels_here + lane // 2
    area_left = jnp.where(z_of_lane < CANOPY, leaf_of(class_left), 0.0)
    u_east = pltpu.roll(side_out[...], LANES - 1, 1)
    corner_above = jnp.where(h < heights - 1, pltpu.roll(side_in[3], last, 1), 0.0)
    corner_below = jnp.where(h > 0, pltpu.roll(side_in[2], LANES - last, 1), 0.0)
    u_above = jnp.where(lane == last, corner_above, pltpu.roll(from_left, LANES - 2, 1))
    u_below = jnp.where(lane == 0, corner_below, pltpu.roll(from_left, 2, 1))
    u_side[...] = from_left + DT * (
        stretch(from_left, from_left, w_left, u_east, u_far, u_above, u_below)
        - drag(area_left, from_left, w_left) * from_left
    )

    u_low, w_low, t_low = ext[0, 0], ext[1, 0], ext[2, 0]
    j = 2 * (2 * levels_here - 1)
    w_east = jnp.where(
        lane == LANES - 1, pltpu.roll(side_in[4], LANES - 2 - j, 1), pltpu.roll(w_low, LANES - 1, 1)
    )
    w_west = jnp.where(lane == 0, pltpu.roll(side_in[2], LANES - j, 1), pltpu.roll(w_low, 1, 1))
    area_low = jnp.where(h * levels_here - 1 < CANOPY, low_in[1], 0.0)
    w_star_low = w_low + DT * (
        stretch(w_low, u_low, w_low, w_east, w_west, ext[1, 1], low_in[0])
        - drag(area_low, u_low, w_low) * w_low
        + THERMAL_LIFT * t_low
    )
    w_star_low = jnp.where(h > 0, w_star_low, 0.0)

    def growth(f, z, u, w):
        q = ext[f, z + 1]
        j = 2 * (f * levels_here + z)
        edge = pltpu.roll(side[...], LANES - 1 - j, 1)
        east = jnp.where(lane == LANES - 1, edge, pltpu.roll(q, LANES - 1, 1))
        west = jnp.where(lane == 0, edge, pltpu.roll(q, 1, 1))
        return stretch(q, u, w, east, west, ext[f, z + 2], ext[f, z])

    def winds(z, w_below):
        u = ext[0, z + 1]
        w = ext[1, z + 1]
        t = ext[2, z + 1]
        friction = drag(leaf[z], u, w)
        u_star = u + DT * (growth(0, z, u, w) - friction * u)
        w_star = w + DT * (growth(1, z, u, w) - friction * w + THERMAL_LIFT * t)
        w_star = jnp.where(h * levels_here + z == nz - 1, 0.0, w_star)
        us[z] = u_star
        ws[z] = w_star
        edge = pltpu.roll(u_side[...], lax.rem(LANES - 2 * z, LANES), 1)
        west = jnp.where(lane == 0, edge, pltpu.roll(u_star, 1, 1))
        d_out[pl.ds(z, planes, stride=levels_here), :] = u_star - west + (w_star - w_below)
        return w_star

    lax.fori_loop(0, levels_here, winds, w_star_low, unroll=UNROLL)

    def exchange(out, into, sems):
        def send(i, c):
            to = lax.rem(h + i, heights)
            pltpu.make_async_remote_copy(
                src_ref=out.at[pl.ds(to * block, block)], dst_ref=into.at[pl.ds(h * block, block)],
                send_sem=sems.at[0], recv_sem=sems.at[1],
                device_id=(r, to), device_id_type=MESH,
            ).start()
            return c

        lax.fori_loop(1, heights, send, 0)
        mine = pl.ds(h * block, block)
        into[mine] = out[mine]

    def finish(buffer, count, sem):
        part = buffer.at[pl.ds(0, count)]
        pltpu.make_async_copy(part, part, sem).wait()

    exchange(d_out, d_in, a2a_sem)
    star_out = [
        pltpu.make_async_copy(us, us_hbm, out_sem.at[0]),
        pltpu.make_async_copy(ws, ws_hbm, out_sem.at[1]),
    ]
    for copy in star_out:
        copy.start()
    for copy in others[:2]:
        copy.wait()

    for copy in leaf_copies:
        copy.wait()
    above1 = jnp.where(h < heights - 1, leaf_in[0], 0.0)
    above2 = jnp.where(h < heights - 2, leaf_in[1], 0.0)
    over = above1 + above2
    sun = sun_ref[...]
    first = jnp.exp(-(0.5 * over + haze_ref[h * levels_here + levels_here]))

    def heat(k, state):
        over, top = state
        z = levels_here - 1 - k
        over = over + leaf[z]
        bottom = jnp.exp(-(0.5 * over + haze_ref[h * levels_here + z]))
        warming = sun * (top - bottom)
        absorb = jnp.where(paved_ref[...] == 1, PAVED_ABSORB, GRASS_ABSORB)
        warming = warming + jnp.where(h * levels_here + z == 0, sun * bottom * absorb, 0.0)
        t = ext[2, z + 1]
        tn_ref[z] = t + DT * (growth(2, z, ext[0, z + 1], ext[1, z + 1]) + warming)
        return over, bottom

    lax.fori_loop(0, levels_here, heat, (over, first), unroll=UNROLL)
    warm_out = pltpu.make_async_copy(tn_ref, tn_hbm, out_sem.at[2])
    warm_out.start()
    for copy in others[2:]:
        copy.wait()

    finish(d_in, (heights - 1) * block, a2a_sem.at[1])
    grid = d_in[...].reshape(heights, 2, levels_here, LANES)
    both = jnp.concatenate([grid[:, 0].reshape(nz, LANES), grid[:, 1].reshape(nz, LANES)], axis=1)
    modes = jnp.dot(cosine_ref[...], both, precision=HIGHEST, preferred_element_type=jnp.float32)

    lane8 = lax.broadcasted_iota(jnp.int32, (8, LANES), 1)
    sub8 = lax.broadcasted_iota(jnp.int32, (8, LANES), 0)
    chunk = min(64, nz)
    lane_c = lax.broadcasted_iota(jnp.int32, (chunk, LANES), 1)

    packed = jnp.zeros((8, LANES), jnp.float32)
    own_next = []
    for y in range(2):
        columns = slice(y * LANES, (y + 1) * LANES)
        for start in range(0, nz, chunk):
            part = slice(start, start + chunk)
            d = modes[part, columns]
            fwd = d
            bwd = d
            for k in range(7):
                s = 1 << k
                fwd = fwd + scan_e_ref[k, part, :] * pltpu.roll(fwd, s, 1)
                bwd = bwd + scan_w_ref[k, part, :] * pltpu.roll(bwd, LANES - s, 1)
            local = gain_ref[part, :] * (fwd + bwd - d)
            ends = jnp.where(lane_c == 0, bwd, fwd)
            if start == 0:
                zero = d[0:8]
                own = jnp.dot(
                    zero, near_ref[...], precision=HIGHEST, preferred_element_type=jnp.float32
                )
                own_next.append(jnp.dot(
                    zero, near_next_ref[...], precision=HIGHEST, preferred_element_type=jnp.float32
                ))
                first_moment = jnp.sum(zero * lane8.astype(jnp.float32), axis=1, keepdims=True)
                slot = (sub8 == 0) & (lane8 == 0)
                pm[0:8, columns] = jnp.where(sub8 == 0, own, local[0:8])
                pm[8:chunk, columns] = local[8:]
            else:
                pm[part, columns] = local
            for i in range(chunk // 8):
                value = ends[8 * i : 8 * i + 8]
                if start == 0 and i == 0:
                    value = jnp.where(slot, jnp.broadcast_to(first_moment, (8, LANES)), value)
                j = 2 * (y * groups + start // 8 + i)
                turned = pltpu.roll(value, j, 1) if j else value
                mine = (lane8 == j) | (lane8 == (j + LANES - 1) % LANES)
                packed = jnp.where(mine, turned, packed)

    mom[r] = packed

    def send_moments(i, c):
        pltpu.make_async_remote_copy(
            src_ref=mom.at[r], dst_ref=mom.at[r], send_sem=mom_sem.at[0], recv_sem=mom_sem.at[1],
            device_id=at(i, 0), device_id_type=MESH,
        ).start()
        return c

    lax.fori_loop(1, rows, send_moments, 0)
    finish(mom, rows - 1, mom_sem.at[1])

    def gather_moments(i, state):
        direct, cross = state
        values = mom[lax.rem(r + i, rows)]
        return direct + direct_ref[i] * values, cross + cross_ref[i] * values

    nothing = jnp.zeros((8, LANES), jnp.float32)
    direct, cross = lax.fori_loop(0, rows, gather_moments, (nothing, nothing))
    inflow = direct + jnp.where(
        lax.rem(lane8, 2) == 0, pltpu.roll(cross, 1, 1), pltpu.roll(cross, LANES - 1, 1)
    )

    for g in range(groups):
        part = slice(8 * g, 8 * g + 8)
        rate, gain = scan_w_ref[0, part, :], gain_ref[part, :]
        next_columns = []
        for y in range(2):
            columns = slice(y * LANES, (y + 1) * LANES)
            j = 2 * (y * groups + g)
            west = (j + LANES - 1) % LANES
            from_east = jnp.broadcast_to(inflow[:, j : j + 1], (8, LANES))
            from_west = jnp.broadcast_to(inflow[:, west : west + 1], (8, LANES))
            onward = pm[part, columns] + phi_w_ref[part, :] * from_west
            pm[part, columns] = onward + phi_e_ref[part, :] * from_east
            beyond = rate * jnp.broadcast_to(onward[:, LANES - 1 :], (8, LANES)) + gain * from_east
            if g == 0:
                beyond = jnp.where(
                    sub8 == 0, own_next[y] + from_west + float(LANES) * from_east, beyond
                )
            next_columns.append(beyond)
        extra[part, :] = jnp.where(lane8 == 0, next_columns[0], next_columns[1])

    beyond = jnp.dot(
        jnp.transpose(extra[...])[0:8], cosine_ref[...],
        precision=HIGHEST, preferred_element_type=jnp.float32,
    )
    solved = jnp.dot(cosine_t_ref[...], pm[...], precision=HIGHEST, preferred_element_type=jnp.float32)
    tall = levels_here + 4
    for to in range(heights):
        z0 = to * levels_here
        half = z0 // LANES
        for y in range(2):
            base = (2 * to + y) * tall
            columns = slice(y * LANES, (y + 1) * LANES)
            top = min(z0 + levels_here, nz - 1)
            p_out[base : base + levels_here] = solved[z0 : z0 + levels_here, columns]
            p_out[base + levels_here : base + levels_here + 1] = solved[top : top + 1, columns]
            p_out[base + levels_here + 1 : base + levels_here + 2] = beyond[
                y : y + 1, half * LANES : (half + 1) * LANES
            ]

    def send_back(i, c):
        to = lax.rem(h + i, heights)
        pltpu.make_async_remote_copy(
            src_ref=p_out.at[pl.ds(to * 2 * tall, 2 * tall)],
            dst_ref=p_in.at[pl.ds(h * 2 * tall, 2 * tall)],
            send_sem=back_sem.at[0], recv_sem=back_sem.at[1],
            device_id=(r, to), device_id_type=MESH,
        ).start()
        return c

    lax.fori_loop(1, heights, send_back, 0)
    mine = pl.ds(h * 2 * tall, 2 * tall)
    own_block = pltpu.make_async_copy(p_out.at[mine], p_in.at[mine], out_sem.at[3])
    own_block.start()
    finish(d_out, (heights - 1) * block, a2a_sem.at[0])
    finish(mom, rows - 1, mom_sem.at[0])
    warm_out.wait()
    for copy in star_out:
        copy.wait()
    own_block.wait()
    finish(p_in, (heights - 1) * 2 * tall, back_sem.at[1])
    finish(p_out, (heights - 1) * 2 * tall, back_sem.at[0])


def project_kernel(
    heights, us_hbm, ws_hbm, p_hbm, warm_hbm, un_hbm, wn_hbm, tn_hbm,
    us, ws, p_in, warm, un, wn, in_sem, out_sem,
):
    loads = [
        pltpu.make_async_copy(src, dst, in_sem.at[i])
        for i, (src, dst) in enumerate(((warm_hbm, warm), (p_hbm, p_in), (us_hbm, us), (ws_hbm, ws)))
    ]
    for load in loads:
        load.start()
    h = lax.axis_index("height")
    levels_here, planes = us.shape[0], us.shape[1]
    tall = levels_here + 4
    lane = lax.broadcasted_iota(jnp.int32, (planes, LANES), 1)
    loads[0].wait()
    warm_out = pltpu.make_async_copy(warm, tn_hbm, out_sem.at[2])
    warm_out.start()
    for load in loads[1:]:
        load.wait()
    beyond = p_in[pl.ds(levels_here + 1, planes, stride=tall), :]
    first = lax.rem(h * levels_here, LANES)

    def project(z, p):
        edge = pltpu.roll(beyond, LANES - 1 - first - z, 1)
        east = jnp.where(lane == LANES - 1, edge, pltpu.roll(p, LANES - 1, 1))
        un[z] = us[z] - (east - p)
        above = p_in[pl.ds(z + 1, planes, stride=tall), :]
        wn[z] = ws[z] - (above - p)
        return above

    lax.fori_loop(0, levels_here, project, p_in[pl.ds(0, planes, stride=tall), :], unroll=UNROLL)
    stores = [
        pltpu.make_async_copy(un, un_hbm, out_sem.at[0]),
        pltpu.make_async_copy(wn, wn_hbm, out_sem.at[1]),
    ]
    for store in stores:
        store.start()
    warm_out.wait()
    for store in stores:
        store.wait()


def solution(mesh):
    rows, heights = mesh.shape["row"], mesh.shape["height"]

    def per_device(u, w, t, classes, paved, sun, lookup):
        levels_here, planes, width = u.shape
        nz = levels_here * heights
        table = tables(nz, width * rows, rows)
        smem = pl.BlockSpec(memory_space=pltpu.SMEM)
        hbm = pl.BlockSpec(memory_space=pl.ANY)
        field = jax.ShapeDtypeStruct(u.shape, jnp.float32)
        plane = (planes, LANES)
        f32 = jnp.float32
        dma = pltpu.SemaphoreType.DMA
        call = pl.pallas_call(
            functools.partial(kernel, rows, heights),
            out_shape=(field, field, jax.ShapeDtypeStruct((2 * heights * (levels_here + 4), LANES), f32), field),
            in_specs=[hbm] * 6 + [smem] * 2 + [hbm] * 11,
            out_specs=(hbm,) * 4,
            scratch_shapes=[
                pltpu.VMEM((levels_here,) + plane, jnp.int32),
                pltpu.VMEM(plane, jnp.int32),
                pltpu.VMEM(plane, f32),
                pltpu.VMEM((nz, nz), f32),
                pltpu.VMEM((nz, nz), f32),
                pltpu.VMEM((7, nz, LANES), f32),
                pltpu.VMEM((7, nz, LANES), f32),
                pltpu.VMEM((nz, LANES), f32),
                pltpu.VMEM((nz, LANES), f32),
                pltpu.VMEM((nz, LANES), f32),
                pltpu.VMEM((LANES, LANES), f32),
                pltpu.VMEM((LANES, LANES), f32),
                pltpu.VMEM((rows, 8, LANES), f32),
                pltpu.VMEM((rows, 8, LANES), f32),
                pltpu.VMEM(u.shape, f32),
                pltpu.VMEM((3, levels_here + 2) + plane, f32),
                pltpu.VMEM((levels_here,) + plane, f32),
                pltpu.VMEM(plane, f32),
                pltpu.VMEM((2,) + plane, f32),
                pltpu.VMEM((2,) + plane, f32),
                pltpu.VMEM((2,) + plane, f32),
                pltpu.VMEM(plane, f32),
                pltpu.VMEM((5,) + plane, f32),
                pltpu.VMEM(plane, f32),
                pltpu.VMEM(plane, f32),
                pltpu.VMEM(u.shape, f32),
                pltpu.VMEM(u.shape, f32),
                pltpu.VMEM((2 * nz, LANES), f32),
                pltpu.VMEM((2 * nz, LANES), f32),
                pltpu.VMEM((nz, 2 * LANES), f32),
                pltpu.VMEM((nz, LANES), f32),
                pltpu.VMEM((rows, 8, LANES), f32),
                pltpu.VMEM((2 * heights * (levels_here + 4), LANES), f32),
                dma((3,)), dma((14,)), dma((4,)), dma((2, 3)), dma((2, 5)), dma((2, 2)),
                dma((2,)), dma((2,)), dma((2,)),
            ],
            compiler_params=pltpu.CompilerParams(
                collective_id=0, has_side_effects=True, vmem_limit_bytes=60 * 1024 * 1024
            ),
        )
        us, ws, p, warm = call(
            u, w, t, classes, paved, sun, lookup, table["haze"], table["cosine"],
            table["cosine_t"], table["scan_e"], table["scan_w"], table["gain"],
            table["phi_west"], table["phi_east"], table["near"], table["near_next"],
            table["direct"], table["cross"],
        )
        project = pl.pallas_call(
            functools.partial(project_kernel, heights),
            out_shape=(field, field, field),
            in_specs=[hbm] * 4,
            out_specs=(hbm,) * 3,
            scratch_shapes=[
                pltpu.VMEM(u.shape, f32), pltpu.VMEM(u.shape, f32), pltpu.VMEM(p.shape, f32),
                pltpu.VMEM(u.shape, f32), pltpu.VMEM(u.shape, f32), pltpu.VMEM(u.shape, f32),
                dma((4,)), dma((3,)),
            ],
            compiler_params=pltpu.CompilerParams(vmem_limit_bytes=60 * 1024 * 1024),
        )
        return project(us, ws, p, warm)

    field = P("height", None, "row")
    line = P(None, "row")
    return jax.shard_map(
        per_device, mesh=mesh, in_specs=(field, field, field, field, line, line, P()),
        out_specs=(field, field, field), check_vma=False,
    )
```

```python
import functools
import math

import jax
import jax.numpy as jnp
import numpy as np
from jax import lax
from jax.experimental import pallas as pl
from jax.experimental.pallas import tpu as pltpu
from jax.sharding import PartitionSpec as P

CANOPY = 48
DT = 0.25
VISCOSITY = 0.05
DRAG_COEF = 0.2
THERMAL_LIFT = 0.2
SPAN_VAR = 0.25
HAZE_EXTINCT = 0.02
PAVED_ABSORB = 0.9
GRASS_ABSORB = 0.5
MESH = pl.DeviceIdType.MESH
UNROLL = True
TALL = 18
SLOT = 24
HIGHEST = lax.Precision.HIGHEST
LANES = 128


def tables(levels, columns, row_count):
    m = np.arange(levels, dtype=np.float64)
    z = np.arange(levels, dtype=np.float64)
    cosine = np.cos(np.pi * m[:, None] * (z[None, :] + 0.5) / levels)
    cosine *= np.where(m == 0, math.sqrt(1.0 / levels), math.sqrt(2.0 / levels))[:, None]
    mu = 2.0 * np.arcsinh(np.sin(np.pi * m / (2.0 * levels)))
    safe = np.where(m == 0, 1.0, mu)
    gain = np.where(m == 0, 0.0, -1.0 / (2.0 * np.sinh(safe)))
    x = np.arange(LANES, dtype=np.float64)
    scan_e = np.zeros((7, levels, LANES))
    scan_w = np.zeros((7, levels, LANES))
    for k in range(7):
        rate = np.exp(-mu * 2.0**k)[:, None]
        scan_e[k] = np.where(x[None, :] >= 2**k, rate, 0.0)
        scan_w[k] = np.where(x[None, :] < LANES - 2**k, rate, 0.0)
    gain_full = np.broadcast_to(gain[:, None], (levels, LANES))
    phi_west = np.where(m[:, None] == 0, 1.0, gain[:, None] * np.exp(-mu[:, None] * (x + 1.0)))
    phi_east = np.where(m[:, None] == 0, x, gain[:, None] * np.exp(-mu[:, None] * (LANES - x)))
    near = 0.5 * np.abs(x[:, None] - x[None, :]) + x[:, None] * x[None, :] / columns
    near_next = np.broadcast_to((0.5 * (LANES - x) + LANES * x / columns)[:, None], (LANES, LANES))
    lane = np.arange(LANES)
    odd = lane % 2 == 1
    group = np.where(odd, (lane + 1) // 2, lane // 2) % 64
    per_plane = levels // 8
    used = group < 2 * per_plane
    mode = 8 * (group % per_plane)[None, :] + np.arange(8)[:, None]
    mode_mu = mu[mode]
    safe_mu = np.where(mode == 0, 1.0, mode_mu)
    direct = np.zeros((row_count, 8, LANES))
    cross = np.zeros((row_count, 8, LANES))
    for shift in range(row_count):
        to_east = shift if shift else row_count
        to_west = row_count - shift
        steps = np.where(odd, to_west, to_east)[None, :]
        usual = np.exp(-safe_mu * LANES * (steps - 1)) / (1.0 - np.exp(-safe_mu * columns))
        away = float(LANES * shift)
        if shift:
            zero_direct = np.where(odd, away / 2 - away**2 / (2 * columns), 1.0 / columns)
            zero_cross = np.where(odd, -0.5 + away / columns, 0.5 - away / columns)
        else:
            zero_direct = np.zeros(LANES)
            zero_cross = np.zeros(LANES)
        direct[shift] = np.where(mode == 0, zero_direct[None, :], usual) * used
        cross[shift] = np.where(mode == 0, zero_cross[None, :], 0.0) * used
    haze = HAZE_EXTINCT * np.exp(-4.0 * (z + 0.5) / levels)
    haze_above = np.concatenate([np.cumsum(haze[::-1])[::-1], [0.0]])
    f32 = lambda a: np.ascontiguousarray(a, dtype=np.float32)
    return dict(
        cosine=f32(cosine), cosine_t=f32(cosine.T), scan_e=f32(scan_e), scan_w=f32(scan_w), gain=f32(gain_full), phi_west=f32(phi_west),
        phi_east=f32(phi_east), near=f32(near), near_next=f32(near_next), direct=f32(direct), cross=f32(cross),
        haze=f32(haze_above),
    )


def kernel(
    rows, heights,
    u_hbm, w_hbm, t_hbm, class_hbm, paved_hbm, sun_hbm, lookup_ref, haze_ref,
    cosine_hbm, cosine_t_hbm, scan_e_hbm, scan_w_hbm, gain_hbm, phi_w_hbm, phi_e_hbm, near_hbm,
    near_next_hbm, direct_hbm, cross_hbm,
    us_hbm, ws_hbm, p_in, tn_hbm,
    class_ref, paved_ref, sun_ref,
    cosine_ref, cosine_t_ref, scan_e_ref, scan_w_ref, gain_ref, phi_w_ref, phi_e_ref, near_ref,
    near_next_ref, direct_ref, cross_ref,
    tn_ref,
    ext, leaf, leaf_sum, leaf_in, low_out, low_in, side_out, side_in, side, u_side, us, ws,
    d_out, d_in, pm, extra, mom, p_out,
    in_sem, other_sem, out_sem,
    z_sem, side_sem, leaf_sem, a2a_sem, mom_sem, back_sem,
):
    r = lax.axis_index("row")
    h = lax.axis_index("height")
    levels_here = class_ref.shape[0]
    planes = class_ref.shape[1]
    nz = levels_here * heights
    block = 2 * levels_here
    groups = nz // 8

    def at(dr, dh):
        return (lax.rem(r + dr + rows, rows), lax.rem(h + dh + heights, heights))

    first_class = pltpu.make_async_copy(class_hbm, class_ref, other_sem.at[0])
    loads = [
        pltpu.make_async_copy(ref, ext.at[f, pl.ds(1, levels_here)], in_sem.at[f])
        for f, ref in enumerate((u_hbm, w_hbm, t_hbm))
    ]
    for load in loads:
        load.start()
    first_class.start()
    others = [
        pltpu.make_async_copy(src, dst, other_sem.at[i + 1])
        for i, (src, dst) in enumerate((
            (paved_hbm, paved_ref), (sun_hbm, sun_ref),
            (cosine_hbm, cosine_ref), (scan_e_hbm, scan_e_ref), (scan_w_hbm, scan_w_ref),
            (gain_hbm, gain_ref), (near_hbm, near_ref), (phi_w_hbm, phi_w_ref),
            (phi_e_hbm, phi_e_ref), (near_next_hbm, near_next_ref), (direct_hbm, direct_ref), (cross_hbm, cross_ref),
            (cosine_t_hbm, cosine_t_ref),
        ))
    ]

    barrier = pltpu.get_barrier_semaphore()

    def greet_height(i, c):
        pl.semaphore_signal(barrier, inc=1, device_id=at(0, i), device_id_type=MESH)
        return c

    def greet_row(i, c):
        pl.semaphore_signal(barrier, inc=1, device_id=at(i, 0), device_id_type=MESH)
        return c

    lax.fori_loop(1, heights, greet_height, 0)
    lax.fori_loop(1, rows, greet_row, 0)
    corners = (at(1, 1), at(1, -1), at(-1, 1))
    for corner in (*corners, at(-1, -1)):
        pl.semaphore_signal(barrier, inc=1, device_id=corner, device_id_type=MESH)
    for copy in others:
        copy.start()
    for load in loads:
        load.wait()
    lane = lax.broadcasted_iota(jnp.int32, (planes, LANES), 1)

    def leaf_of(classes):
        area = jnp.zeros((planes, LANES), jnp.float32)
        for c in range(lookup_ref.shape[0]):
            area = jnp.where(classes == c, lookup_ref[c], area)
        return area

    def pack_sides(z, acc):
        for f in range(3):
            j = 2 * (f * levels_here + z)
            turned = pltpu.roll(ext[f, z + 1], j + 1, 1)
            acc = jnp.where((lane == j) | (lane == j + 1), turned, acc)
        j = 6 * levels_here + 2 * z
        turned = pltpu.roll(ext[0, z + 1], lax.rem(j + 2, LANES), 1)
        acc = jnp.where(lane == j, turned, acc)
        turned = pltpu.roll(class_ref[z].astype(jnp.float32), lax.rem(j + 2, LANES), 1)
        return jnp.where(lane == j + 1, turned, acc)

    first_class.wait()
    side_out[...] = lax.fori_loop(0, levels_here, pack_sides, jnp.zeros((planes, LANES), jnp.float32), unroll=True)
    low_out[0] = ext[1, levels_here - 1]
    low_out[1] = leaf_of(class_ref[levels_here - 1])
    pl.semaphore_wait(barrier, heights + rows + 2)

    def remote(src, dst, sems, slot, device):
        return pltpu.make_async_remote_copy(
            src_ref=src, dst_ref=dst, send_sem=sems.at[0, slot], recv_sem=sems.at[1, slot],
            device_id=device, device_id_type=MESH,
        )

    halo = [
        remote(side_out, side_in.at[0], side_sem, 0, at(1, 0)),
        remote(side_out, side_in.at[1], side_sem, 1, at(-1, 0)),
        remote(ext.at[:, levels_here], ext.at[:, 0], z_sem, 0, at(0, 1)),
        remote(ext.at[:, 1], ext.at[:, levels_here + 1], z_sem, 1, at(0, -1)),
        remote(low_out, low_in, z_sem, 2, at(0, 1)),
    ] + [
        remote(side_out, side_in.at[2 + i], side_sem, 2 + i, corner) for i, corner in enumerate(corners)
    ]
    for copy in halo:
        copy.start()

    def leaf_level(z, total):
        area = leaf_of(class_ref[z])
        area = jnp.where(h * levels_here + z < CANOPY, area, 0.0)
        leaf[z] = area
        return total + area

    leaf_sum[...] = lax.fori_loop(0, levels_here, leaf_level, jnp.zeros((planes, LANES), jnp.float32), unroll=UNROLL)
    leaf_copies = [
        remote(leaf_sum, leaf_in.at[0], leaf_sem, 0, at(0, -1)),
        remote(leaf_sum, leaf_in.at[1], leaf_sem, 1, at(0, -2)),
    ]
    for copy in leaf_copies:
        copy.start()

    for copy in halo:
        copy.wait()

    @pl.when(h == 0)
    def _():
        ext[:, 0] = jnp.zeros((3, planes, LANES), jnp.float32)

    @pl.when(h == heights - 1)
    def _():
        ext[:, levels_here + 1] = jnp.zeros((3, planes, LANES), jnp.float32)

    even = lax.rem(lane, 2) == 0
    from_left = side_in[0]
    side[...] = jnp.where(even, pltpu.roll(side_in[1], LANES - 1, 1), pltpu.roll(from_left, 1, 1))

    def stretch(q, u, w, east, west, above, below):
        advect = u * (east - west) * 0.5 + w * (above - below) * 0.5
        diffuse = VISCOSITY * (east + west + above + below - 4.0 * q)
        return diffuse - advect

    def drag(area, u, w):
        return DRAG_COEF * area * jnp.sqrt(u * u + w * w + SPAN_VAR)

    last = 2 * (levels_here - 1)
    w_left = pltpu.roll(from_left, LANES - 2 * levels_here, 1)
    u_far = pltpu.roll(from_left, LANES - 6 * levels_here, 1)
    class_left = pltpu.roll(from_left, LANES - 6 * levels_here - 1, 1)
    z_of_lane = h * levels_here + lane // 2
    area_left = jnp.where(z_of_lane < CANOPY, leaf_of(class_left), 0.0)
    u_east = pltpu.roll(side_out[...], LANES - 1, 1)
    corner_above = jnp.where(h < heights - 1, pltpu.roll(side_in[3], last, 1), 0.0)
    corner_below = jnp.where(h > 0, pltpu.roll(side_in[2], LANES - last, 1), 0.0)
    u_above = jnp.where(lane == last, corner_above, pltpu.roll(from_left, LANES - 2, 1))
    u_below = jnp.where(lane == 0, corner_below, pltpu.roll(from_left, 2, 1))
    u_side[...] = from_left + DT * (
        stretch(from_left, from_left, w_left, u_east, u_far, u_above, u_below)
        - drag(area_left, from_left, w_left) * from_left
    )

    u_low, w_low, t_low = ext[0, 0], ext[1, 0], ext[2, 0]
    j = 2 * (2 * levels_here - 1)
    w_east = jnp.where(
        lane == LANES - 1, pltpu.roll(side_in[4], LANES - 2 - j, 1), pltpu.roll(w_low, LANES - 1, 1)
    )
    w_west = jnp.where(lane == 0, pltpu.roll(side_in[2], LANES - j, 1), pltpu.roll(w_low, 1, 1))
    area_low = jnp.where(h * levels_here - 1 < CANOPY, low_in[1], 0.0)
    w_star_low = w_low + DT * (
        stretch(w_low, u_low, w_low, w_east, w_west, ext[1, 1], low_in[0])
        - drag(area_low, u_low, w_low) * w_low
        + THERMAL_LIFT * t_low
    )
    w_star_low = jnp.where(h > 0, w_star_low, 0.0)

    def growth(f, z, u, w):
        q = ext[f, z + 1]
        j = 2 * (f * levels_here + z)
        edge = pltpu.roll(side[...], LANES - 1 - j, 1)
        east = jnp.where(lane == LANES - 1, edge, pltpu.roll(q, LANES - 1, 1))
        west = jnp.where(lane == 0, edge, pltpu.roll(q, 1, 1))
        return stretch(q, u, w, east, west, ext[f, z + 2], ext[f, z])

    def winds(z, w_below):
        u = ext[0, z + 1]
        w = ext[1, z + 1]
        t = ext[2, z + 1]
        friction = drag(leaf[z], u, w)
        u_star = u + DT * (growth(0, z, u, w) - friction * u)
        w_star = w + DT * (growth(1, z, u, w) - friction * w + THERMAL_LIFT * t)
        w_star = jnp.where(h * levels_here + z == nz - 1, 0.0, w_star)
        us[z] = u_star
        ws[z] = w_star
        edge = pltpu.roll(u_side[...], lax.rem(LANES - 2 * z, LANES), 1)
        west = jnp.where(lane == 0, edge, pltpu.roll(u_star, 1, 1))
        d_out[pl.ds(z, planes, stride=levels_here), :] = u_star - west + (w_star - w_below)
        return w_star

    lax.fori_loop(0, levels_here, winds, w_star_low, unroll=UNROLL)

    def finish(buffer, count, sem):
        part = buffer.at[pl.ds(0, count)]
        pltpu.make_async_copy(part, part, sem).wait()

    for y in range(2):

        def send_plane(i, c, y=y):
            to = lax.rem(h + i, heights)
            pltpu.make_async_remote_copy(
                src_ref=d_out.at[pl.ds((2 * to + y) * levels_here, levels_here)],
                dst_ref=d_in.at[y, pl.ds(h * levels_here, levels_here)],
                send_sem=a2a_sem.at[0], recv_sem=a2a_sem.at[1 + y],
                device_id=(r, to), device_id_type=MESH,
            ).start()
            return c

        lax.fori_loop(1, heights, send_plane, 0)
    for y in range(2):
        d_in[y, pl.ds(h * levels_here, levels_here)] = d_out[
            pl.ds((2 * h + y) * levels_here, levels_here)
        ]
    star_out = [
        pltpu.make_async_copy(us, us_hbm, out_sem.at[0]),
        pltpu.make_async_copy(ws, ws_hbm, out_sem.at[1]),
    ]
    for copy in star_out:
        copy.start()
    for copy in others[:2]:
        copy.wait()

    for copy in leaf_copies:
        copy.wait()
    above1 = jnp.where(h < heights - 1, leaf_in[0], 0.0)
    above2 = jnp.where(h < heights - 2, leaf_in[1], 0.0)
    over = above1 + above2
    sun = sun_ref[...]
    first = jnp.exp(-(0.5 * over + haze_ref[h * levels_here + levels_here]))

    def heat(k, state):
        over, top = state
        z = levels_here - 1 - k
        over = over + leaf[z]
        bottom = jnp.exp(-(0.5 * over + haze_ref[h * levels_here + z]))
        warming = sun * (top - bottom)
        absorb = jnp.where(paved_ref[...] == 1, PAVED_ABSORB, GRASS_ABSORB)
        warming = warming + jnp.where(h * levels_here + z == 0, sun * bottom * absorb, 0.0)
        t = ext[2, z + 1]
        tn_ref[z] = t + DT * (growth(2, z, ext[0, z + 1], ext[1, z + 1]) + warming)
        return over, bottom

    lax.fori_loop(0, levels_here, heat, (over, first), unroll=UNROLL)
    warm_out = pltpu.make_async_copy(tn_ref, tn_hbm, out_sem.at[2])
    warm_out.start()
    for copy in others[2:]:
        copy.wait()

    lane8 = lax.broadcasted_iota(jnp.int32, (8, LANES), 1)
    sub8 = lax.broadcasted_iota(jnp.int32, (8, LANES), 0)
    chunk = min(64, nz)
    lane_c = lax.broadcasted_iota(jnp.int32, (chunk, LANES), 1)
    slot = (sub8 == 0) & (lane8 == 0)

    def row_scans(y):
        finish(d_in.at[y], (heights - 1) * levels_here, a2a_sem.at[1 + y])
        modes = jnp.dot(
            cosine_ref[...], d_in[y], precision=HIGHEST, preferred_element_type=jnp.float32
        )
        packed = jnp.zeros((8, LANES), jnp.float32)
        for start in range(0, nz, chunk):
            part = slice(start, start + chunk)
            d = modes[part]
            fwd = d
            bwd = d
            for k in range(7):
                s = 1 << k
                fwd = fwd + scan_e_ref[k, part, :] * pltpu.roll(fwd, s, 1)
                bwd = bwd + scan_w_ref[k, part, :] * pltpu.roll(bwd, LANES - s, 1)
            local = gain_ref[part, :] * (fwd + bwd - d)
            ends = jnp.where(lane_c == 0, bwd, fwd)
            if start == 0:
                zero = d[0:8]
                own = jnp.dot(
                    zero, near_ref[...], precision=HIGHEST, preferred_element_type=jnp.float32
                )
                own_next = jnp.dot(
                    zero, near_next_ref[...], precision=HIGHEST, preferred_element_type=jnp.float32
                )
                first_moment = jnp.sum(zero * lane8.astype(jnp.float32), axis=1, keepdims=True)
                pm[y, 0:8] = jnp.where(sub8 == 0, own, local[0:8])
                pm[y, 8:chunk] = local[8:]
            else:
                pm[y, part] = local
            for i in range(chunk // 8):
                value = ends[8 * i : 8 * i + 8]
                if start == 0 and i == 0:
                    value = jnp.where(slot, jnp.broadcast_to(first_moment, (8, LANES)), value)
                j = 2 * (start // 8 + i)
                turned = pltpu.roll(value, j, 1) if j else value
                mine = (lane8 == j) | (lane8 == (j + LANES - 1) % LANES)
                packed = jnp.where(mine, turned, packed)
        mom[y, r] = packed

        def send_moments(i, c):
            pltpu.make_async_remote_copy(
                src_ref=mom.at[y, r], dst_ref=mom.at[y, r],
                send_sem=mom_sem.at[0], recv_sem=mom_sem.at[1 + y],
                device_id=at(i, 0), device_id_type=MESH,
            ).start()
            return c

        lax.fori_loop(1, rows, send_moments, 0)
        return own_next

    def row_solve(y, own_next):
        finish(mom.at[y], rows - 1, mom_sem.at[1 + y])

        def gather_moments(i, state):
            direct, cross = state
            values = mom[y, lax.rem(r + i, rows)]
            return direct + direct_ref[i] * values, cross + cross_ref[i] * values

        nothing = jnp.zeros((8, LANES), jnp.float32)
        direct, cross = lax.fori_loop(0, rows, gather_moments, (nothing, nothing), unroll=UNROLL)
        inflow = direct + jnp.where(
            lax.rem(lane8, 2) == 0, pltpu.roll(cross, 1, 1), pltpu.roll(cross, LANES - 1, 1)
        )
        for g in range(groups):
            part = slice(8 * g, 8 * g + 8)
            j = 2 * g
            west = (j + LANES - 1) % LANES
            from_east = jnp.broadcast_to(inflow[:, j : j + 1], (8, LANES))
            from_west = jnp.broadcast_to(inflow[:, west : west + 1], (8, LANES))
            onward = pm[y, part] + phi_w_ref[part, :] * from_west
            pm[y, part] = onward + phi_e_ref[part, :] * from_east
            beyond = (
                scan_w_ref[0, part, :] * jnp.broadcast_to(onward[:, LANES - 1 :], (8, LANES))
                + gain_ref[part, :] * from_east
            )
            if g == 0:
                beyond = jnp.where(
                    sub8 == 0, own_next + from_west + float(LANES) * from_east, beyond
                )
            extra[part, :] = beyond
        solved = jnp.dot(
            cosine_t_ref[...], pm[y], precision=HIGHEST, preferred_element_type=jnp.float32
        )
        beyond = jnp.dot(
            jnp.transpose(extra[...])[0:8], cosine_ref[...],
            precision=HIGHEST, preferred_element_type=jnp.float32,
        )
        for to in range(heights):
            z0 = to * levels_here
            half = z0 // LANES
            top = min(z0 + levels_here, nz - 1)
            p_out[y, to, 0:levels_here] = solved[z0 : z0 + levels_here]
            p_out[y, to, levels_here : levels_here + 1] = solved[top : top + 1]
            p_out[y, to, levels_here + 1 : levels_here + 2] = beyond[
                0:1, half * LANES : (half + 1) * LANES
            ]

        def send_back(i, c):
            to = lax.rem(h + i, heights)
            pltpu.make_async_remote_copy(
                src_ref=p_out.at[y, to, pl.ds(0, TALL)],
                dst_ref=p_in.at[2 * h + y, pl.ds(0, TALL)],
                send_sem=back_sem.at[0], recv_sem=back_sem.at[1],
                device_id=(r, to), device_id_type=MESH,
            ).start()
            return c

        lax.fori_loop(1, heights, send_back, 0)
        own_block = pltpu.make_async_copy(
            p_out.at[y, h, pl.ds(0, TALL)], p_in.at[2 * h + y, pl.ds(0, TALL)], out_sem.at[3 + y]
        )
        own_block.start()
        return own_block

    own_next = [row_scans(0), row_scans(1)]
    own_blocks = [row_solve(0, own_next[0]), row_solve(1, own_next[1])]
    finish(d_out, (heights - 1) * block, a2a_sem.at[0])
    part = mom.at[:, pl.ds(0, rows - 1)]
    pltpu.make_async_copy(part, part, mom_sem.at[0]).wait()
    warm_out.wait()
    for copy in star_out + own_blocks:
        copy.wait()
    for sem in (back_sem.at[1], back_sem.at[0]):
        part = p_in.at[pl.ds(0, 2 * (heights - 1)), pl.ds(0, TALL)]
        pltpu.make_async_copy(part, part, sem).wait()


def project_kernel(
    heights, us_hbm, ws_hbm, p_hbm, warm_hbm, un_hbm, wn_hbm, tn_hbm,
    us, ws, p_in, warm, un, wn, in_sem, out_sem,
):
    loads = [
        pltpu.make_async_copy(src, dst, in_sem.at[i])
        for i, (src, dst) in enumerate(((warm_hbm, warm), (p_hbm, p_in), (us_hbm, us), (ws_hbm, ws)))
    ]
    for load in loads:
        load.start()
    h = lax.axis_index("height")
    levels_here, planes = us.shape[0], us.shape[1]
    tall = SLOT
    lane = lax.broadcasted_iota(jnp.int32, (planes, LANES), 1)
    loads[0].wait()
    warm_out = pltpu.make_async_copy(warm, tn_hbm, out_sem.at[2])
    warm_out.start()
    for load in loads[1:]:
        load.wait()
    beyond = p_in[pl.ds(levels_here + 1, planes, stride=tall), :]
    first = lax.rem(h * levels_here, LANES)

    def project(z, p):
        edge = pltpu.roll(beyond, LANES - 1 - first - z, 1)
        east = jnp.where(lane == LANES - 1, edge, pltpu.roll(p, LANES - 1, 1))
        un[z] = us[z] - (east - p)
        above = p_in[pl.ds(z + 1, planes, stride=tall), :]
        wn[z] = ws[z] - (above - p)
        return above

    lax.fori_loop(0, levels_here, project, p_in[pl.ds(0, planes, stride=tall), :], unroll=UNROLL)
    stores = [
        pltpu.make_async_copy(un, un_hbm, out_sem.at[0]),
        pltpu.make_async_copy(wn, wn_hbm, out_sem.at[1]),
    ]
    for store in stores:
        store.start()
    warm_out.wait()
    for store in stores:
        store.wait()


def solution(mesh):
    rows, heights = mesh.shape["row"], mesh.shape["height"]

    def per_device(u, w, t, classes, paved, sun, lookup):
        levels_here, planes, width = u.shape
        nz = levels_here * heights
        table = tables(nz, width * rows, rows)
        smem = pl.BlockSpec(memory_space=pltpu.SMEM)
        hbm = pl.BlockSpec(memory_space=pl.ANY)
        field = jax.ShapeDtypeStruct(u.shape, jnp.float32)
        plane = (planes, LANES)
        f32 = jnp.float32
        dma = pltpu.SemaphoreType.DMA
        call = pl.pallas_call(
            functools.partial(kernel, rows, heights),
            out_shape=(field, field, jax.ShapeDtypeStruct((planes, SLOT, LANES), f32), field),
            in_specs=[hbm] * 6 + [smem] * 2 + [hbm] * 11,
            out_specs=(hbm,) * 4,
            scratch_shapes=[
                pltpu.VMEM((levels_here,) + plane, jnp.int32),
                pltpu.VMEM(plane, jnp.int32),
                pltpu.VMEM(plane, f32),
                pltpu.VMEM((nz, nz), f32),
                pltpu.VMEM((nz, nz), f32),
                pltpu.VMEM((7, nz, LANES), f32),
                pltpu.VMEM((7, nz, LANES), f32),
                pltpu.VMEM((nz, LANES), f32),
                pltpu.VMEM((nz, LANES), f32),
                pltpu.VMEM((nz, LANES), f32),
                pltpu.VMEM((LANES, LANES), f32),
                pltpu.VMEM((LANES, LANES), f32),
                pltpu.VMEM((rows, 8, LANES), f32),
                pltpu.VMEM((rows, 8, LANES), f32),
                pltpu.VMEM(u.shape, f32),
                pltpu.VMEM((3, levels_here + 2) + plane, f32),
                pltpu.VMEM((levels_here,) + plane, f32),
                pltpu.VMEM(plane, f32),
                pltpu.VMEM((2,) + plane, f32),
                pltpu.VMEM((2,) + plane, f32),
                pltpu.VMEM((2,) + plane, f32),
                pltpu.VMEM(plane, f32),
                pltpu.VMEM((5,) + plane, f32),
                pltpu.VMEM(plane, f32),
                pltpu.VMEM(plane, f32),
                pltpu.VMEM(u.shape, f32),
                pltpu.VMEM(u.shape, f32),
                pltpu.VMEM((2 * nz, LANES), f32),
                pltpu.VMEM((2, nz, LANES), f32),
                pltpu.VMEM((2, nz, LANES), f32),
                pltpu.VMEM((nz, LANES), f32),
                pltpu.VMEM((2, rows, 8, LANES), f32),
                pltpu.VMEM((2, heights, SLOT, LANES), f32),
                dma((3,)), dma((14,)), dma((5,)), dma((2, 3)), dma((2, 5)), dma((2, 2)),
                dma((3,)), dma((3,)), dma((2,)),
            ],
            compiler_params=pltpu.CompilerParams(
                collective_id=0, has_side_effects=True, vmem_limit_bytes=60 * 1024 * 1024
            ),
        )
        us, ws, p, warm = call(
            u, w, t, classes, paved, sun, lookup, table["haze"], table["cosine"],
            table["cosine_t"], table["scan_e"], table["scan_w"], table["gain"],
            table["phi_west"], table["phi_east"], table["near"], table["near_next"],
            table["direct"], table["cross"],
        )
        project = pl.pallas_call(
            functools.partial(project_kernel, heights),
            out_shape=(field, field, field),
            in_specs=[hbm] * 4,
            out_specs=(hbm,) * 3,
            scratch_shapes=[
                pltpu.VMEM(u.shape, f32), pltpu.VMEM(u.shape, f32), pltpu.VMEM((planes * SLOT, LANES), f32),
                pltpu.VMEM(u.shape, f32), pltpu.VMEM(u.shape, f32), pltpu.VMEM(u.shape, f32),
                dma((4,)), dma((3,)),
            ],
            compiler_params=pltpu.CompilerParams(vmem_limit_bytes=60 * 1024 * 1024),
        )
        return project(us, ws, p.reshape(planes * SLOT, LANES), warm)

    field = P("height", None, "row")
    line = P(None, "row")
    return jax.shard_map(
        per_device, mesh=mesh, in_specs=(field, field, field, field, line, line, P()),
        out_specs=(field, field, field), check_vma=False,
    )
```

```python
import functools
import math

import jax
import jax.numpy as jnp
import numpy as np
from jax import lax
from jax.experimental import pallas as pl
from jax.experimental.pallas import tpu as pltpu
from jax.sharding import PartitionSpec as P

CANOPY = 48
DT = 0.25
VISCOSITY = 0.05
DRAG_COEF = 0.2
THERMAL_LIFT = 0.2
SPAN_VAR = 0.25
HAZE_EXTINCT = 0.02
PAVED_ABSORB = 0.9
GRASS_ABSORB = 0.5
MESH = pl.DeviceIdType.MESH
UNROLL = True
TALL = 18
SLOT = 24
HIGHEST = lax.Precision.HIGHEST
LANES = 128


def tables(levels, columns, row_count):
    m = np.arange(levels, dtype=np.float64)
    z = np.arange(levels, dtype=np.float64)
    cosine = np.cos(np.pi * m[:, None] * (z[None, :] + 0.5) / levels)
    cosine *= np.where(m == 0, math.sqrt(1.0 / levels), math.sqrt(2.0 / levels))[:, None]
    mu = 2.0 * np.arcsinh(np.sin(np.pi * m / (2.0 * levels)))
    safe = np.where(m == 0, 1.0, mu)
    gain = np.where(m == 0, 0.0, -1.0 / (2.0 * np.sinh(safe)))
    x = np.arange(LANES, dtype=np.float64)
    scan_e = np.zeros((7, levels, LANES))
    scan_w = np.zeros((7, levels, LANES))
    for k in range(7):
        rate = np.exp(-mu * 2.0**k)[:, None]
        scan_e[k] = np.where(x[None, :] >= 2**k, rate, 0.0)
        scan_w[k] = np.where(x[None, :] < LANES - 2**k, rate, 0.0)
    gain_full = np.broadcast_to(gain[:, None], (levels, LANES))
    phi_west = np.where(m[:, None] == 0, 1.0, gain[:, None] * np.exp(-mu[:, None] * (x + 1.0)))
    phi_east = np.where(m[:, None] == 0, x, gain[:, None] * np.exp(-mu[:, None] * (LANES - x)))
    near = 0.5 * np.abs(x[:, None] - x[None, :]) + x[:, None] * x[None, :] / columns
    near_next = np.broadcast_to((0.5 * (LANES - x) + LANES * x / columns)[:, None], (LANES, LANES))
    lane = np.arange(LANES)
    odd = lane % 2 == 1
    group = np.where(odd, (lane + 1) // 2, lane // 2) % 64
    per_plane = levels // 8
    used = group < 2 * per_plane
    mode = 8 * (group % per_plane)[None, :] + np.arange(8)[:, None]
    mode_mu = mu[mode]
    safe_mu = np.where(mode == 0, 1.0, mode_mu)
    direct = np.zeros((row_count, 8, LANES))
    cross = np.zeros((row_count, 8, LANES))
    for shift in range(row_count):
        to_east = shift if shift else row_count
        to_west = row_count - shift
        steps = np.where(odd, to_west, to_east)[None, :]
        usual = np.exp(-safe_mu * LANES * (steps - 1)) / (1.0 - np.exp(-safe_mu * columns))
        away = float(LANES * shift)
        if shift:
            zero_direct = np.where(odd, away / 2 - away**2 / (2 * columns), 1.0 / columns)
            zero_cross = np.where(odd, -0.5 + away / columns, 0.5 - away / columns)
        else:
            zero_direct = np.zeros(LANES)
            zero_cross = np.zeros(LANES)
        direct[shift] = np.where(mode == 0, zero_direct[None, :], usual) * used
        cross[shift] = np.where(mode == 0, zero_cross[None, :], 0.0) * used
    haze = HAZE_EXTINCT * np.exp(-4.0 * (z + 0.5) / levels)
    haze_above = np.concatenate([np.cumsum(haze[::-1])[::-1], [0.0]])
    f32 = lambda a: np.ascontiguousarray(a, dtype=np.float32)
    return dict(
        cosine=f32(cosine), cosine_t=f32(cosine.T), scan_e=f32(scan_e), scan_w=f32(scan_w), gain=f32(gain_full), phi_west=f32(phi_west),
        phi_east=f32(phi_east), near=f32(near), near_next=f32(near_next), direct=f32(direct), cross=f32(cross),
        haze=f32(haze_above),
    )


def kernel(
    rows, heights,
    u_hbm, w_hbm, t_hbm, class_hbm, paved_hbm, sun_hbm, lookup_ref, haze_ref,
    cosine_hbm, cosine_t_hbm, scan_e_hbm, scan_w_hbm, gain_hbm, phi_w_hbm, phi_e_hbm, near_hbm,
    near_next_hbm, direct_hbm, cross_hbm,
    us_hbm, ws_hbm, p_in, tn_hbm,
    class_ref, paved_ref, sun_ref,
    cosine_ref, cosine_t_ref, scan_e_ref, scan_w_ref, gain_ref, phi_w_ref, phi_e_ref, near_ref,
    near_next_ref, direct_ref, cross_ref,
    tn_ref,
    ext, leaf, leaf_sum, leaf_in, low_out, low_in, side_out, side_in, side, u_side, us, ws,
    d_out, d_in, pm, extra, mom, p_out,
    in_sem, other_sem, out_sem,
    z_sem, side_sem, leaf_sem, a2a_sem, mom_sem, back_sem,
):
    r = lax.axis_index("row")
    h = lax.axis_index("height")
    levels_here = class_ref.shape[0]
    planes = class_ref.shape[1]
    nz = levels_here * heights
    block = 2 * levels_here
    groups = nz // 8

    def at(dr, dh):
        return (lax.rem(r + dr + rows, rows), lax.rem(h + dh + heights, heights))

    depth = 8 if rows % 8 == 0 else rows
    wide = rows // depth
    x_of, z_of = lax.div(r, depth), lax.rem(r, depth)

    def outward(i, count):
        return count // 2 + ((i + 1) // 2) * (1 - 2 * (i % 2))

    def row_peer(i):
        x = lax.rem(x_of + outward(i // depth, wide), wide)
        return (x * depth + lax.rem(z_of + outward(i % depth, depth), depth), h)

    def height_peer(i):
        return lax.rem(h + outward(i, heights), heights)

    barrier = pltpu.get_barrier_semaphore()

    for i in range(rows - 1):
        pl.semaphore_signal(barrier, inc=1, device_id=row_peer(i), device_id_type=MESH)
    for i in range(heights - 1):
        pl.semaphore_signal(barrier, inc=1, device_id=(r, height_peer(i)), device_id_type=MESH)
    corners = (at(1, 1), at(1, -1), at(-1, 1))
    for corner in (*corners, at(-1, -1)):
        pl.semaphore_signal(barrier, inc=1, device_id=corner, device_id_type=MESH)
    first_class = pltpu.make_async_copy(class_hbm, class_ref, other_sem.at[0])
    loads = [
        pltpu.make_async_copy(ref, ext.at[f, pl.ds(1, levels_here)], in_sem.at[f])
        for f, ref in enumerate((u_hbm, w_hbm, t_hbm))
    ]
    for load in loads:
        load.start()
    first_class.start()
    others = [
        pltpu.make_async_copy(src, dst, other_sem.at[i + 1])
        for i, (src, dst) in enumerate((
            (paved_hbm, paved_ref), (sun_hbm, sun_ref),
            (cosine_hbm, cosine_ref), (scan_e_hbm, scan_e_ref), (scan_w_hbm, scan_w_ref),
            (gain_hbm, gain_ref), (near_hbm, near_ref), (phi_w_hbm, phi_w_ref),
            (phi_e_hbm, phi_e_ref), (near_next_hbm, near_next_ref), (direct_hbm, direct_ref), (cross_hbm, cross_ref),
            (cosine_t_hbm, cosine_t_ref),
        ))
    ]
    for copy in others:
        copy.start()
    for load in loads:
        load.wait()
    lane = lax.broadcasted_iota(jnp.int32, (planes, LANES), 1)

    def leaf_of(classes):
        area = jnp.zeros((planes, LANES), jnp.float32)
        for c in range(lookup_ref.shape[0]):
            area = jnp.where(classes == c, lookup_ref[c], area)
        return area

    def pack_sides(z, acc):
        for f in range(3):
            j = 2 * (f * levels_here + z)
            turned = pltpu.roll(ext[f, z + 1], j + 1, 1)
            acc = jnp.where((lane == j) | (lane == j + 1), turned, acc)
        j = 6 * levels_here + 2 * z
        turned = pltpu.roll(ext[0, z + 1], lax.rem(j + 2, LANES), 1)
        acc = jnp.where(lane == j, turned, acc)
        turned = pltpu.roll(class_ref[z].astype(jnp.float32), lax.rem(j + 2, LANES), 1)
        return jnp.where(lane == j + 1, turned, acc)

    first_class.wait()
    side_out[...] = lax.fori_loop(0, levels_here, pack_sides, jnp.zeros((planes, LANES), jnp.float32), unroll=True)
    low_out[0] = ext[1, levels_here - 1]
    low_out[1] = leaf_of(class_ref[levels_here - 1])
    pl.semaphore_wait(barrier, heights + rows + 2)

    def remote(src, dst, sems, slot, device):
        return pltpu.make_async_remote_copy(
            src_ref=src, dst_ref=dst, send_sem=sems.at[0, slot], recv_sem=sems.at[1, slot],
            device_id=device, device_id_type=MESH,
        )

    halo = [
        remote(side_out, side_in.at[0], side_sem, 0, at(1, 0)),
        remote(side_out, side_in.at[1], side_sem, 1, at(-1, 0)),
        remote(ext.at[:, levels_here], ext.at[:, 0], z_sem, 0, at(0, 1)),
        remote(ext.at[:, 1], ext.at[:, levels_here + 1], z_sem, 1, at(0, -1)),
        remote(low_out, low_in, z_sem, 2, at(0, 1)),
    ] + [
        remote(side_out, side_in.at[2 + i], side_sem, 2 + i, corner) for i, corner in enumerate(corners)
    ]
    for copy in halo:
        copy.start()

    def leaf_level(z, total):
        area = leaf_of(class_ref[z])
        area = jnp.where(h * levels_here + z < CANOPY, area, 0.0)
        leaf[z] = area
        return total + area

    leaf_sum[...] = lax.fori_loop(0, levels_here, leaf_level, jnp.zeros((planes, LANES), jnp.float32), unroll=UNROLL)
    leaf_copies = [
        remote(leaf_sum, leaf_in.at[0], leaf_sem, 0, at(0, -1)),
        remote(leaf_sum, leaf_in.at[1], leaf_sem, 1, at(0, -2)),
    ]
    for copy in leaf_copies:
        copy.start()

    for copy in halo:
        copy.wait()

    @pl.when(h == 0)
    def _():
        ext[:, 0] = jnp.zeros((3, planes, LANES), jnp.float32)

    @pl.when(h == heights - 1)
    def _():
        ext[:, levels_here + 1] = jnp.zeros((3, planes, LANES), jnp.float32)

    even = lax.rem(lane, 2) == 0
    from_left = side_in[0]
    side[...] = jnp.where(even, pltpu.roll(side_in[1], LANES - 1, 1), pltpu.roll(from_left, 1, 1))

    def stretch(q, u, w, east, west, above, below):
        advect = u * (east - west) * 0.5 + w * (above - below) * 0.5
        diffuse = VISCOSITY * (east + west + above + below - 4.0 * q)
        return diffuse - advect

    def drag(area, u, w):
        return DRAG_COEF * area * jnp.sqrt(u * u + w * w + SPAN_VAR)

    last = 2 * (levels_here - 1)
    w_left = pltpu.roll(from_left, LANES - 2 * levels_here, 1)
    u_far = pltpu.roll(from_left, LANES - 6 * levels_here, 1)
    class_left = pltpu.roll(from_left, LANES - 6 * levels_here - 1, 1)
    z_of_lane = h * levels_here + lane // 2
    area_left = jnp.where(z_of_lane < CANOPY, leaf_of(class_left), 0.0)
    u_east = pltpu.roll(side_out[...], LANES - 1, 1)
    corner_above = jnp.where(h < heights - 1, pltpu.roll(side_in[3], last, 1), 0.0)
    corner_below = jnp.where(h > 0, pltpu.roll(side_in[2], LANES - last, 1), 0.0)
    u_above = jnp.where(lane == last, corner_above, pltpu.roll(from_left, LANES - 2, 1))
    u_below = jnp.where(lane == 0, corner_below, pltpu.roll(from_left, 2, 1))
    u_side[...] = from_left + DT * (
        stretch(from_left, from_left, w_left, u_east, u_far, u_above, u_below)
        - drag(area_left, from_left, w_left) * from_left
    )

    u_low, w_low, t_low = ext[0, 0], ext[1, 0], ext[2, 0]
    j = 2 * (2 * levels_here - 1)
    w_east = jnp.where(
        lane == LANES - 1, pltpu.roll(side_in[4], LANES - 2 - j, 1), pltpu.roll(w_low, LANES - 1, 1)
    )
    w_west = jnp.where(lane == 0, pltpu.roll(side_in[2], LANES - j, 1), pltpu.roll(w_low, 1, 1))
    area_low = jnp.where(h * levels_here - 1 < CANOPY, low_in[1], 0.0)
    w_star_low = w_low + DT * (
        stretch(w_low, u_low, w_low, w_east, w_west, ext[1, 1], low_in[0])
        - drag(area_low, u_low, w_low) * w_low
        + THERMAL_LIFT * t_low
    )
    w_star_low = jnp.where(h > 0, w_star_low, 0.0)

    def growth(f, z, u, w):
        q = ext[f, z + 1]
        j = 2 * (f * levels_here + z)
        edge = pltpu.roll(side[...], LANES - 1 - j, 1)
        east = jnp.where(lane == LANES - 1, edge, pltpu.roll(q, LANES - 1, 1))
        west = jnp.where(lane == 0, edge, pltpu.roll(q, 1, 1))
        return stretch(q, u, w, east, west, ext[f, z + 2], ext[f, z])

    def winds(z, w_below):
        u = ext[0, z + 1]
        w = ext[1, z + 1]
        t = ext[2, z + 1]
        friction = drag(leaf[z], u, w)
        u_star = u + DT * (growth(0, z, u, w) - friction * u)
        w_star = w + DT * (growth(1, z, u, w) - friction * w + THERMAL_LIFT * t)
        w_star = jnp.where(h * levels_here + z == nz - 1, 0.0, w_star)
        us[z] = u_star
        ws[z] = w_star
        edge = pltpu.roll(u_side[...], lax.rem(LANES - 2 * z, LANES), 1)
        west = jnp.where(lane == 0, edge, pltpu.roll(u_star, 1, 1))
        d_out[pl.ds(z, planes, stride=levels_here), :] = u_star - west + (w_star - w_below)
        return w_star

    lax.fori_loop(0, levels_here, winds, w_star_low, unroll=UNROLL)

    def finish(buffer, count, sem):
        part = buffer.at[pl.ds(0, count)]
        pltpu.make_async_copy(part, part, sem).wait()

    for y in range(2):

        for i in range(heights - 1):
            to = height_peer(i)
            pltpu.make_async_remote_copy(
                src_ref=d_out.at[pl.ds((2 * to + y) * levels_here, levels_here)],
                dst_ref=d_in.at[y, pl.ds(h * levels_here, levels_here)],
                send_sem=a2a_sem.at[0], recv_sem=a2a_sem.at[1 + y],
                device_id=(r, to), device_id_type=MESH,
            ).start()
    for y in range(2):
        d_in[y, pl.ds(h * levels_here, levels_here)] = d_out[
            pl.ds((2 * h + y) * levels_here, levels_here)
        ]
    star_out = [
        pltpu.make_async_copy(us, us_hbm, out_sem.at[0]),
        pltpu.make_async_copy(ws, ws_hbm, out_sem.at[1]),
    ]
    for copy in star_out:
        copy.start()
    for copy in others[:2]:
        copy.wait()

    for copy in leaf_copies:
        copy.wait()
    above1 = jnp.where(h < heights - 1, leaf_in[0], 0.0)
    above2 = jnp.where(h < heights - 2, leaf_in[1], 0.0)
    over = above1 + above2
    sun = sun_ref[...]
    first = jnp.exp(-(0.5 * over + haze_ref[h * levels_here + levels_here]))

    def heat(k, state):
        over, top = state
        z = levels_here - 1 - k
        over = over + leaf[z]
        bottom = jnp.exp(-(0.5 * over + haze_ref[h * levels_here + z]))
        warming = sun * (top - bottom)
        absorb = jnp.where(paved_ref[...] == 1, PAVED_ABSORB, GRASS_ABSORB)
        warming = warming + jnp.where(h * levels_here + z == 0, sun * bottom * absorb, 0.0)
        t = ext[2, z + 1]
        tn_ref[z] = t + DT * (growth(2, z, ext[0, z + 1], ext[1, z + 1]) + warming)
        return over, bottom

    lax.fori_loop(0, levels_here, heat, (over, first), unroll=UNROLL)
    warm_out = pltpu.make_async_copy(tn_ref, tn_hbm, out_sem.at[2])
    warm_out.start()
    for copy in others[2:]:
        copy.wait()

    lane8 = lax.broadcasted_iota(jnp.int32, (8, LANES), 1)
    sub8 = lax.broadcasted_iota(jnp.int32, (8, LANES), 0)
    chunk = min(64, nz)
    lane_c = lax.broadcasted_iota(jnp.int32, (chunk, LANES), 1)
    slot = (sub8 == 0) & (lane8 == 0)

    def row_scans(y):
        finish(d_in.at[y], (heights - 1) * levels_here, a2a_sem.at[1 + y])
        modes = jnp.dot(
            cosine_ref[...], d_in[y], precision=HIGHEST, preferred_element_type=jnp.float32
        )
        packed = jnp.zeros((8, LANES), jnp.float32)
        for start in range(0, nz, chunk):
            part = slice(start, start + chunk)
            d = modes[part]
            fwd = d
            bwd = d
            for k in range(7):
                s = 1 << k
                fwd = fwd + scan_e_ref[k, part, :] * pltpu.roll(fwd, s, 1)
                bwd = bwd + scan_w_ref[k, part, :] * pltpu.roll(bwd, LANES - s, 1)
            local = gain_ref[part, :] * (fwd + bwd - d)
            ends = jnp.where(lane_c == 0, bwd, fwd)
            if start == 0:
                zero = d[0:8]
                own = jnp.dot(
                    zero, near_ref[...], precision=HIGHEST, preferred_element_type=jnp.float32
                )
                own_next = jnp.dot(
                    zero, near_next_ref[...], precision=HIGHEST, preferred_element_type=jnp.float32
                )
                first_moment = jnp.sum(zero * lane8.astype(jnp.float32), axis=1, keepdims=True)
                pm[y, 0:8] = jnp.where(sub8 == 0, own, local[0:8])
                pm[y, 8:chunk] = local[8:]
            else:
                pm[y, part] = local
            for i in range(chunk // 8):
                value = ends[8 * i : 8 * i + 8]
                if start == 0 and i == 0:
                    value = jnp.where(slot, jnp.broadcast_to(first_moment, (8, LANES)), value)
                j = 2 * (start // 8 + i)
                turned = pltpu.roll(value, j, 1) if j else value
                mine = (lane8 == j) | (lane8 == (j + LANES - 1) % LANES)
                packed = jnp.where(mine, turned, packed)
        mom[y, r] = packed

        for i in range(rows - 1):
            pltpu.make_async_remote_copy(
                src_ref=mom.at[y, r], dst_ref=mom.at[y, r],
                send_sem=mom_sem.at[0], recv_sem=mom_sem.at[1 + y],
                device_id=row_peer(i), device_id_type=MESH,
            ).start()
        return own_next

    def row_solve(y, own_next):
        finish(mom.at[y], rows - 1, mom_sem.at[1 + y])

        def gather_moments(i, state):
            direct, cross = state
            values = mom[y, lax.rem(r + i, rows)]
            return direct + direct_ref[i] * values, cross + cross_ref[i] * values

        nothing = jnp.zeros((8, LANES), jnp.float32)
        direct, cross = lax.fori_loop(0, rows, gather_moments, (nothing, nothing), unroll=UNROLL)
        inflow = direct + jnp.where(
            lax.rem(lane8, 2) == 0, pltpu.roll(cross, 1, 1), pltpu.roll(cross, LANES - 1, 1)
        )
        for g in range(groups):
            part = slice(8 * g, 8 * g + 8)
            j = 2 * g
            west = (j + LANES - 1) % LANES
            from_east = jnp.broadcast_to(inflow[:, j : j + 1], (8, LANES))
            from_west = jnp.broadcast_to(inflow[:, west : west + 1], (8, LANES))
            onward = pm[y, part] + phi_w_ref[part, :] * from_west
            pm[y, part] = onward + phi_e_ref[part, :] * from_east
            beyond = (
                scan_w_ref[0, part, :] * jnp.broadcast_to(onward[:, LANES - 1 :], (8, LANES))
                + gain_ref[part, :] * from_east
            )
            if g == 0:
                beyond = jnp.where(
                    sub8 == 0, own_next + from_west + float(LANES) * from_east, beyond
                )
            extra[part, :] = beyond
        solved = jnp.dot(
            cosine_t_ref[...], pm[y], precision=HIGHEST, preferred_element_type=jnp.float32
        )
        beyond = jnp.dot(
            jnp.transpose(extra[...])[0:8], cosine_ref[...],
            precision=HIGHEST, preferred_element_type=jnp.float32,
        )
        for to in range(heights):
            z0 = to * levels_here
            half = z0 // LANES
            top = min(z0 + levels_here, nz - 1)
            p_out[y, to, 0:levels_here] = solved[z0 : z0 + levels_here]
            p_out[y, to, levels_here : levels_here + 1] = solved[top : top + 1]
            p_out[y, to, levels_here + 1 : levels_here + 2] = beyond[
                0:1, half * LANES : (half + 1) * LANES
            ]

        for i in range(heights - 1):
            to = height_peer(i)
            pltpu.make_async_remote_copy(
                src_ref=p_out.at[y, to, pl.ds(0, TALL)],
                dst_ref=p_in.at[2 * h + y, pl.ds(0, TALL)],
                send_sem=back_sem.at[0], recv_sem=back_sem.at[1],
                device_id=(r, to), device_id_type=MESH,
            ).start()
        own_block = pltpu.make_async_copy(
            p_out.at[y, h, pl.ds(0, TALL)], p_in.at[2 * h + y, pl.ds(0, TALL)], out_sem.at[3 + y]
        )
        own_block.start()
        return own_block

    own_next = [row_scans(0), row_scans(1)]
    own_blocks = [row_solve(0, own_next[0]), row_solve(1, own_next[1])]
    finish(d_out, (heights - 1) * block, a2a_sem.at[0])
    part = mom.at[:, pl.ds(0, rows - 1)]
    pltpu.make_async_copy(part, part, mom_sem.at[0]).wait()
    warm_out.wait()
    for copy in star_out + own_blocks:
        copy.wait()
    for sem in (back_sem.at[1], back_sem.at[0]):
        part = p_in.at[pl.ds(0, 2 * (heights - 1)), pl.ds(0, TALL)]
        pltpu.make_async_copy(part, part, sem).wait()


def project_kernel(
    heights, us_hbm, ws_hbm, p_hbm, warm_hbm, un_hbm, wn_hbm, tn_hbm,
    us, ws, p_in, warm, un, wn, in_sem, out_sem,
):
    loads = [
        pltpu.make_async_copy(src, dst, in_sem.at[i])
        for i, (src, dst) in enumerate(((warm_hbm, warm), (p_hbm, p_in), (us_hbm, us), (ws_hbm, ws)))
    ]
    for load in loads:
        load.start()
    h = lax.axis_index("height")
    levels_here, planes = us.shape[0], us.shape[1]
    tall = SLOT
    lane = lax.broadcasted_iota(jnp.int32, (planes, LANES), 1)
    loads[0].wait()
    warm_out = pltpu.make_async_copy(warm, tn_hbm, out_sem.at[2])
    warm_out.start()
    for load in loads[1:]:
        load.wait()
    beyond = p_in[pl.ds(levels_here + 1, planes, stride=tall), :]
    first = lax.rem(h * levels_here, LANES)

    def project(z, p):
        edge = pltpu.roll(beyond, LANES - 1 - first - z, 1)
        east = jnp.where(lane == LANES - 1, edge, pltpu.roll(p, LANES - 1, 1))
        un[z] = us[z] - (east - p)
        above = p_in[pl.ds(z + 1, planes, stride=tall), :]
        wn[z] = ws[z] - (above - p)
        return above

    lax.fori_loop(0, levels_here, project, p_in[pl.ds(0, planes, stride=tall), :], unroll=UNROLL)
    stores = [
        pltpu.make_async_copy(un, un_hbm, out_sem.at[0]),
        pltpu.make_async_copy(wn, wn_hbm, out_sem.at[1]),
    ]
    for store in stores:
        store.start()
    warm_out.wait()
    for store in stores:
        store.wait()


def solution(mesh):
    rows, heights = mesh.shape["row"], mesh.shape["height"]

    def per_device(u, w, t, classes, paved, sun, lookup):
        levels_here, planes, width = u.shape
        nz = levels_here * heights
        table = tables(nz, width * rows, rows)
        smem = pl.BlockSpec(memory_space=pltpu.SMEM)
        hbm = pl.BlockSpec(memory_space=pl.ANY)
        field = jax.ShapeDtypeStruct(u.shape, jnp.float32)
        plane = (planes, LANES)
        f32 = jnp.float32
        dma = pltpu.SemaphoreType.DMA
        call = pl.pallas_call(
            functools.partial(kernel, rows, heights),
            out_shape=(field, field, jax.ShapeDtypeStruct((planes, SLOT, LANES), f32), field),
            in_specs=[hbm] * 6 + [smem] * 2 + [hbm] * 11,
            out_specs=(hbm,) * 4,
            scratch_shapes=[
                pltpu.VMEM((levels_here,) + plane, jnp.int32),
                pltpu.VMEM(plane, jnp.int32),
                pltpu.VMEM(plane, f32),
                pltpu.VMEM((nz, nz), f32),
                pltpu.VMEM((nz, nz), f32),
                pltpu.VMEM((7, nz, LANES), f32),
                pltpu.VMEM((7, nz, LANES), f32),
                pltpu.VMEM((nz, LANES), f32),
                pltpu.VMEM((nz, LANES), f32),
                pltpu.VMEM((nz, LANES), f32),
                pltpu.VMEM((LANES, LANES), f32),
                pltpu.VMEM((LANES, LANES), f32),
                pltpu.VMEM((rows, 8, LANES), f32),
                pltpu.VMEM((rows, 8, LANES), f32),
                pltpu.VMEM(u.shape, f32),
                pltpu.VMEM((3, levels_here + 2) + plane, f32),
                pltpu.VMEM((levels_here,) + plane, f32),
                pltpu.VMEM(plane, f32),
                pltpu.VMEM((2,) + plane, f32),
                pltpu.VMEM((2,) + plane, f32),
                pltpu.VMEM((2,) + plane, f32),
                pltpu.VMEM(plane, f32),
                pltpu.VMEM((5,) + plane, f32),
                pltpu.VMEM(plane, f32),
                pltpu.VMEM(plane, f32),
                pltpu.VMEM(u.shape, f32),
                pltpu.VMEM(u.shape, f32),
                pltpu.VMEM((2 * nz, LANES), f32),
                pltpu.VMEM((2, nz, LANES), f32),
                pltpu.VMEM((2, nz, LANES), f32),
                pltpu.VMEM((nz, LANES), f32),
                pltpu.VMEM((2, rows, 8, LANES), f32),
                pltpu.VMEM((2, heights, SLOT, LANES), f32),
                dma((3,)), dma((14,)), dma((5,)), dma((2, 3)), dma((2, 5)), dma((2, 2)),
                dma((3,)), dma((3,)), dma((2,)),
            ],
            compiler_params=pltpu.CompilerParams(
                collective_id=0, has_side_effects=True, vmem_limit_bytes=60 * 1024 * 1024
            ),
        )
        us, ws, p, warm = call(
            u, w, t, classes, paved, sun, lookup, table["haze"], table["cosine"],
            table["cosine_t"], table["scan_e"], table["scan_w"], table["gain"],
            table["phi_west"], table["phi_east"], table["near"], table["near_next"],
            table["direct"], table["cross"],
        )
        project = pl.pallas_call(
            functools.partial(project_kernel, heights),
            out_shape=(field, field, field),
            in_specs=[hbm] * 4,
            out_specs=(hbm,) * 3,
            scratch_shapes=[
                pltpu.VMEM(u.shape, f32), pltpu.VMEM(u.shape, f32), pltpu.VMEM((planes * SLOT, LANES), f32),
                pltpu.VMEM(u.shape, f32), pltpu.VMEM(u.shape, f32), pltpu.VMEM(u.shape, f32),
                dma((4,)), dma((3,)),
            ],
            compiler_params=pltpu.CompilerParams(vmem_limit_bytes=60 * 1024 * 1024),
        )
        return project(us, ws, p.reshape(planes * SLOT, LANES), warm)

    field = P("height", None, "row")
    line = P(None, "row")
    return jax.shard_map(
        per_device, mesh=mesh, in_specs=(field, field, field, field, line, line, P()),
        out_specs=(field, field, field), check_vma=False,
    )
```

```python
import functools
import math

import jax
import jax.numpy as jnp
import numpy as np
from jax import lax
from jax.experimental import pallas as pl
from jax.experimental.pallas import tpu as pltpu
from jax.sharding import PartitionSpec as P

CANOPY = 48
DT = 0.25
VISCOSITY = 0.05
DRAG_COEF = 0.2
THERMAL_LIFT = 0.2
SPAN_VAR = 0.25
HAZE_EXTINCT = 0.02
PAVED_ABSORB = 0.9
GRASS_ABSORB = 0.5
MESH = pl.DeviceIdType.MESH
UNROLL = True
TALL = 18
SLOT = 24
HIGHEST = lax.Precision.HIGHEST
LANES = 128


def tables(levels, columns, row_count):
    m = np.arange(levels, dtype=np.float64)
    z = np.arange(levels, dtype=np.float64)
    cosine = np.cos(np.pi * m[:, None] * (z[None, :] + 0.5) / levels)
    cosine *= np.where(m == 0, math.sqrt(1.0 / levels), math.sqrt(2.0 / levels))[:, None]
    mu = 2.0 * np.arcsinh(np.sin(np.pi * m / (2.0 * levels)))
    safe = np.where(m == 0, 1.0, mu)
    gain = np.where(m == 0, 0.0, -1.0 / (2.0 * np.sinh(safe)))
    x = np.arange(LANES, dtype=np.float64)
    scan_e = np.zeros((7, levels, LANES))
    scan_w = np.zeros((7, levels, LANES))
    for k in range(7):
        rate = np.exp(-mu * 2.0**k)[:, None]
        scan_e[k] = np.where(x[None, :] >= 2**k, rate, 0.0)
        scan_w[k] = np.where(x[None, :] < LANES - 2**k, rate, 0.0)
    gain_full = np.broadcast_to(gain[:, None], (levels, LANES))
    phi_west = np.where(m[:, None] == 0, 1.0, gain[:, None] * np.exp(-mu[:, None] * (x + 1.0)))
    phi_east = np.where(m[:, None] == 0, x, gain[:, None] * np.exp(-mu[:, None] * (LANES - x)))
    near = 0.5 * np.abs(x[:, None] - x[None, :]) + x[:, None] * x[None, :] / columns
    near_next = np.broadcast_to((0.5 * (LANES - x) + LANES * x / columns)[:, None], (LANES, LANES))
    lane = np.arange(LANES)
    odd = lane % 2 == 1
    group = np.where(odd, (lane + 1) // 2, lane // 2) % 64
    per_plane = levels // 8
    used = group < 2 * per_plane
    mode = 8 * (group % per_plane)[None, :] + np.arange(8)[:, None]
    mode_mu = mu[mode]
    safe_mu = np.where(mode == 0, 1.0, mode_mu)
    direct = np.zeros((row_count, 8, LANES))
    cross = np.zeros((row_count, 8, LANES))
    for shift in range(row_count):
        to_east = shift if shift else row_count
        to_west = row_count - shift
        steps = np.where(odd, to_west, to_east)[None, :]
        usual = np.exp(-safe_mu * LANES * (steps - 1)) / (1.0 - np.exp(-safe_mu * columns))
        away = float(LANES * shift)
        if shift:
            zero_direct = np.where(odd, away / 2 - away**2 / (2 * columns), 1.0 / columns)
            zero_cross = np.where(odd, -0.5 + away / columns, 0.5 - away / columns)
        else:
            zero_direct = np.zeros(LANES)
            zero_cross = np.zeros(LANES)
        direct[shift] = np.where(mode == 0, zero_direct[None, :], usual) * used
        cross[shift] = np.where(mode == 0, zero_cross[None, :], 0.0) * used
    haze = HAZE_EXTINCT * np.exp(-4.0 * (z + 0.5) / levels)
    haze_above = np.concatenate([np.cumsum(haze[::-1])[::-1], [0.0]])
    f32 = lambda a: np.ascontiguousarray(a, dtype=np.float32)
    return dict(
        cosine=f32(cosine), cosine_t=f32(cosine.T), scan_e=f32(scan_e), scan_w=f32(scan_w), gain=f32(gain_full), phi_west=f32(phi_west),
        phi_east=f32(phi_east), near=f32(near), near_next=f32(near_next), direct=f32(direct), cross=f32(cross),
        haze=f32(haze_above),
    )


def kernel(
    rows, heights,
    u_hbm, w_hbm, t_hbm, class_hbm, paved_hbm, sun_hbm, lookup_ref, haze_ref,
    cosine_hbm, cosine_t_hbm, scan_e_hbm, scan_w_hbm, gain_hbm, phi_w_hbm, phi_e_hbm, near_hbm,
    near_next_hbm, direct_hbm, cross_hbm,
    us, ws, p_in, tn_ref,
    class_ref, paved_ref, sun_ref,
    cosine_ref, cosine_t_ref, scan_e_ref, scan_w_ref, gain_ref, phi_w_ref, phi_e_ref, near_ref,
    near_next_ref, direct_ref, cross_ref,
    ext, leaf, leaf_sum, leaf_in, low_out, low_in, side_out, side_in, side, u_side,
    d_out, d_in, pm, extra, mom, p_out,
    in_sem, other_sem,
    z_sem, side_sem, leaf_sem, a2a_sem, mom_sem, back_sem,
):
    r = lax.axis_index("row")
    h = lax.axis_index("height")
    levels_here = class_ref.shape[0]
    planes = class_ref.shape[1]
    nz = levels_here * heights
    block = 2 * levels_here
    groups = nz // 8

    def at(dr, dh):
        return (lax.rem(r + dr + rows, rows), lax.rem(h + dh + heights, heights))

    depth = 8 if rows % 8 == 0 else rows
    wide = rows // depth
    x_of, z_of = lax.div(r, depth), lax.rem(r, depth)

    def outward(i, count):
        return count // 2 + ((i + 1) // 2) * (1 - 2 * (i % 2))

    def row_peer(i):
        x = lax.rem(x_of + outward(i // depth, wide), wide)
        return (x * depth + lax.rem(z_of + outward(i % depth, depth), depth), h)

    def height_peer(i):
        return lax.rem(h + outward(i, heights), heights)

    barrier = pltpu.get_barrier_semaphore()

    for i in range(rows - 1):
        pl.semaphore_signal(barrier, inc=1, device_id=row_peer(i), device_id_type=MESH)
    for i in range(heights - 1):
        pl.semaphore_signal(barrier, inc=1, device_id=(r, height_peer(i)), device_id_type=MESH)
    corners = (at(1, 1), at(1, -1), at(-1, 1))
    for corner in (*corners, at(-1, -1)):
        pl.semaphore_signal(barrier, inc=1, device_id=corner, device_id_type=MESH)
    first_class = pltpu.make_async_copy(class_hbm, class_ref, other_sem.at[0])
    loads = [
        pltpu.make_async_copy(ref, ext.at[f, pl.ds(1, levels_here)], in_sem.at[f])
        for f, ref in enumerate((u_hbm, w_hbm, t_hbm))
    ]
    for load in loads:
        load.start()
    first_class.start()
    others = [
        pltpu.make_async_copy(src, dst, other_sem.at[i + 1])
        for i, (src, dst) in enumerate((
            (paved_hbm, paved_ref), (sun_hbm, sun_ref),
            (cosine_hbm, cosine_ref), (scan_e_hbm, scan_e_ref), (scan_w_hbm, scan_w_ref),
            (gain_hbm, gain_ref), (near_hbm, near_ref), (phi_w_hbm, phi_w_ref),
            (phi_e_hbm, phi_e_ref), (near_next_hbm, near_next_ref), (direct_hbm, direct_ref), (cross_hbm, cross_ref),
            (cosine_t_hbm, cosine_t_ref),
        ))
    ]
    for copy in others:
        copy.start()
    for load in loads:
        load.wait()
    lane = lax.broadcasted_iota(jnp.int32, (planes, LANES), 1)

    def leaf_of(classes):
        area = jnp.zeros((planes, LANES), jnp.float32)
        for c in range(lookup_ref.shape[0]):
            area = jnp.where(classes == c, lookup_ref[c], area)
        return area

    def pack_sides(z, acc):
        for f in range(3):
            j = 2 * (f * levels_here + z)
            turned = pltpu.roll(ext[f, z + 1], j + 1, 1)
            acc = jnp.where((lane == j) | (lane == j + 1), turned, acc)
        j = 6 * levels_here + 2 * z
        turned = pltpu.roll(ext[0, z + 1], lax.rem(j + 2, LANES), 1)
        acc = jnp.where(lane == j, turned, acc)
        turned = pltpu.roll(class_ref[z].astype(jnp.float32), lax.rem(j + 2, LANES), 1)
        return jnp.where(lane == j + 1, turned, acc)

    first_class.wait()
    side_out[...] = lax.fori_loop(0, levels_here, pack_sides, jnp.zeros((planes, LANES), jnp.float32), unroll=True)
    low_out[0] = ext[1, levels_here - 1]
    low_out[1] = leaf_of(class_ref[levels_here - 1])
    pl.semaphore_wait(barrier, heights + rows + 2)

    def remote(src, dst, sems, slot, device):
        return pltpu.make_async_remote_copy(
            src_ref=src, dst_ref=dst, send_sem=sems.at[0, slot], recv_sem=sems.at[1, slot],
            device_id=device, device_id_type=MESH,
        )

    halo = [
        remote(side_out, side_in.at[0], side_sem, 0, at(1, 0)),
        remote(side_out, side_in.at[1], side_sem, 1, at(-1, 0)),
        remote(ext.at[:, levels_here], ext.at[:, 0], z_sem, 0, at(0, 1)),
        remote(ext.at[:, 1], ext.at[:, levels_here + 1], z_sem, 1, at(0, -1)),
        remote(low_out, low_in, z_sem, 2, at(0, 1)),
    ] + [
        remote(side_out, side_in.at[2 + i], side_sem, 2 + i, corner) for i, corner in enumerate(corners)
    ]
    for copy in halo:
        copy.start()

    def leaf_level(z, total):
        area = leaf_of(class_ref[z])
        area = jnp.where(h * levels_here + z < CANOPY, area, 0.0)
        leaf[z] = area
        return total + area

    leaf_sum[...] = lax.fori_loop(0, levels_here, leaf_level, jnp.zeros((planes, LANES), jnp.float32), unroll=UNROLL)
    leaf_copies = [
        remote(leaf_sum, leaf_in.at[0], leaf_sem, 0, at(0, -1)),
        remote(leaf_sum, leaf_in.at[1], leaf_sem, 1, at(0, -2)),
    ]
    for copy in leaf_copies:
        copy.start()

    for copy in halo:
        copy.wait()

    @pl.when(h == 0)
    def _():
        ext[:, 0] = jnp.zeros((3, planes, LANES), jnp.float32)

    @pl.when(h == heights - 1)
    def _():
        ext[:, levels_here + 1] = jnp.zeros((3, planes, LANES), jnp.float32)

    even = lax.rem(lane, 2) == 0
    from_left = side_in[0]
    side[...] = jnp.where(even, pltpu.roll(side_in[1], LANES - 1, 1), pltpu.roll(from_left, 1, 1))

    def stretch(q, u, w, east, west, above, below):
        advect = u * (east - west) * 0.5 + w * (above - below) * 0.5
        diffuse = VISCOSITY * (east + west + above + below - 4.0 * q)
        return diffuse - advect

    def drag(area, u, w):
        return DRAG_COEF * area * jnp.sqrt(u * u + w * w + SPAN_VAR)

    last = 2 * (levels_here - 1)
    w_left = pltpu.roll(from_left, LANES - 2 * levels_here, 1)
    u_far = pltpu.roll(from_left, LANES - 6 * levels_here, 1)
    class_left = pltpu.roll(from_left, LANES - 6 * levels_here - 1, 1)
    z_of_lane = h * levels_here + lane // 2
    area_left = jnp.where(z_of_lane < CANOPY, leaf_of(class_left), 0.0)
    u_east = pltpu.roll(side_out[...], LANES - 1, 1)
    corner_above = jnp.where(h < heights - 1, pltpu.roll(side_in[3], last, 1), 0.0)
    corner_below = jnp.where(h > 0, pltpu.roll(side_in[2], LANES - last, 1), 0.0)
    u_above = jnp.where(lane == last, corner_above, pltpu.roll(from_left, LANES - 2, 1))
    u_below = jnp.where(lane == 0, corner_below, pltpu.roll(from_left, 2, 1))
    u_side[...] = from_left + DT * (
        stretch(from_left, from_left, w_left, u_east, u_far, u_above, u_below)
        - drag(area_left, from_left, w_left) * from_left
    )

    u_low, w_low, t_low = ext[0, 0], ext[1, 0], ext[2, 0]
    j = 2 * (2 * levels_here - 1)
    w_east = jnp.where(
        lane == LANES - 1, pltpu.roll(side_in[4], LANES - 2 - j, 1), pltpu.roll(w_low, LANES - 1, 1)
    )
    w_west = jnp.where(lane == 0, pltpu.roll(side_in[2], LANES - j, 1), pltpu.roll(w_low, 1, 1))
    area_low = jnp.where(h * levels_here - 1 < CANOPY, low_in[1], 0.0)
    w_star_low = w_low + DT * (
        stretch(w_low, u_low, w_low, w_east, w_west, ext[1, 1], low_in[0])
        - drag(area_low, u_low, w_low) * w_low
        + THERMAL_LIFT * t_low
    )
    w_star_low = jnp.where(h > 0, w_star_low, 0.0)

    def growth(f, z, u, w):
        q = ext[f, z + 1]
        j = 2 * (f * levels_here + z)
        edge = pltpu.roll(side[...], LANES - 1 - j, 1)
        east = jnp.where(lane == LANES - 1, edge, pltpu.roll(q, LANES - 1, 1))
        west = jnp.where(lane == 0, edge, pltpu.roll(q, 1, 1))
        return stretch(q, u, w, east, west, ext[f, z + 2], ext[f, z])

    def winds(z, w_below):
        u = ext[0, z + 1]
        w = ext[1, z + 1]
        t = ext[2, z + 1]
        friction = drag(leaf[z], u, w)
        u_star = u + DT * (growth(0, z, u, w) - friction * u)
        w_star = w + DT * (growth(1, z, u, w) - friction * w + THERMAL_LIFT * t)
        w_star = jnp.where(h * levels_here + z == nz - 1, 0.0, w_star)
        us[z] = u_star
        ws[z] = w_star
        edge = pltpu.roll(u_side[...], lax.rem(LANES - 2 * z, LANES), 1)
        west = jnp.where(lane == 0, edge, pltpu.roll(u_star, 1, 1))
        d_out[pl.ds(z, planes, stride=levels_here), :] = u_star - west + (w_star - w_below)
        return w_star

    lax.fori_loop(0, levels_here, winds, w_star_low, unroll=UNROLL)

    def finish(buffer, count, sem):
        part = buffer.at[pl.ds(0, count)]
        pltpu.make_async_copy(part, part, sem).wait()

    for y in range(2):

        for i in range(heights - 1):
            to = height_peer(i)
            pltpu.make_async_remote_copy(
                src_ref=d_out.at[pl.ds((2 * to + y) * levels_here, levels_here)],
                dst_ref=d_in.at[y, pl.ds(h * levels_here, levels_here)],
                send_sem=a2a_sem.at[0], recv_sem=a2a_sem.at[1 + y],
                device_id=(r, to), device_id_type=MESH,
            ).start()
    for y in range(2):
        d_in[y, pl.ds(h * levels_here, levels_here)] = d_out[
            pl.ds((2 * h + y) * levels_here, levels_here)
        ]
    for copy in others[:2]:
        copy.wait()

    for copy in leaf_copies:
        copy.wait()
    above1 = jnp.where(h < heights - 1, leaf_in[0], 0.0)
    above2 = jnp.where(h < heights - 2, leaf_in[1], 0.0)
    over = above1 + above2
    sun = sun_ref[...]
    first = jnp.exp(-(0.5 * over + haze_ref[h * levels_here + levels_here]))

    def heat(k, state):
        over, top = state
        z = levels_here - 1 - k
        over = over + leaf[z]
        bottom = jnp.exp(-(0.5 * over + haze_ref[h * levels_here + z]))
        warming = sun * (top - bottom)
        absorb = jnp.where(paved_ref[...] == 1, PAVED_ABSORB, GRASS_ABSORB)
        warming = warming + jnp.where(h * levels_here + z == 0, sun * bottom * absorb, 0.0)
        t = ext[2, z + 1]
        tn_ref[z] = t + DT * (growth(2, z, ext[0, z + 1], ext[1, z + 1]) + warming)
        return over, bottom

    lax.fori_loop(0, levels_here, heat, (over, first), unroll=UNROLL)
    for copy in others[2:]:
        copy.wait()

    lane8 = lax.broadcasted_iota(jnp.int32, (8, LANES), 1)
    sub8 = lax.broadcasted_iota(jnp.int32, (8, LANES), 0)
    chunk = min(64, nz)
    lane_c = lax.broadcasted_iota(jnp.int32, (chunk, LANES), 1)
    slot = (sub8 == 0) & (lane8 == 0)

    def row_scans(y):
        finish(d_in.at[y], (heights - 1) * levels_here, a2a_sem.at[1 + y])
        modes = jnp.dot(
            cosine_ref[...], d_in[y], precision=HIGHEST, preferred_element_type=jnp.float32
        )
        packed = jnp.zeros((8, LANES), jnp.float32)
        for start in range(0, nz, chunk):
            part = slice(start, start + chunk)
            d = modes[part]
            fwd = d
            bwd = d
            for k in range(7):
                s = 1 << k
                fwd = fwd + scan_e_ref[k, part, :] * pltpu.roll(fwd, s, 1)
                bwd = bwd + scan_w_ref[k, part, :] * pltpu.roll(bwd, LANES - s, 1)
            local = gain_ref[part, :] * (fwd + bwd - d)
            ends = jnp.where(lane_c == 0, bwd, fwd)
            if start == 0:
                zero = d[0:8]
                first_moment = jnp.sum(zero * lane8.astype(jnp.float32), axis=1, keepdims=True)
            pm[y, part] = local
            for i in range(chunk // 8):
                value = ends[8 * i : 8 * i + 8]
                if start == 0 and i == 0:
                    value = jnp.where(slot, jnp.broadcast_to(first_moment, (8, LANES)), value)
                j = 2 * (start // 8 + i)
                turned = pltpu.roll(value, j, 1) if j else value
                mine = (lane8 == j) | (lane8 == (j + LANES - 1) % LANES)
                packed = jnp.where(mine, turned, packed)
        mom[y, r] = packed

        for i in range(rows - 1):
            pltpu.make_async_remote_copy(
                src_ref=mom.at[y, r], dst_ref=mom.at[y, r],
                send_sem=mom_sem.at[0], recv_sem=mom_sem.at[1 + y],
                device_id=row_peer(i), device_id_type=MESH,
            ).start()
        own = jnp.dot(zero, near_ref[...], precision=HIGHEST, preferred_element_type=jnp.float32)
        pm[y, 0:8] = jnp.where(sub8 == 0, own, pm[y, 0:8])
        return jnp.dot(
            zero, near_next_ref[...], precision=HIGHEST, preferred_element_type=jnp.float32
        )

    def row_solve(y, own_next):
        finish(mom.at[y], rows - 1, mom_sem.at[1 + y])

        def gather_moments(i, state):
            direct, cross = state
            values = mom[y, lax.rem(r + i, rows)]
            return direct + direct_ref[i] * values, cross + cross_ref[i] * values

        nothing = jnp.zeros((8, LANES), jnp.float32)
        direct, cross = lax.fori_loop(0, rows, gather_moments, (nothing, nothing), unroll=UNROLL)
        inflow = direct + jnp.where(
            lax.rem(lane8, 2) == 0, pltpu.roll(cross, 1, 1), pltpu.roll(cross, LANES - 1, 1)
        )
        for g in range(groups):
            part = slice(8 * g, 8 * g + 8)
            j = 2 * g
            west = (j + LANES - 1) % LANES
            from_east = jnp.broadcast_to(inflow[:, j : j + 1], (8, LANES))
            from_west = jnp.broadcast_to(inflow[:, west : west + 1], (8, LANES))
            onward = pm[y, part] + phi_w_ref[part, :] * from_west
            pm[y, part] = onward + phi_e_ref[part, :] * from_east
            beyond = (
                scan_w_ref[0, part, :] * jnp.broadcast_to(onward[:, LANES - 1 :], (8, LANES))
                + gain_ref[part, :] * from_east
            )
            if g == 0:
                beyond = jnp.where(
                    sub8 == 0, own_next + from_west + float(LANES) * from_east, beyond
                )
            extra[part, :] = beyond
        solved = jnp.dot(
            cosine_t_ref[...], pm[y], precision=HIGHEST, preferred_element_type=jnp.float32
        )
        beyond = jnp.dot(
            jnp.transpose(extra[...])[0:8], cosine_ref[...],
            precision=HIGHEST, preferred_element_type=jnp.float32,
        )
        for to in range(heights):
            z0 = to * levels_here
            half = z0 // LANES
            top = min(z0 + levels_here, nz - 1)
            p_out[y, to, 0:levels_here] = solved[z0 : z0 + levels_here]
            p_out[y, to, levels_here : levels_here + 1] = solved[top : top + 1]
            p_out[y, to, levels_here + 1 : levels_here + 2] = beyond[
                0:1, half * LANES : (half + 1) * LANES
            ]

        for i in range(heights - 1):
            to = height_peer(i)
            pltpu.make_async_remote_copy(
                src_ref=p_out.at[y, to, pl.ds(0, TALL)],
                dst_ref=p_in.at[2 * h + y, pl.ds(0, TALL)],
                send_sem=back_sem.at[0], recv_sem=back_sem.at[1],
                device_id=(r, to), device_id_type=MESH,
            ).start()
        p_in[2 * h + y] = p_out[y, h]

    own_next = [row_scans(0), row_scans(1)]
    for y in range(2):
        row_solve(y, own_next[y])
    finish(d_out, (heights - 1) * block, a2a_sem.at[0])
    part = mom.at[:, pl.ds(0, rows - 1)]
    pltpu.make_async_copy(part, part, mom_sem.at[0]).wait()
    for sem in (back_sem.at[1], back_sem.at[0]):
        part = p_in.at[pl.ds(0, 2 * (heights - 1)), pl.ds(0, TALL)]
        pltpu.make_async_copy(part, part, sem).wait()


def project_kernel(
    heights, us, ws, p_in, warm, un_hbm, wn_hbm, tn_hbm, un, wn, out_sem,
):
    warm_out = pltpu.make_async_copy(warm, tn_hbm, out_sem.at[4])
    warm_out.start()
    h = lax.axis_index("height")
    levels_here, planes = us.shape[0], us.shape[1]
    lane = lax.broadcasted_iota(jnp.int32, (planes, LANES), 1)
    beyond = p_in[pl.ds(levels_here + 1, planes, stride=SLOT), :]
    first = lax.rem(h * levels_here, LANES)

    def project(z, p):
        edge = pltpu.roll(beyond, LANES - 1 - first - z, 1)
        east = jnp.where(lane == LANES - 1, edge, pltpu.roll(p, LANES - 1, 1))
        un[z] = us[z] - (east - p)
        above = p_in[pl.ds(z + 1, planes, stride=SLOT), :]
        wn[z] = ws[z] - (above - p)
        return above

    p = p_in[pl.ds(0, planes, stride=SLOT), :]
    half = levels_here // 2
    stores = []
    for part in range(2):
        p = lax.fori_loop(part * half, part * half + half, project, p, unroll=UNROLL)
        rows_here = pl.ds(part * half, half)
        for i, (src, dst) in enumerate(((un, un_hbm), (wn, wn_hbm))):
            store = pltpu.make_async_copy(
                src.at[rows_here], dst.at[rows_here], out_sem.at[2 * part + i]
            )
            store.start()
            stores.append(store)
    warm_out.wait()
    for store in stores:
        store.wait()


def solution(mesh):
    rows, heights = mesh.shape["row"], mesh.shape["height"]

    def per_device(u, w, t, classes, paved, sun, lookup):
        levels_here, planes, width = u.shape
        nz = levels_here * heights
        table = tables(nz, width * rows, rows)
        smem = pl.BlockSpec(memory_space=pltpu.SMEM)
        hbm = pl.BlockSpec(memory_space=pltpu.HBM)
        vmem = pl.BlockSpec(memory_space=pltpu.VMEM)
        field = jax.ShapeDtypeStruct(u.shape, jnp.float32)
        plane = (planes, LANES)
        f32 = jnp.float32
        dma = pltpu.SemaphoreType.DMA
        call = pl.pallas_call(
            functools.partial(kernel, rows, heights),
            out_shape=(field, field, jax.ShapeDtypeStruct((planes, SLOT, LANES), f32), field),
            in_specs=[hbm] * 6 + [smem] * 2 + [hbm] * 11,
            out_specs=(vmem,) * 4,
            scratch_shapes=[
                pltpu.VMEM((levels_here,) + plane, jnp.int32),
                pltpu.VMEM(plane, jnp.int32),
                pltpu.VMEM(plane, f32),
                pltpu.VMEM((nz, nz), f32),
                pltpu.VMEM((nz, nz), f32),
                pltpu.VMEM((7, nz, LANES), f32),
                pltpu.VMEM((7, nz, LANES), f32),
                pltpu.VMEM((nz, LANES), f32),
                pltpu.VMEM((nz, LANES), f32),
                pltpu.VMEM((nz, LANES), f32),
                pltpu.VMEM((LANES, LANES), f32),
                pltpu.VMEM((LANES, LANES), f32),
                pltpu.VMEM((rows, 8, LANES), f32),
                pltpu.VMEM((rows, 8, LANES), f32),
                pltpu.VMEM((3, levels_here + 2) + plane, f32),
                pltpu.VMEM((levels_here,) + plane, f32),
                pltpu.VMEM(plane, f32),
                pltpu.VMEM((2,) + plane, f32),
                pltpu.VMEM((2,) + plane, f32),
                pltpu.VMEM((2,) + plane, f32),
                pltpu.VMEM(plane, f32),
                pltpu.VMEM((5,) + plane, f32),
                pltpu.VMEM(plane, f32),
                pltpu.VMEM(plane, f32),
                pltpu.VMEM((2 * nz, LANES), f32),
                pltpu.VMEM((2, nz, LANES), f32),
                pltpu.VMEM((2, nz, LANES), f32),
                pltpu.VMEM((nz, LANES), f32),
                pltpu.VMEM((2, rows, 8, LANES), f32),
                pltpu.VMEM((2, heights, SLOT, LANES), f32),
                dma((3,)), dma((14,)), dma((2, 3)), dma((2, 5)), dma((2, 2)),
                dma((3,)), dma((3,)), dma((2,)),
            ],
            compiler_params=pltpu.CompilerParams(
                collective_id=0, has_side_effects=True, vmem_limit_bytes=24 * 1024 * 1024
            ),
        )
        stay = lambda a: pltpu.with_memory_space_constraint(jnp.asarray(a), pltpu.HBM)
        table = {name: stay(values) for name, values in table.items()}
        u, w, t, classes, paved, sun, lookup = map(
            stay, (u, w, t, classes, paved, sun, lookup)
        )
        us, ws, p, warm = call(
            u, w, t, classes, paved, sun, lookup, table["haze"], table["cosine"],
            table["cosine_t"], table["scan_e"], table["scan_w"], table["gain"],
            table["phi_west"], table["phi_east"], table["near"], table["near_next"],
            table["direct"], table["cross"],
        )
        project = pl.pallas_call(
            functools.partial(project_kernel, heights),
            out_shape=(field, field, field),
            in_specs=[vmem] * 4,
            out_specs=(hbm,) * 3,
            scratch_shapes=[pltpu.VMEM(u.shape, f32), pltpu.VMEM(u.shape, f32), dma((5,))],
            compiler_params=pltpu.CompilerParams(vmem_limit_bytes=24 * 1024 * 1024),
        )
        return project(us, ws, p.reshape(planes * SLOT, LANES), warm)

    field = P("height", None, "row")
    line = P(None, "row")
    return jax.shard_map(
        per_device, mesh=mesh, in_specs=(field, field, field, field, line, line, P()),
        out_specs=(field, field, field), check_vma=False,
    )
```

```python
import functools
import math

import jax
import jax.numpy as jnp
import numpy as np
from jax import lax
from jax.experimental import pallas as pl
from jax.experimental.pallas import tpu as pltpu
from jax.sharding import PartitionSpec as P

CANOPY = 48
DT = 0.25
VISCOSITY = 0.05
DRAG_COEF = 0.2
THERMAL_LIFT = 0.2
SPAN_VAR = 0.25
HAZE_EXTINCT = 0.02
PAVED_ABSORB = 0.9
GRASS_ABSORB = 0.5
MESH = pl.DeviceIdType.MESH
UNROLL = True
TALL = 18
SLOT = 24
HIGHEST = lax.Precision.HIGHEST
LANES = 128


def tables(levels, columns, row_count):
    m = np.arange(levels, dtype=np.float64)
    z = np.arange(levels, dtype=np.float64)
    cosine = np.cos(np.pi * m[:, None] * (z[None, :] + 0.5) / levels)
    cosine *= np.where(m == 0, math.sqrt(1.0 / levels), math.sqrt(2.0 / levels))[:, None]
    mu = 2.0 * np.arcsinh(np.sin(np.pi * m / (2.0 * levels)))
    safe = np.where(m == 0, 1.0, mu)
    gain = np.where(m == 0, 0.0, -1.0 / (2.0 * np.sinh(safe)))
    x = np.arange(LANES, dtype=np.float64)
    scan_e = np.zeros((7, levels, LANES))
    scan_w = np.zeros((7, levels, LANES))
    for k in range(7):
        rate = np.exp(-mu * 2.0**k)[:, None]
        scan_e[k] = np.where(x[None, :] >= 2**k, rate, 0.0)
        scan_w[k] = np.where(x[None, :] < LANES - 2**k, rate, 0.0)
    gain_full = np.broadcast_to(gain[:, None], (levels, LANES))
    phi_west = np.where(m[:, None] == 0, 1.0, gain[:, None] * np.exp(-mu[:, None] * (x + 1.0)))
    phi_east = np.where(m[:, None] == 0, x, gain[:, None] * np.exp(-mu[:, None] * (LANES - x)))
    near = 0.5 * np.abs(x[:, None] - x[None, :]) + x[:, None] * x[None, :] / columns
    near_next = np.broadcast_to((0.5 * (LANES - x) + LANES * x / columns)[:, None], (LANES, LANES))
    lane = np.arange(LANES)
    odd = lane % 2 == 1
    group = np.where(odd, (lane + 1) // 2, lane // 2) % 64
    per_plane = levels // 8
    used = group < 2 * per_plane
    mode = 8 * (group % per_plane)[None, :] + np.arange(8)[:, None]
    mode_mu = mu[mode]
    safe_mu = np.where(mode == 0, 1.0, mode_mu)
    direct = np.zeros((row_count, 8, LANES))
    cross = np.zeros((row_count, 8, LANES))
    for shift in range(row_count):
        to_east = shift if shift else row_count
        to_west = row_count - shift
        steps = np.where(odd, to_west, to_east)[None, :]
        usual = np.exp(-safe_mu * LANES * (steps - 1)) / (1.0 - np.exp(-safe_mu * columns))
        away = float(LANES * shift)
        if shift:
            zero_direct = np.where(odd, away / 2 - away**2 / (2 * columns), 1.0 / columns)
            zero_cross = np.where(odd, -0.5 + away / columns, 0.5 - away / columns)
        else:
            zero_direct = np.zeros(LANES)
            zero_cross = np.zeros(LANES)
        direct[shift] = np.where(mode == 0, zero_direct[None, :], usual) * used
        cross[shift] = np.where(mode == 0, zero_cross[None, :], 0.0) * used
    haze = HAZE_EXTINCT * np.exp(-4.0 * (z + 0.5) / levels)
    haze_above = np.concatenate([np.cumsum(haze[::-1])[::-1], [0.0]])
    f32 = lambda a: np.ascontiguousarray(a, dtype=np.float32)
    return dict(
        cosine=f32(cosine), cosine_t=f32(cosine.T), scan_e=f32(scan_e), scan_w=f32(scan_w), gain=f32(gain_full), phi_west=f32(phi_west),
        phi_east=f32(phi_east), near=f32(near), near_next=f32(near_next), direct=f32(direct), cross=f32(cross),
        haze=f32(haze_above),
    )


def kernel(
    rows, heights,
    u_hbm, w_hbm, t_hbm, class_hbm, paved_hbm, sun_hbm, lookup_ref, haze_ref,
    cosine_hbm, cosine_t_hbm, scan_e_hbm, scan_w_hbm, gain_hbm, phi_w_hbm, phi_e_hbm, near_hbm,
    near_next_hbm, direct_hbm, cross_hbm,
    us, ws, p_in, tn_ref,
    class_ref, paved_ref, sun_ref,
    cosine_ref, cosine_t_ref, scan_e_ref, scan_w_ref, gain_ref, phi_w_ref, phi_e_ref, near_ref,
    near_next_ref, direct_ref, cross_ref,
    ext, leaf, leaf_sum, leaf_in, low_out, low_in, side_out, side_in, side, u_side,
    d_out, d_in, pm, extra, mom, p_out,
    in_sem, other_sem,
    z_sem, side_sem, leaf_sem, a2a_sem, mom_sem, back_sem,
):
    r = lax.axis_index("row")
    h = lax.axis_index("height")
    levels_here = class_ref.shape[0]
    planes = class_ref.shape[1]
    nz = levels_here * heights
    block = 2 * levels_here
    groups = nz // 8

    def at(dr, dh):
        return (lax.rem(r + dr + rows, rows), lax.rem(h + dh + heights, heights))

    depth = 8 if rows % 8 == 0 else rows
    wide = rows // depth
    x_of, z_of = lax.div(r, depth), lax.rem(r, depth)

    def outward(i, count):
        return count // 2 + ((i + 1) // 2) * (1 - 2 * (i % 2))

    def row_peer(i):
        x = lax.rem(x_of + outward(i // depth, wide), wide)
        return (x * depth + lax.rem(z_of + outward(i % depth, depth), depth), h)

    def height_peer(i):
        return lax.rem(h + outward(i, heights), heights)

    barrier = pltpu.get_barrier_semaphore()

    for i in range(rows - 1):
        pl.semaphore_signal(barrier, inc=1, device_id=row_peer(i), device_id_type=MESH)
    for i in range(heights - 1):
        pl.semaphore_signal(barrier, inc=1, device_id=(r, height_peer(i)), device_id_type=MESH)
    corners = (at(1, 1), at(1, -1), at(-1, 1))
    for corner in (*corners, at(-1, -1)):
        pl.semaphore_signal(barrier, inc=1, device_id=corner, device_id_type=MESH)
    first_class = pltpu.make_async_copy(class_hbm, class_ref, other_sem.at[0])
    loads = [
        pltpu.make_async_copy(ref, ext.at[f, pl.ds(1, levels_here)], in_sem.at[f])
        for f, ref in enumerate((u_hbm, w_hbm, t_hbm))
    ]
    for load in loads:
        load.start()
    first_class.start()
    others = [
        pltpu.make_async_copy(src, dst, other_sem.at[i + 1])
        for i, (src, dst) in enumerate((
            (paved_hbm, paved_ref), (sun_hbm, sun_ref),
            (cosine_hbm, cosine_ref), (scan_e_hbm, scan_e_ref), (scan_w_hbm, scan_w_ref),
            (gain_hbm, gain_ref), (near_hbm, near_ref), (phi_w_hbm, phi_w_ref),
            (phi_e_hbm, phi_e_ref), (near_next_hbm, near_next_ref), (direct_hbm, direct_ref), (cross_hbm, cross_ref),
            (cosine_t_hbm, cosine_t_ref),
        ))
    ]
    for load in loads:
        load.wait()
    lane = lax.broadcasted_iota(jnp.int32, (planes, LANES), 1)

    def leaf_of(classes):
        area = jnp.zeros((planes, LANES), jnp.float32)
        for c in range(lookup_ref.shape[0]):
            area = jnp.where(classes == c, lookup_ref[c], area)
        return area

    def pack_sides(z, acc):
        for f in range(3):
            j = 2 * (f * levels_here + z)
            turned = pltpu.roll(ext[f, z + 1], j + 1, 1)
            acc = jnp.where((lane == j) | (lane == j + 1), turned, acc)
        j = 6 * levels_here + 2 * z
        turned = pltpu.roll(ext[0, z + 1], lax.rem(j + 2, LANES), 1)
        acc = jnp.where(lane == j, turned, acc)
        turned = pltpu.roll(class_ref[z].astype(jnp.float32), lax.rem(j + 2, LANES), 1)
        return jnp.where(lane == j + 1, turned, acc)

    first_class.wait()
    side_out[...] = lax.fori_loop(0, levels_here, pack_sides, jnp.zeros((planes, LANES), jnp.float32), unroll=True)
    low_out[0] = ext[1, levels_here - 1]
    low_out[1] = leaf_of(class_ref[levels_here - 1])
    pl.semaphore_wait(barrier, heights + rows + 2)

    def remote(src, dst, sems, slot, device):
        return pltpu.make_async_remote_copy(
            src_ref=src, dst_ref=dst, send_sem=sems.at[0, slot], recv_sem=sems.at[1, slot],
            device_id=device, device_id_type=MESH,
        )

    halo = [
        remote(side_out, side_in.at[0], side_sem, 0, at(1, 0)),
        remote(side_out, side_in.at[1], side_sem, 1, at(-1, 0)),
        remote(ext.at[:, levels_here], ext.at[:, 0], z_sem, 0, at(0, 1)),
        remote(ext.at[:, 1], ext.at[:, levels_here + 1], z_sem, 1, at(0, -1)),
        remote(low_out, low_in, z_sem, 2, at(0, 1)),
    ] + [
        remote(side_out, side_in.at[2 + i], side_sem, 2 + i, corner) for i, corner in enumerate(corners)
    ]
    for copy in halo:
        copy.start()
    for copy in others:
        copy.start()

    def leaf_level(z, total):
        area = leaf_of(class_ref[z])
        area = jnp.where(h * levels_here + z < CANOPY, area, 0.0)
        leaf[z] = area
        return total + area

    leaf_sum[...] = lax.fori_loop(0, levels_here, leaf_level, jnp.zeros((planes, LANES), jnp.float32), unroll=UNROLL)
    leaf_copies = [
        remote(leaf_sum, leaf_in.at[0], leaf_sem, 0, at(0, -1)),
        remote(leaf_sum, leaf_in.at[1], leaf_sem, 1, at(0, -2)),
    ]
    for copy in leaf_copies:
        copy.start()

    def stretch(q, u, w, east, west, above, below):
        advect = u * (east - west) * 0.5 + w * (above - below) * 0.5
        diffuse = VISCOSITY * (east + west + above + below - 4.0 * q)
        return diffuse - advect

    def drag(area, u, w):
        return DRAG_COEF * area * jnp.sqrt(u * u + w * w + SPAN_VAR)

    still = jnp.zeros((planes, LANES), jnp.float32)
    for z in range(levels_here):
        u, w, t = ext[0, z + 1], ext[1, z + 1], ext[2, z + 1]
        friction = drag(leaf[z], u, w)
        for f, q, star, lift in ((0, u, us, 0.0), (1, w, ws, THERMAL_LIFT * t)):
            east = jnp.where(lane == LANES - 1, 0.0, pltpu.roll(q, LANES - 1, 1))
            west = jnp.where(lane == 0, 0.0, pltpu.roll(q, 1, 1))
            above = ext[f, z + 2] if z < levels_here - 1 else still
            below = ext[f, z] if z > 0 else still
            star[z] = q + DT * (stretch(q, u, w, east, west, above, below) - friction * q + lift)

    for copy in halo:
        copy.wait()

    @pl.when(h == 0)
    def _():
        ext[:, 0] = jnp.zeros((3, planes, LANES), jnp.float32)

    @pl.when(h == heights - 1)
    def _():
        ext[:, levels_here + 1] = jnp.zeros((3, planes, LANES), jnp.float32)

    even = lax.rem(lane, 2) == 0
    from_left = side_in[0]
    side[...] = jnp.where(even, pltpu.roll(side_in[1], LANES - 1, 1), pltpu.roll(from_left, 1, 1))

    last = 2 * (levels_here - 1)
    w_left = pltpu.roll(from_left, LANES - 2 * levels_here, 1)
    u_far = pltpu.roll(from_left, LANES - 6 * levels_here, 1)
    class_left = pltpu.roll(from_left, LANES - 6 * levels_here - 1, 1)
    z_of_lane = h * levels_here + lane // 2
    area_left = jnp.where(z_of_lane < CANOPY, leaf_of(class_left), 0.0)
    u_east = pltpu.roll(side_out[...], LANES - 1, 1)
    corner_above = jnp.where(h < heights - 1, pltpu.roll(side_in[3], last, 1), 0.0)
    corner_below = jnp.where(h > 0, pltpu.roll(side_in[2], LANES - last, 1), 0.0)
    u_above = jnp.where(lane == last, corner_above, pltpu.roll(from_left, LANES - 2, 1))
    u_below = jnp.where(lane == 0, corner_below, pltpu.roll(from_left, 2, 1))
    u_side[...] = from_left + DT * (
        stretch(from_left, from_left, w_left, u_east, u_far, u_above, u_below)
        - drag(area_left, from_left, w_left) * from_left
    )

    u_low, w_low, t_low = ext[0, 0], ext[1, 0], ext[2, 0]
    j = 2 * (2 * levels_here - 1)
    w_east = jnp.where(
        lane == LANES - 1, pltpu.roll(side_in[4], LANES - 2 - j, 1), pltpu.roll(w_low, LANES - 1, 1)
    )
    w_west = jnp.where(lane == 0, pltpu.roll(side_in[2], LANES - j, 1), pltpu.roll(w_low, 1, 1))
    area_low = jnp.where(h * levels_here - 1 < CANOPY, low_in[1], 0.0)
    w_star_low = w_low + DT * (
        stretch(w_low, u_low, w_low, w_east, w_west, ext[1, 1], low_in[0])
        - drag(area_low, u_low, w_low) * w_low
        + THERMAL_LIFT * t_low
    )
    w_star_low = jnp.where(h > 0, w_star_low, 0.0)

    def growth(f, z, u, w):
        q = ext[f, z + 1]
        j = 2 * (f * levels_here + z)
        edge = pltpu.roll(side[...], LANES - 1 - j, 1)
        east = jnp.where(lane == LANES - 1, edge, pltpu.roll(q, LANES - 1, 1))
        west = jnp.where(lane == 0, edge, pltpu.roll(q, 1, 1))
        return stretch(q, u, w, east, west, ext[f, z + 2], ext[f, z])

    w_below = w_star_low
    for z in range(levels_here):
        u, w = ext[0, z + 1], ext[1, z + 1]
        sides = jnp.where(
            lane == 0, VISCOSITY + 0.5 * u, jnp.where(lane == LANES - 1, VISCOSITY - 0.5 * u, 0.0)
        )
        stars = []
        for f, star in ((0, us), (1, ws)):
            edge = pltpu.roll(side[...], LANES - 1 - 2 * (f * levels_here + z), 1)
            share = sides * edge
            if z == 0:
                share = share + (VISCOSITY + 0.5 * w) * ext[f, 0]
            if z == levels_here - 1:
                share = share + (VISCOSITY - 0.5 * w) * ext[f, levels_here + 1]
            stars.append(star[z] + DT * share)
        u_star, w_star = stars
        if z == levels_here - 1:
            w_star = jnp.where(h == heights - 1, 0.0, w_star)
        us[z] = u_star
        ws[z] = w_star
        edge = pltpu.roll(u_side[...], (LANES - 2 * z) % LANES, 1)
        west = jnp.where(lane == 0, edge, pltpu.roll(u_star, 1, 1))
        d_out[pl.ds(z, planes, stride=levels_here), :] = u_star - west + (w_star - w_below)
        w_below = w_star

    def finish(buffer, count, sem):
        part = buffer.at[pl.ds(0, count)]
        pltpu.make_async_copy(part, part, sem).wait()

    for y in range(2):

        for i in range(heights - 1):
            to = height_peer(i)
            pltpu.make_async_remote_copy(
                src_ref=d_out.at[pl.ds((2 * to + y) * levels_here, levels_here)],
                dst_ref=d_in.at[y, pl.ds(h * levels_here, levels_here)],
                send_sem=a2a_sem.at[0], recv_sem=a2a_sem.at[1 + y],
                device_id=(r, to), device_id_type=MESH,
            ).start()
    for y in range(2):
        d_in[y, pl.ds(h * levels_here, levels_here)] = d_out[
            pl.ds((2 * h + y) * levels_here, levels_here)
        ]
    for copy in others[:2]:
        copy.wait()

    for copy in leaf_copies:
        copy.wait()
    above1 = jnp.where(h < heights - 1, leaf_in[0], 0.0)
    above2 = jnp.where(h < heights - 2, leaf_in[1], 0.0)
    over = above1 + above2
    sun = sun_ref[...]
    first = jnp.exp(-(0.5 * over + haze_ref[h * levels_here + levels_here]))

    def heat(k, state):
        over, top = state
        z = levels_here - 1 - k
        over = over + leaf[z]
        bottom = jnp.exp(-(0.5 * over + haze_ref[h * levels_here + z]))
        warming = sun * (top - bottom)
        absorb = jnp.where(paved_ref[...] == 1, PAVED_ABSORB, GRASS_ABSORB)
        warming = warming + jnp.where(h * levels_here + z == 0, sun * bottom * absorb, 0.0)
        t = ext[2, z + 1]
        tn_ref[z] = t + DT * (growth(2, z, ext[0, z + 1], ext[1, z + 1]) + warming)
        return over, bottom

    lax.fori_loop(0, levels_here, heat, (over, first), unroll=UNROLL)
    for copy in others[2:]:
        copy.wait()

    lane8 = lax.broadcasted_iota(jnp.int32, (8, LANES), 1)
    sub8 = lax.broadcasted_iota(jnp.int32, (8, LANES), 0)
    chunk = min(64, nz)
    lane_c = lax.broadcasted_iota(jnp.int32, (chunk, LANES), 1)
    slot = (sub8 == 0) & (lane8 == 0)

    def row_scans(y):
        finish(d_in.at[y], (heights - 1) * levels_here, a2a_sem.at[1 + y])
        modes = jnp.dot(
            cosine_ref[...], d_in[y], precision=HIGHEST, preferred_element_type=jnp.float32
        )
        packed = jnp.zeros((8, LANES), jnp.float32)
        for start in range(0, nz, chunk):
            part = slice(start, start + chunk)
            d = modes[part]
            fwd = d
            bwd = d
            for k in range(7):
                s = 1 << k
                fwd = fwd + scan_e_ref[k, part, :] * pltpu.roll(fwd, s, 1)
                bwd = bwd + scan_w_ref[k, part, :] * pltpu.roll(bwd, LANES - s, 1)
            local = gain_ref[part, :] * (fwd + bwd - d)
            ends = jnp.where(lane_c == 0, bwd, fwd)
            if start == 0:
                zero = d[0:8]
                first_moment = jnp.sum(zero * lane8.astype(jnp.float32), axis=1, keepdims=True)
            pm[y, part] = local
            for i in range(chunk // 8):
                value = ends[8 * i : 8 * i + 8]
                if start == 0 and i == 0:
                    value = jnp.where(slot, jnp.broadcast_to(first_moment, (8, LANES)), value)
                j = 2 * (start // 8 + i)
                turned = pltpu.roll(value, j, 1) if j else value
                mine = (lane8 == j) | (lane8 == (j + LANES - 1) % LANES)
                packed = jnp.where(mine, turned, packed)
        mom[y, r] = packed

        for i in range(rows - 1):
            pltpu.make_async_remote_copy(
                src_ref=mom.at[y, r], dst_ref=mom.at[y, r],
                send_sem=mom_sem.at[0], recv_sem=mom_sem.at[1 + y],
                device_id=row_peer(i), device_id_type=MESH,
            ).start()
        own = jnp.dot(zero, near_ref[...], precision=HIGHEST, preferred_element_type=jnp.float32)
        pm[y, 0:8] = jnp.where(sub8 == 0, own, pm[y, 0:8])
        return jnp.dot(
            zero, near_next_ref[...], precision=HIGHEST, preferred_element_type=jnp.float32
        )

    def row_solve(y, own_next):
        finish(mom.at[y], rows - 1, mom_sem.at[1 + y])

        def gather_moments(i, state):
            direct, cross = state
            values = mom[y, lax.rem(r + i, rows)]
            return direct + direct_ref[i] * values, cross + cross_ref[i] * values

        nothing = jnp.zeros((8, LANES), jnp.float32)
        direct, cross = lax.fori_loop(0, rows, gather_moments, (nothing, nothing), unroll=UNROLL)
        inflow = direct + jnp.where(
            lax.rem(lane8, 2) == 0, pltpu.roll(cross, 1, 1), pltpu.roll(cross, LANES - 1, 1)
        )
        for g in range(groups):
            part = slice(8 * g, 8 * g + 8)
            j = 2 * g
            west = (j + LANES - 1) % LANES
            from_east = jnp.broadcast_to(inflow[:, j : j + 1], (8, LANES))
            from_west = jnp.broadcast_to(inflow[:, west : west + 1], (8, LANES))
            onward = pm[y, part] + phi_w_ref[part, :] * from_west
            pm[y, part] = onward + phi_e_ref[part, :] * from_east
            beyond = (
                scan_w_ref[0, part, :] * jnp.broadcast_to(onward[:, LANES - 1 :], (8, LANES))
                + gain_ref[part, :] * from_east
            )
            if g == 0:
                beyond = jnp.where(
                    sub8 == 0, own_next + from_west + float(LANES) * from_east, beyond
                )
            extra[part, :] = beyond
        solved = jnp.dot(
            cosine_t_ref[...], pm[y], precision=HIGHEST, preferred_element_type=jnp.float32
        )
        beyond = jnp.dot(
            jnp.transpose(extra[...])[0:8], cosine_ref[...],
            precision=HIGHEST, preferred_element_type=jnp.float32,
        )
        for to in range(heights):
            z0 = to * levels_here
            half = z0 // LANES
            top = min(z0 + levels_here, nz - 1)
            p_out[y, to, 0:levels_here] = solved[z0 : z0 + levels_here]
            p_out[y, to, levels_here : levels_here + 1] = solved[top : top + 1]
            p_out[y, to, levels_here + 1 : levels_here + 2] = beyond[
                0:1, half * LANES : (half + 1) * LANES
            ]

        for i in range(heights - 1):
            to = height_peer(i)
            pltpu.make_async_remote_copy(
                src_ref=p_out.at[y, to, pl.ds(0, TALL)],
                dst_ref=p_in.at[2 * h + y, pl.ds(0, TALL)],
                send_sem=back_sem.at[0], recv_sem=back_sem.at[1],
                device_id=(r, to), device_id_type=MESH,
            ).start()
        p_in[2 * h + y] = p_out[y, h]

    own_next = [row_scans(0), row_scans(1)]
    for y in range(2):
        row_solve(y, own_next[y])
    finish(d_out, (heights - 1) * block, a2a_sem.at[0])
    part = mom.at[:, pl.ds(0, rows - 1)]
    pltpu.make_async_copy(part, part, mom_sem.at[0]).wait()
    for sem in (back_sem.at[1], back_sem.at[0]):
        part = p_in.at[pl.ds(0, 2 * (heights - 1)), pl.ds(0, TALL)]
        pltpu.make_async_copy(part, part, sem).wait()


def project_kernel(
    heights, us, ws, p_in, warm, un_hbm, wn_hbm, tn_hbm, un, wn, out_sem,
):
    warm_out = pltpu.make_async_copy(warm, tn_hbm, out_sem.at[4])
    warm_out.start()
    h = lax.axis_index("height")
    levels_here, planes = us.shape[0], us.shape[1]
    lane = lax.broadcasted_iota(jnp.int32, (planes, LANES), 1)
    beyond = p_in[pl.ds(levels_here + 1, planes, stride=SLOT), :]
    first = lax.rem(h * levels_here, LANES)

    def project(z, p):
        edge = pltpu.roll(beyond, LANES - 1 - first - z, 1)
        east = jnp.where(lane == LANES - 1, edge, pltpu.roll(p, LANES - 1, 1))
        un[z] = us[z] - (east - p)
        above = p_in[pl.ds(z + 1, planes, stride=SLOT), :]
        wn[z] = ws[z] - (above - p)
        return above

    p = p_in[pl.ds(0, planes, stride=SLOT), :]
    half = levels_here // 2
    stores = []
    for part in range(2):
        p = lax.fori_loop(part * half, part * half + half, project, p, unroll=UNROLL)
        rows_here = pl.ds(part * half, half)
        for i, (src, dst) in enumerate(((un, un_hbm), (wn, wn_hbm))):
            store = pltpu.make_async_copy(
                src.at[rows_here], dst.at[rows_here], out_sem.at[2 * part + i]
            )
            store.start()
            stores.append(store)
    warm_out.wait()
    for store in stores:
        store.wait()


def solution(mesh):
    rows, heights = mesh.shape["row"], mesh.shape["height"]

    def per_device(u, w, t, classes, paved, sun, lookup):
        levels_here, planes, width = u.shape
        nz = levels_here * heights
        table = tables(nz, width * rows, rows)
        smem = pl.BlockSpec(memory_space=pltpu.SMEM)
        hbm = pl.BlockSpec(memory_space=pltpu.HBM)
        vmem = pl.BlockSpec(memory_space=pltpu.VMEM)
        field = jax.ShapeDtypeStruct(u.shape, jnp.float32)
        plane = (planes, LANES)
        f32 = jnp.float32
        dma = pltpu.SemaphoreType.DMA
        call = pl.pallas_call(
            functools.partial(kernel, rows, heights),
            out_shape=(field, field, jax.ShapeDtypeStruct((planes, SLOT, LANES), f32), field),
            in_specs=[hbm] * 6 + [smem] * 2 + [hbm] * 11,
            out_specs=(vmem,) * 4,
            scratch_shapes=[
                pltpu.VMEM((levels_here,) + plane, jnp.int32),
                pltpu.VMEM(plane, jnp.int32),
                pltpu.VMEM(plane, f32),
                pltpu.VMEM((nz, nz), f32),
                pltpu.VMEM((nz, nz), f32),
                pltpu.VMEM((7, nz, LANES), f32),
                pltpu.VMEM((7, nz, LANES), f32),
                pltpu.VMEM((nz, LANES), f32),
                pltpu.VMEM((nz, LANES), f32),
                pltpu.VMEM((nz, LANES), f32),
                pltpu.VMEM((LANES, LANES), f32),
                pltpu.VMEM((LANES, LANES), f32),
                pltpu.VMEM((rows, 8, LANES), f32),
                pltpu.VMEM((rows, 8, LANES), f32),
                pltpu.VMEM((3, levels_here + 2) + plane, f32),
                pltpu.VMEM((levels_here,) + plane, f32),
                pltpu.VMEM(plane, f32),
                pltpu.VMEM((2,) + plane, f32),
                pltpu.VMEM((2,) + plane, f32),
                pltpu.VMEM((2,) + plane, f32),
                pltpu.VMEM(plane, f32),
                pltpu.VMEM((5,) + plane, f32),
                pltpu.VMEM(plane, f32),
                pltpu.VMEM(plane, f32),
                pltpu.VMEM((2 * nz, LANES), f32),
                pltpu.VMEM((2, nz, LANES), f32),
                pltpu.VMEM((2, nz, LANES), f32),
                pltpu.VMEM((nz, LANES), f32),
                pltpu.VMEM((2, rows, 8, LANES), f32),
                pltpu.VMEM((2, heights, SLOT, LANES), f32),
                dma((3,)), dma((14,)), dma((2, 3)), dma((2, 5)), dma((2, 2)),
                dma((3,)), dma((3,)), dma((2,)),
            ],
            compiler_params=pltpu.CompilerParams(
                collective_id=0, has_side_effects=True, vmem_limit_bytes=24 * 1024 * 1024
            ),
        )
        stay = lambda a: pltpu.with_memory_space_constraint(jnp.asarray(a), pltpu.HBM)
        table = {name: stay(values) for name, values in table.items()}
        u, w, t, classes, paved, sun, lookup = map(
            stay, (u, w, t, classes, paved, sun, lookup)
        )
        us, ws, p, warm = call(
            u, w, t, classes, paved, sun, lookup, table["haze"], table["cosine"],
            table["cosine_t"], table["scan_e"], table["scan_w"], table["gain"],
            table["phi_west"], table["phi_east"], table["near"], table["near_next"],
            table["direct"], table["cross"],
        )
        project = pl.pallas_call(
            functools.partial(project_kernel, heights),
            out_shape=(field, field, field),
            in_specs=[vmem] * 4,
            out_specs=(hbm,) * 3,
            scratch_shapes=[pltpu.VMEM(u.shape, f32), pltpu.VMEM(u.shape, f32), dma((5,))],
            compiler_params=pltpu.CompilerParams(vmem_limit_bytes=24 * 1024 * 1024),
        )
        return project(us, ws, p.reshape(planes * SLOT, LANES), warm)

    field = P("height", None, "row")
    line = P(None, "row")
    return jax.shard_map(
        per_device, mesh=mesh, in_specs=(field, field, field, field, line, line, P()),
        out_specs=(field, field, field), check_vma=False,
    )
```

```python
import functools
import math

import jax
import jax.numpy as jnp
import numpy as np
from jax import lax
from jax.experimental import pallas as pl
from jax.experimental.pallas import tpu as pltpu
from jax.sharding import PartitionSpec as P

CANOPY = 48
DT = 0.25
VISCOSITY = 0.05
DRAG_COEF = 0.2
THERMAL_LIFT = 0.2
SPAN_VAR = 0.25
HAZE_EXTINCT = 0.02
PAVED_ABSORB = 0.9
GRASS_ABSORB = 0.5
MESH = pl.DeviceIdType.MESH
UNROLL = True
TALL = 18
SLOT = 24
HIGHEST = lax.Precision.HIGHEST
LANES = 128


def tables(levels, columns, row_count):
    m = np.arange(levels, dtype=np.float64)
    z = np.arange(levels, dtype=np.float64)
    cosine = np.cos(np.pi * m[:, None] * (z[None, :] + 0.5) / levels)
    cosine *= np.where(m == 0, math.sqrt(1.0 / levels), math.sqrt(2.0 / levels))[:, None]
    mu = 2.0 * np.arcsinh(np.sin(np.pi * m / (2.0 * levels)))
    safe = np.where(m == 0, 1.0, mu)
    gain = np.where(m == 0, 0.0, -1.0 / (2.0 * np.sinh(safe)))
    x = np.arange(LANES, dtype=np.float64)
    scan_e = np.zeros((7, levels, LANES))
    scan_w = np.zeros((7, levels, LANES))
    for k in range(7):
        rate = np.exp(-mu * 2.0**k)[:, None]
        scan_e[k] = np.where(x[None, :] >= 2**k, rate, 0.0)
        scan_w[k] = np.where(x[None, :] < LANES - 2**k, rate, 0.0)
    gain_full = np.broadcast_to(gain[:, None], (levels, LANES))
    phi_west = np.where(m[:, None] == 0, 1.0, gain[:, None] * np.exp(-mu[:, None] * (x + 1.0)))
    phi_east = np.where(m[:, None] == 0, x, gain[:, None] * np.exp(-mu[:, None] * (LANES - x)))
    near = 0.5 * np.abs(x[:, None] - x[None, :]) + x[:, None] * x[None, :] / columns
    near_next = np.broadcast_to((0.5 * (LANES - x) + LANES * x / columns)[:, None], (LANES, LANES))
    lane = np.arange(LANES)
    odd = lane % 2 == 1
    group = np.where(odd, (lane + 1) // 2, lane // 2) % 64
    per_plane = levels // 8
    used = group < 2 * per_plane
    mode = 8 * (group % per_plane)[None, :] + np.arange(8)[:, None]
    mode_mu = mu[mode]
    safe_mu = np.where(mode == 0, 1.0, mode_mu)
    direct = np.zeros((row_count, 8, LANES))
    cross = np.zeros((row_count, 8, LANES))
    for shift in range(row_count):
        to_east = shift if shift else row_count
        to_west = row_count - shift
        steps = np.where(odd, to_west, to_east)[None, :]
        usual = np.exp(-safe_mu * LANES * (steps - 1)) / (1.0 - np.exp(-safe_mu * columns))
        away = float(LANES * shift)
        if shift:
            zero_direct = np.where(odd, away / 2 - away**2 / (2 * columns), 1.0 / columns)
            zero_cross = np.where(odd, -0.5 + away / columns, 0.5 - away / columns)
        else:
            zero_direct = np.zeros(LANES)
            zero_cross = np.zeros(LANES)
        direct[shift] = np.where(mode == 0, zero_direct[None, :], usual) * used
        cross[shift] = np.where(mode == 0, zero_cross[None, :], 0.0) * used
    haze = HAZE_EXTINCT * np.exp(-4.0 * (z + 0.5) / levels)
    haze_above = np.concatenate([np.cumsum(haze[::-1])[::-1], [0.0]])
    f32 = lambda a: np.ascontiguousarray(a, dtype=np.float32)
    return dict(
        cosine=f32(cosine), cosine_t=f32(cosine.T), scan_e=f32(scan_e), scan_w=f32(scan_w), gain=f32(gain_full), phi_west=f32(phi_west),
        phi_east=f32(phi_east), near=f32(near), near_next=f32(near_next), direct=f32(direct), cross=f32(cross),
        haze=f32(haze_above),
    )


def kernel(
    rows, heights,
    u_hbm, w_hbm, t_hbm, class_hbm, paved_hbm, sun_hbm, lookup_ref, haze_ref,
    cosine_hbm, cosine_t_hbm, scan_e_hbm, scan_w_hbm, gain_hbm, phi_w_hbm, phi_e_hbm, near_hbm,
    near_next_hbm, direct_hbm, cross_hbm,
    us, ws, p_in, tn_ref,
    class_ref, paved_ref, sun_ref,
    cosine_ref, cosine_t_ref, scan_e_ref, scan_w_ref, gain_ref, phi_w_ref, phi_e_ref, near_ref,
    near_next_ref, direct_ref, cross_ref,
    ext, leaf, leaf_sum, leaf_in, low_out, low_in, side_out, side_in, side, u_side,
    d_out, d_in, pm, extra, mom, p_out,
    in_sem, other_sem,
    z_sem, side_sem, leaf_sem, a2a_sem, mom_sem, back_sem,
):
    r = lax.axis_index("row")
    h = lax.axis_index("height")
    levels_here = class_ref.shape[0]
    planes = class_ref.shape[1]
    nz = levels_here * heights
    block = 2 * levels_here
    groups = nz // 8

    def at(dr, dh):
        return (lax.rem(r + dr + rows, rows), lax.rem(h + dh + heights, heights))

    depth = 8 if rows % 8 == 0 else rows
    wide = rows // depth
    x_of, z_of = lax.div(r, depth), lax.rem(r, depth)

    def outward(i, count):
        return count // 2 + ((i + 1) // 2) * (1 - 2 * (i % 2))

    def row_peer(i):
        x = lax.rem(x_of + outward(i // depth, wide), wide)
        return (x * depth + lax.rem(z_of + outward(i % depth, depth), depth), h)

    def height_peer(i):
        return lax.rem(h + outward(i, heights), heights)

    first_class = pltpu.make_async_copy(class_hbm, class_ref, other_sem.at[0])
    loads = [
        pltpu.make_async_copy(ref, ext.at[f, pl.ds(1, levels_here)], in_sem.at[f])
        for f, ref in enumerate((u_hbm, w_hbm, t_hbm))
    ]
    for load in loads:
        load.start()
    first_class.start()
    barrier = pltpu.get_barrier_semaphore()

    for i in range(rows - 1):
        pl.semaphore_signal(barrier, inc=1, device_id=row_peer(i), device_id_type=MESH)
    for i in range(heights - 1):
        pl.semaphore_signal(barrier, inc=1, device_id=(r, height_peer(i)), device_id_type=MESH)
    corners = (at(1, 1), at(1, -1), at(-1, 1))
    for corner in (*corners, at(-1, -1)):
        pl.semaphore_signal(barrier, inc=1, device_id=corner, device_id_type=MESH)
    others = [
        pltpu.make_async_copy(src, dst, other_sem.at[i + 1])
        for i, (src, dst) in enumerate((
            (paved_hbm, paved_ref), (sun_hbm, sun_ref),
            (cosine_hbm, cosine_ref), (scan_e_hbm, scan_e_ref), (scan_w_hbm, scan_w_ref),
            (gain_hbm, gain_ref), (near_hbm, near_ref), (phi_w_hbm, phi_w_ref),
            (phi_e_hbm, phi_e_ref), (near_next_hbm, near_next_ref), (direct_hbm, direct_ref), (cross_hbm, cross_ref),
            (cosine_t_hbm, cosine_t_ref),
        ))
    ]
    for load in loads:
        load.wait()
    lane = lax.broadcasted_iota(jnp.int32, (planes, LANES), 1)

    def leaf_of(classes):
        area = jnp.zeros((planes, LANES), jnp.float32)
        for c in range(lookup_ref.shape[0]):
            area = jnp.where(classes == c, lookup_ref[c], area)
        return area

    def pack_sides(z, acc):
        for f in range(3):
            j = 2 * (f * levels_here + z)
            turned = pltpu.roll(ext[f, z + 1], j + 1, 1)
            acc = jnp.where((lane == j) | (lane == j + 1), turned, acc)
        j = 6 * levels_here + 2 * z
        turned = pltpu.roll(ext[0, z + 1], lax.rem(j + 2, LANES), 1)
        acc = jnp.where(lane == j, turned, acc)
        turned = pltpu.roll(class_ref[z].astype(jnp.float32), lax.rem(j + 2, LANES), 1)
        return jnp.where(lane == j + 1, turned, acc)

    first_class.wait()
    side_out[...] = lax.fori_loop(0, levels_here, pack_sides, jnp.zeros((planes, LANES), jnp.float32), unroll=True)
    low_out[0] = ext[1, levels_here - 1]
    low_out[1] = leaf_of(class_ref[levels_here - 1])
    pl.semaphore_wait(barrier, heights + rows + 2)

    def remote(src, dst, sems, slot, device):
        return pltpu.make_async_remote_copy(
            src_ref=src, dst_ref=dst, send_sem=sems.at[0, slot], recv_sem=sems.at[1, slot],
            device_id=device, device_id_type=MESH,
        )

    halo = [
        remote(side_out, side_in.at[0], side_sem, 0, at(1, 0)),
        remote(side_out, side_in.at[1], side_sem, 1, at(-1, 0)),
        remote(ext.at[:, levels_here], ext.at[:, 0], z_sem, 0, at(0, 1)),
        remote(ext.at[:, 1], ext.at[:, levels_here + 1], z_sem, 1, at(0, -1)),
        remote(low_out, low_in, z_sem, 2, at(0, 1)),
    ] + [
        remote(side_out, side_in.at[2 + i], side_sem, 2 + i, corner) for i, corner in enumerate(corners)
    ]
    for copy in halo:
        copy.start()
    for copy in others:
        copy.start()

    def leaf_level(z, total):
        area = leaf_of(class_ref[z])
        area = jnp.where(h * levels_here + z < CANOPY, area, 0.0)
        leaf[z] = area
        return total + area

    leaf_sum[...] = lax.fori_loop(0, levels_here, leaf_level, jnp.zeros((planes, LANES), jnp.float32), unroll=UNROLL)
    leaf_copies = [
        remote(leaf_sum, leaf_in.at[0], leaf_sem, 0, at(0, -1)),
        remote(leaf_sum, leaf_in.at[1], leaf_sem, 1, at(0, -2)),
    ]
    for copy in leaf_copies:
        copy.start()

    def stretch(q, u, w, east, west, above, below):
        advect = u * (east - west) * 0.5 + w * (above - below) * 0.5
        diffuse = VISCOSITY * (east + west + above + below - 4.0 * q)
        return diffuse - advect

    def drag(area, u, w):
        return DRAG_COEF * area * jnp.sqrt(u * u + w * w + SPAN_VAR)

    still = jnp.zeros((planes, LANES), jnp.float32)
    for z in range(levels_here):
        u, w, t = ext[0, z + 1], ext[1, z + 1], ext[2, z + 1]
        friction = drag(leaf[z], u, w)
        for f, q, star, lift in ((0, u, us, 0.0), (1, w, ws, THERMAL_LIFT * t)):
            east = jnp.where(lane == LANES - 1, 0.0, pltpu.roll(q, LANES - 1, 1))
            west = jnp.where(lane == 0, 0.0, pltpu.roll(q, 1, 1))
            above = ext[f, z + 2] if z < levels_here - 1 else still
            below = ext[f, z] if z > 0 else still
            star[z] = q + DT * (stretch(q, u, w, east, west, above, below) - friction * q + lift)

    for copy in halo:
        copy.wait()

    @pl.when(h == 0)
    def _():
        ext[:, 0] = jnp.zeros((3, planes, LANES), jnp.float32)

    @pl.when(h == heights - 1)
    def _():
        ext[:, levels_here + 1] = jnp.zeros((3, planes, LANES), jnp.float32)

    even = lax.rem(lane, 2) == 0
    from_left = side_in[0]
    side[...] = jnp.where(even, pltpu.roll(side_in[1], LANES - 1, 1), pltpu.roll(from_left, 1, 1))

    last = 2 * (levels_here - 1)
    w_left = pltpu.roll(from_left, LANES - 2 * levels_here, 1)
    u_far = pltpu.roll(from_left, LANES - 6 * levels_here, 1)
    class_left = pltpu.roll(from_left, LANES - 6 * levels_here - 1, 1)
    z_of_lane = h * levels_here + lane // 2
    area_left = jnp.where(z_of_lane < CANOPY, leaf_of(class_left), 0.0)
    u_east = pltpu.roll(side_out[...], LANES - 1, 1)
    corner_above = jnp.where(h < heights - 1, pltpu.roll(side_in[3], last, 1), 0.0)
    corner_below = jnp.where(h > 0, pltpu.roll(side_in[2], LANES - last, 1), 0.0)
    u_above = jnp.where(lane == last, corner_above, pltpu.roll(from_left, LANES - 2, 1))
    u_below = jnp.where(lane == 0, corner_below, pltpu.roll(from_left, 2, 1))
    u_side[...] = from_left + DT * (
        stretch(from_left, from_left, w_left, u_east, u_far, u_above, u_below)
        - drag(area_left, from_left, w_left) * from_left
    )

    u_low, w_low, t_low = ext[0, 0], ext[1, 0], ext[2, 0]
    j = 2 * (2 * levels_here - 1)
    w_east = jnp.where(
        lane == LANES - 1, pltpu.roll(side_in[4], LANES - 2 - j, 1), pltpu.roll(w_low, LANES - 1, 1)
    )
    w_west = jnp.where(lane == 0, pltpu.roll(side_in[2], LANES - j, 1), pltpu.roll(w_low, 1, 1))
    area_low = jnp.where(h * levels_here - 1 < CANOPY, low_in[1], 0.0)
    w_star_low = w_low + DT * (
        stretch(w_low, u_low, w_low, w_east, w_west, ext[1, 1], low_in[0])
        - drag(area_low, u_low, w_low) * w_low
        + THERMAL_LIFT * t_low
    )
    w_star_low = jnp.where(h > 0, w_star_low, 0.0)

    def growth(f, z, u, w):
        q = ext[f, z + 1]
        j = 2 * (f * levels_here + z)
        edge = pltpu.roll(side[...], LANES - 1 - j, 1)
        east = jnp.where(lane == LANES - 1, edge, pltpu.roll(q, LANES - 1, 1))
        west = jnp.where(lane == 0, edge, pltpu.roll(q, 1, 1))
        return stretch(q, u, w, east, west, ext[f, z + 2], ext[f, z])

    w_below = w_star_low
    for z in range(levels_here):
        u, w = ext[0, z + 1], ext[1, z + 1]
        sides = jnp.where(
            lane == 0, VISCOSITY + 0.5 * u, jnp.where(lane == LANES - 1, VISCOSITY - 0.5 * u, 0.0)
        )
        stars = []
        for f, star in ((0, us), (1, ws)):
            edge = pltpu.roll(side[...], LANES - 1 - 2 * (f * levels_here + z), 1)
            share = sides * edge
            if z == 0:
                share = share + (VISCOSITY + 0.5 * w) * ext[f, 0]
            if z == levels_here - 1:
                share = share + (VISCOSITY - 0.5 * w) * ext[f, levels_here + 1]
            stars.append(star[z] + DT * share)
        u_star, w_star = stars
        if z == levels_here - 1:
            w_star = jnp.where(h == heights - 1, 0.0, w_star)
        us[z] = u_star
        ws[z] = w_star
        edge = pltpu.roll(u_side[...], (LANES - 2 * z) % LANES, 1)
        west = jnp.where(lane == 0, edge, pltpu.roll(u_star, 1, 1))
        d_out[pl.ds(z, planes, stride=levels_here), :] = u_star - west + (w_star - w_below)
        w_below = w_star

    def finish(buffer, count, sem):
        part = buffer.at[pl.ds(0, count)]
        pltpu.make_async_copy(part, part, sem).wait()

    for y in range(2):

        for i in range(heights - 1):
            to = height_peer(i)
            pltpu.make_async_remote_copy(
                src_ref=d_out.at[pl.ds((2 * to + y) * levels_here, levels_here)],
                dst_ref=d_in.at[y, pl.ds(h * levels_here, levels_here)],
                send_sem=a2a_sem.at[0], recv_sem=a2a_sem.at[1 + y],
                device_id=(r, to), device_id_type=MESH,
            ).start()
    for y in range(2):
        d_in[y, pl.ds(h * levels_here, levels_here)] = d_out[
            pl.ds((2 * h + y) * levels_here, levels_here)
        ]
    for copy in others[:2]:
        copy.wait()

    for copy in leaf_copies:
        copy.wait()
    above1 = jnp.where(h < heights - 1, leaf_in[0], 0.0)
    above2 = jnp.where(h < heights - 2, leaf_in[1], 0.0)
    over = above1 + above2
    sun = sun_ref[...]
    first = jnp.exp(-(0.5 * over + haze_ref[h * levels_here + levels_here]))

    def heat(k, state):
        over, top = state
        z = levels_here - 1 - k
        over = over + leaf[z]
        bottom = jnp.exp(-(0.5 * over + haze_ref[h * levels_here + z]))
        warming = sun * (top - bottom)
        absorb = jnp.where(paved_ref[...] == 1, PAVED_ABSORB, GRASS_ABSORB)
        warming = warming + jnp.where(h * levels_here + z == 0, sun * bottom * absorb, 0.0)
        t = ext[2, z + 1]
        tn_ref[z] = t + DT * (growth(2, z, ext[0, z + 1], ext[1, z + 1]) + warming)
        return over, bottom

    lax.fori_loop(0, levels_here, heat, (over, first), unroll=UNROLL)
    for copy in others[2:]:
        copy.wait()

    lane8 = lax.broadcasted_iota(jnp.int32, (8, LANES), 1)
    sub8 = lax.broadcasted_iota(jnp.int32, (8, LANES), 0)
    chunk = min(64, nz)
    lane_c = lax.broadcasted_iota(jnp.int32, (chunk, LANES), 1)
    slot = (sub8 == 0) & (lane8 == 0)

    def row_scans(y):
        finish(d_in.at[y], (heights - 1) * levels_here, a2a_sem.at[1 + y])
        modes = jnp.dot(
            cosine_ref[...], d_in[y], precision=HIGHEST, preferred_element_type=jnp.float32
        )
        packed = jnp.zeros((8, LANES), jnp.float32)
        for start in range(0, nz, chunk):
            part = slice(start, start + chunk)
            d = modes[part]
            fwd = d
            bwd = d
            for k in range(7):
                s = 1 << k
                fwd = fwd + scan_e_ref[k, part, :] * pltpu.roll(fwd, s, 1)
                bwd = bwd + scan_w_ref[k, part, :] * pltpu.roll(bwd, LANES - s, 1)
            local = gain_ref[part, :] * (fwd + bwd - d)
            ends = jnp.where(lane_c == 0, bwd, fwd)
            if start == 0:
                zero = d[0:8]
                first_moment = jnp.sum(zero * lane8.astype(jnp.float32), axis=1, keepdims=True)
            pm[y, part] = local
            for i in range(chunk // 8):
                value = ends[8 * i : 8 * i + 8]
                if start == 0 and i == 0:
                    value = jnp.where(slot, jnp.broadcast_to(first_moment, (8, LANES)), value)
                j = 2 * (start // 8 + i)
                turned = pltpu.roll(value, j, 1) if j else value
                mine = (lane8 == j) | (lane8 == (j + LANES - 1) % LANES)
                packed = jnp.where(mine, turned, packed)
        mom[y, r] = packed

        for i in range(rows - 1):
            pltpu.make_async_remote_copy(
                src_ref=mom.at[y, r], dst_ref=mom.at[y, r],
                send_sem=mom_sem.at[0], recv_sem=mom_sem.at[1 + y],
                device_id=row_peer(i), device_id_type=MESH,
            ).start()
        own = jnp.dot(zero, near_ref[...], precision=HIGHEST, preferred_element_type=jnp.float32)
        pm[y, 0:8] = jnp.where(sub8 == 0, own, pm[y, 0:8])
        return jnp.dot(
            zero, near_next_ref[...], precision=HIGHEST, preferred_element_type=jnp.float32
        )

    def row_solve(y, own_next):
        finish(mom.at[y], rows - 1, mom_sem.at[1 + y])

        def gather_moments(i, state):
            direct, cross = state
            values = mom[y, lax.rem(r + i, rows)]
            return direct + direct_ref[i] * values, cross + cross_ref[i] * values

        nothing = jnp.zeros((8, LANES), jnp.float32)
        direct, cross = lax.fori_loop(0, rows, gather_moments, (nothing, nothing), unroll=UNROLL)
        inflow = direct + jnp.where(
            lax.rem(lane8, 2) == 0, pltpu.roll(cross, 1, 1), pltpu.roll(cross, LANES - 1, 1)
        )
        for g in range(groups):
            part = slice(8 * g, 8 * g + 8)
            j = 2 * g
            west = (j + LANES - 1) % LANES
            from_east = jnp.broadcast_to(inflow[:, j : j + 1], (8, LANES))
            from_west = jnp.broadcast_to(inflow[:, west : west + 1], (8, LANES))
            onward = pm[y, part] + phi_w_ref[part, :] * from_west
            pm[y, part] = onward + phi_e_ref[part, :] * from_east
            beyond = (
                scan_w_ref[0, part, :] * jnp.broadcast_to(onward[:, LANES - 1 :], (8, LANES))
                + gain_ref[part, :] * from_east
            )
            if g == 0:
                beyond = jnp.where(
                    sub8 == 0, own_next + from_west + float(LANES) * from_east, beyond
                )
            extra[part, :] = beyond
        solved = jnp.dot(
            cosine_t_ref[...], pm[y], precision=HIGHEST, preferred_element_type=jnp.float32
        )
        beyond = jnp.dot(
            jnp.transpose(extra[...])[0:8], cosine_ref[...],
            precision=HIGHEST, preferred_element_type=jnp.float32,
        )
        for to in range(heights):
            z0 = to * levels_here
            half = z0 // LANES
            top = min(z0 + levels_here, nz - 1)
            p_out[y, to, 0:levels_here] = solved[z0 : z0 + levels_here]
            p_out[y, to, levels_here : levels_here + 1] = solved[top : top + 1]
            p_out[y, to, levels_here + 1 : levels_here + 2] = beyond[
                0:1, half * LANES : (half + 1) * LANES
            ]

        for i in range(heights - 1):
            to = height_peer(i)
            pltpu.make_async_remote_copy(
                src_ref=p_out.at[y, to, pl.ds(0, TALL)],
                dst_ref=p_in.at[2 * h + y, pl.ds(0, TALL)],
                send_sem=back_sem.at[0], recv_sem=back_sem.at[1],
                device_id=(r, to), device_id_type=MESH,
            ).start()
        p_in[2 * h + y] = p_out[y, h]

    own_next = [row_scans(0), row_scans(1)]
    for y in range(2):
        row_solve(y, own_next[y])
    finish(d_out, (heights - 1) * block, a2a_sem.at[0])
    part = mom.at[:, pl.ds(0, rows - 1)]
    pltpu.make_async_copy(part, part, mom_sem.at[0]).wait()
    for sem in (back_sem.at[1], back_sem.at[0]):
        part = p_in.at[pl.ds(0, 2 * (heights - 1)), pl.ds(0, TALL)]
        pltpu.make_async_copy(part, part, sem).wait()


def project_kernel(
    heights, us, ws, p_in, warm, un_hbm, wn_hbm, tn_hbm, un, wn, out_sem,
):
    warm_out = pltpu.make_async_copy(warm, tn_hbm, out_sem.at[4])
    warm_out.start()
    h = lax.axis_index("height")
    levels_here, planes = us.shape[0], us.shape[1]
    lane = lax.broadcasted_iota(jnp.int32, (planes, LANES), 1)
    beyond = p_in[pl.ds(levels_here + 1, planes, stride=SLOT), :]
    first = lax.rem(h * levels_here, LANES)

    def project(z, p):
        edge = pltpu.roll(beyond, LANES - 1 - first - z, 1)
        east = jnp.where(lane == LANES - 1, edge, pltpu.roll(p, LANES - 1, 1))
        un[z] = us[z] - (east - p)
        above = p_in[pl.ds(z + 1, planes, stride=SLOT), :]
        wn[z] = ws[z] - (above - p)
        return above

    p = p_in[pl.ds(0, planes, stride=SLOT), :]
    half = levels_here // 2
    stores = []
    for part in range(2):
        p = lax.fori_loop(part * half, part * half + half, project, p, unroll=UNROLL)
        rows_here = pl.ds(part * half, half)
        for i, (src, dst) in enumerate(((un, un_hbm), (wn, wn_hbm))):
            store = pltpu.make_async_copy(
                src.at[rows_here], dst.at[rows_here], out_sem.at[2 * part + i]
            )
            store.start()
            stores.append(store)
    warm_out.wait()
    for store in stores:
        store.wait()


def solution(mesh):
    rows, heights = mesh.shape["row"], mesh.shape["height"]

    def per_device(u, w, t, classes, paved, sun, lookup):
        levels_here, planes, width = u.shape
        nz = levels_here * heights
        table = tables(nz, width * rows, rows)
        smem = pl.BlockSpec(memory_space=pltpu.SMEM)
        hbm = pl.BlockSpec(memory_space=pltpu.HBM)
        vmem = pl.BlockSpec(memory_space=pltpu.VMEM)
        field = jax.ShapeDtypeStruct(u.shape, jnp.float32)
        plane = (planes, LANES)
        f32 = jnp.float32
        dma = pltpu.SemaphoreType.DMA
        call = pl.pallas_call(
            functools.partial(kernel, rows, heights),
            out_shape=(field, field, jax.ShapeDtypeStruct((planes, SLOT, LANES), f32), field),
            in_specs=[hbm] * 6 + [smem] * 2 + [hbm] * 11,
            out_specs=(vmem,) * 4,
            scratch_shapes=[
                pltpu.VMEM((levels_here,) + plane, jnp.int32),
                pltpu.VMEM(plane, jnp.int32),
                pltpu.VMEM(plane, f32),
                pltpu.VMEM((nz, nz), f32),
                pltpu.VMEM((nz, nz), f32),
                pltpu.VMEM((7, nz, LANES), f32),
                pltpu.VMEM((7, nz, LANES), f32),
                pltpu.VMEM((nz, LANES), f32),
                pltpu.VMEM((nz, LANES), f32),
                pltpu.VMEM((nz, LANES), f32),
                pltpu.VMEM((LANES, LANES), f32),
                pltpu.VMEM((LANES, LANES), f32),
                pltpu.VMEM((rows, 8, LANES), f32),
                pltpu.VMEM((rows, 8, LANES), f32),
                pltpu.VMEM((3, levels_here + 2) + plane, f32),
                pltpu.VMEM((levels_here,) + plane, f32),
                pltpu.VMEM(plane, f32),
                pltpu.VMEM((2,) + plane, f32),
                pltpu.VMEM((2,) + plane, f32),
                pltpu.VMEM((2,) + plane, f32),
                pltpu.VMEM(plane, f32),
                pltpu.VMEM((5,) + plane, f32),
                pltpu.VMEM(plane, f32),
                pltpu.VMEM(plane, f32),
                pltpu.VMEM((2 * nz, LANES), f32),
                pltpu.VMEM((2, nz, LANES), f32),
                pltpu.VMEM((2, nz, LANES), f32),
                pltpu.VMEM((nz, LANES), f32),
                pltpu.VMEM((2, rows, 8, LANES), f32),
                pltpu.VMEM((2, heights, SLOT, LANES), f32),
                dma((3,)), dma((14,)), dma((2, 3)), dma((2, 5)), dma((2, 2)),
                dma((3,)), dma((3,)), dma((2,)),
            ],
            compiler_params=pltpu.CompilerParams(
                collective_id=0, has_side_effects=True, vmem_limit_bytes=24 * 1024 * 1024
            ),
        )
        stay = lambda a: pltpu.with_memory_space_constraint(jnp.asarray(a), pltpu.HBM)
        table = {name: stay(values) for name, values in table.items()}
        u, w, t, classes, paved, sun, lookup = map(
            stay, (u, w, t, classes, paved, sun, lookup)
        )
        us, ws, p, warm = call(
            u, w, t, classes, paved, sun, lookup, table["haze"], table["cosine"],
            table["cosine_t"], table["scan_e"], table["scan_w"], table["gain"],
            table["phi_west"], table["phi_east"], table["near"], table["near_next"],
            table["direct"], table["cross"],
        )
        project = pl.pallas_call(
            functools.partial(project_kernel, heights),
            out_shape=(field, field, field),
            in_specs=[vmem] * 4,
            out_specs=(hbm,) * 3,
            scratch_shapes=[pltpu.VMEM(u.shape, f32), pltpu.VMEM(u.shape, f32), dma((5,))],
            compiler_params=pltpu.CompilerParams(vmem_limit_bytes=24 * 1024 * 1024),
        )
        return project(us, ws, p.reshape(planes * SLOT, LANES), warm)

    field = P("height", None, "row")
    line = P(None, "row")
    return jax.shard_map(
        per_device, mesh=mesh, in_specs=(field, field, field, field, line, line, P()),
        out_specs=(field, field, field), check_vma=False,
    )
```
